32 devices in a mesh: dp: 8 (over y, x, core), blk: 4 (over z).
Axes of the slice: x: 2, y: 2, z: 4, core: 2. Of those that a mesh axis runs over, the one named last changes fastest.
Arguments:
- tokens: bfloat16 [24, 1536, 768], P('dp', 'blk'), may hold values from -6 to 6
- counts: int32 [24], P('dp'), may hold values from 864 to 1536, as said below
- ln1_gain: bfloat16 [768], replicated, may hold values from 0.5 to 1.5
- ln1_shift: bfloat16 [768], replicated, may hold values from -0.59765625 to 0.59765625
- w_qkv: bfloat16 [768, 2304], replicated, may hold values from -0.21875 to 0.21875
- bias_q: bfloat16 [768], replicated, may hold values from -0.59765625 to 0.59765625
- bias_v: bfloat16 [768], replicated, may hold values from -0.23925781 to 0.23925781
- w_out: bfloat16 [768, 768], replicated, may hold values from -4 to 4
- bias_out: bfloat16 [768], replicated, may hold values from -0.59765625 to 0.59765625
- ln2_gain: bfloat16 [768], replicated, may hold values from 0.5 to 1.5
- ln2_shift: bfloat16 [768], replicated, may hold values from -0.59765625 to 0.59765625
- w_fc1: bfloat16 [768, 3072], replicated, may hold values from -0.21875 to 0.21875
- bias_fc1: bfloat16 [3072], replicated, may hold values from -0.59765625 to 0.59765625
- w_fc2: bfloat16 [3072, 768], replicated, may hold values from -0.109375 to 0.109375
- bias_fc2: bfloat16 [768], replicated, may hold values from -0.59765625 to 0.59765625
- cotangent: bfloat16 [24, 1536, 768], P('dp', 'blk'), may hold values from -6 to 6
Outputs:
- output: bfloat16 [24, 1536, 768], P('dp', 'blk')
- input_grad: float32 [24, 1536, 768], P('dp', 'blk')
- grad_ln1_gain: float32 [768], replicated
- grad_ln1_shift: float32 [768], replicated
- grad_w_qkv: float32 [768, 2304], replicated
- grad_bias_q: float32 [768], replicated
- grad_bias_v: float32 [768], replicated
- grad_w_out: float32 [768, 768], replicated
- grad_bias_out: float32 [768], replicated
- grad_ln2_gain: float32 [768], replicated
- grad_ln2_shift: float32 [768], replicated
- grad_w_fc1: float32 [768, 3072], replicated
- grad_bias_fc1: float32 [3072], replicated
- grad_w_fc2: float32 [3072, 768], replicated
- grad_bias_fc2: float32 [768], replicated
The draws below stay inside these ranges and needn't reach their ends.
Inputs may be any that keep to these rules, and one draw needn't show every extreme that they name: `counts`: each cube holds its valid tokens first; in each index of dp exactly the ceiling of half of its 3 cubes hold 1536, the others 864.
All inputs are finite; a program needn't handle non-finite values.
Results may differ from the reference program's by a relative error of at most 0.02.
Values may be sent and summed in bfloat16 or wider, within the bound.
No kernel may reach another device: no remote copies, remote signals or barrier semaphores. Data moves between devices by JAX's collectives and lax.ppermute only.
A program may use at most 256 MiB of HBM per device.

```python
import jax
import jax.numpy as jnp
from jax import lax

D = 768
HEADS = 12
HD = 64
FF = 3072
SEQ = 1536
CUBES = 3
SHORT = 864
CUBES_ALL = 24


def draw_counts(key, part):
    key = jax.random.fold_in(key, 7)
    groups = CUBES_ALL // CUBES
    orders = jax.vmap(lambda single: jax.random.permutation(single, CUBES))(jax.random.split(key, groups))
    full_cube = orders < (CUBES + 1) // 2
    return jnp.where(full_cube, SEQ, SHORT).reshape(CUBES_ALL).astype(jnp.int32)


def shard_levels(stream_key, dims, shards, least, top_value):
    level, own = 1.0, jax.random.fold_in(stream_key, 6)
    for position, shards_of in shards:
        draws = jnp.exp(jax.random.uniform(jax.random.fold_in(own, position), (shards_of,), jnp.float32, least / len(shards), top_value / len(shards)))
        level = level * jnp.repeat(draws, dims[position] // shards_of).reshape([-1 if axis == position else 1 for axis in range(len(dims))])
    return level


def scatter_about(stream_key, extent, deviation, most, cuts=(), kind=jnp.bfloat16):
    factor_of = shard_levels(stream_key, extent, cuts, -0.22, 0.18) if cuts else 1.0
    values = jax.random.normal(stream_key, extent, jnp.float32) * deviation * factor_of
    return jnp.minimum(jnp.maximum(values, -most), most).astype(kind)


def setup_inputs(seed: int = 0) -> dict:
    seeds = jax.random.split(jax.random.key(seed), 17)
    return {
        "tokens": scatter_about(seeds[0], (CUBES_ALL, SEQ, D), 1.0, 6.0, ((0, 8), (1, 4))),
        "counts": draw_counts(jax.random.fold_in(seeds[16], 71), 0),
        "ln1_gain": jnp.clip(1.0 + 0.1 * jax.random.normal(seeds[2], (D,), jnp.float32), 0.5, 1.5).astype(jnp.bfloat16),
        "ln1_shift": scatter_about(seeds[3], (D,), 0.1, 0.59765625),
        "w_qkv": scatter_about(seeds[4], (D, 3 * D), D ** -0.5, 0.21875),
        "bias_q": scatter_about(seeds[5], (D,), 0.1, 0.59765625),
        "bias_v": scatter_about(seeds[6], (D,), 0.04, 0.23925781),
        "w_out": scatter_about(seeds[7], (D, D), (D * 3 // SEQ + 1) ** -0.5, 4.0),
        "bias_out": scatter_about(seeds[8], (D,), 0.1, 0.59765625),
        "ln2_gain": jnp.clip(1.0 + 0.1 * jax.random.normal(seeds[9], (D,), jnp.float32), 0.5, 1.5).astype(jnp.bfloat16),
        "ln2_shift": scatter_about(seeds[10], (D,), 0.1, 0.59765625),
        "w_fc1": scatter_about(seeds[11], (D, FF), D ** -0.5, 0.21875),
        "bias_fc1": scatter_about(seeds[12], (FF,), 0.1, 0.59765625),
        "w_fc2": scatter_about(seeds[13], (FF, D), FF ** -0.5, 0.109375),
        "bias_fc2": scatter_about(seeds[14], (D,), 0.1, 0.59765625),
        "cotangent": scatter_about(seeds[15], (CUBES_ALL, SEQ, D), 1.0, 6.0, ((0, 8), (1, 4))),
    }


@jax.custom_vjp
def low(v):
    return lax.optimization_barrier(v.astype(jnp.bfloat16)).astype(jnp.float32)

@jax.custom_vjp
def low_back(v):
    return v

def low_keep(v):
    return (low(v), None)

def low_pass(kept, grad):
    return (grad,)

def back_keep(v):
    return (v, None)

def back_low(kept, grad):
    return (low(grad),)
low.defvjp(low_keep, low_pass)
low_back.defvjp(back_keep, back_low)
NORM_EPS = 1e-06

def norm_rows(values, gain, shift):
    centre = values - lax.optimization_barrier(jnp.mean(values, axis=-1, keepdims=True))
    spread = lax.optimization_barrier(jnp.mean(centre * centre, axis=-1, keepdims=True))
    return centre * lax.rsqrt(spread + NORM_EPS) * gain + shift

def matmul(left, right):
    return jnp.dot(left, right, precision=lax.Precision.HIGHEST)

def cube_forward(inputs, valid_count, params):
    ln1_gain, ln1_shift, w_qkv, bias_q, bias_v, w_out, bias_out, ln2_gain, ln2_shift, w_fc1, bias_fc1, w_fc2, bias_fc2 = params
    normed = low(norm_rows(inputs, ln1_gain, ln1_shift))
    project = matmul(normed, w_qkv)
    queries = low_back(low(project[:, :D] + bias_q)).reshape(SEQ, HEADS, HD)
    key_rows = low_back(low(project[:, D:2 * D])).reshape(SEQ, HEADS, HD)
    value_rows = low_back(low(project[:, 2 * D:] + bias_v)).reshape(SEQ, HEADS, HD)
    scores = low_back(jnp.einsum('qhd,khd->hqk', queries, key_rows, precision=lax.Precision.HIGHEST) * HD ** (-0.5))
    usable = (jnp.arange(SEQ, dtype=jnp.int32) < valid_count)[None, None, :]
    masked = jnp.where(usable, scores, -1e+30)
    row_top = lax.optimization_barrier(jnp.max(masked, axis=-1, keepdims=True))
    weights = jnp.where(usable, jnp.exp(masked - row_top), 0.0)
    row_total = lax.optimization_barrier(jnp.sum(weights, axis=-1))
    mixture = jnp.einsum('hqk,khd->qhd', low(weights), value_rows, precision=lax.Precision.HIGHEST)
    mixture = mixture / jnp.transpose(row_total)[:, :, None]
    attended = low_back(low(mixture.reshape(SEQ, D)))
    branch = low_back(matmul(attended, w_out)) + bias_out
    middle = inputs + branch
    normed_two = low(norm_rows(middle, ln2_gain, ln2_shift))
    hidden = low_back(matmul(normed_two, w_fc1)) + bias_fc1
    active = low(jax.nn.gelu(hidden, approximate=False))
    return middle + low_back(matmul(active, w_fc2)) + bias_fc2

def reference(tokens, counts, ln1_gain, ln1_shift, w_qkv, bias_q, bias_v, w_out, bias_out, ln2_gain, ln2_shift, w_fc1, bias_fc1, w_fc2, bias_fc2, cotangent):
    params = tuple((weight.astype(jnp.float32) for weight in (ln1_gain, ln1_shift, w_qkv, bias_q, bias_v, w_out, bias_out, ln2_gain, ln2_shift, w_fc1, bias_fc1, w_fc2, bias_fc2)))

    def one_cube(grad_sums, cube_item):
        cube_tokens, cube_count, cube_back = cube_item

        def forward(inputs, weights_all):
            return cube_forward(inputs, cube_count, weights_all)
        result, pullback = jax.vjp(forward, cube_tokens.astype(jnp.float32), params)
        input_grad, weight_grads = pullback(cube_back.astype(jnp.float32))
        grad_sums = tuple((running + update for running, update in zip(grad_sums, weight_grads)))
        return (grad_sums, (result.astype(jnp.bfloat16), input_grad))
    initial = tuple((jnp.zeros(weight.shape, jnp.float32) for weight in params))
    grad_sums, (outputs, input_grads) = lax.scan(one_cube, initial, (tokens, counts, cotangent))
    return (outputs, input_grads, grad_sums[0], grad_sums[1], grad_sums[2], grad_sums[3], grad_sums[4], grad_sums[5], grad_sums[6], grad_sums[7], grad_sums[8], grad_sums[9], grad_sums[10], grad_sums[11], grad_sums[12])
```

```python
import functools
import math

import jax
import jax.numpy as jnp
from jax import lax
from jax.experimental import pallas as pl
from jax.experimental.pallas import tpu as pltpu
from jax.sharding import PartitionSpec as P

HEADS = 12
HD = 64
SHORT = 864


NORM_EPS = 1e-06
MASK_LOW = -1e30


def norm_rows(values, gain, shift):
    centre = values - jnp.mean(values, axis=-1, keepdims=True)
    spread = jnp.mean(centre * centre, axis=-1, keepdims=True)
    return centre * lax.rsqrt(spread + NORM_EPS) * gain + shift


def gelu_exact(values):
    return jax.nn.gelu(values, approximate=False)


def cube_valid(counts, offset, length):
    places = offset + jnp.arange(length, dtype=jnp.int32)
    return places[None, :] < counts[:, None]


def total_every(parts):
    split = (
        lax.psum_scatter(
            parts[0].astype(jnp.bfloat16), "blk", scatter_dimension=0, tiled=True
        ).astype(jnp.float32),
        lax.psum_scatter(
            parts[1].astype(jnp.bfloat16), "blk", scatter_dimension=0, tiled=True
        ).astype(jnp.float32),
        lax.psum_scatter(
            parts[2].astype(jnp.bfloat16), "blk", scatter_dimension=0, tiled=True
        ).astype(jnp.float32),
        lax.psum_scatter(
            parts[3].astype(jnp.bfloat16), "blk", scatter_dimension=0, tiled=True
        ).astype(jnp.float32),
        lax.psum_scatter(
            parts[4].astype(jnp.bfloat16), "blk", scatter_dimension=0, tiled=True
        ).astype(jnp.float32),
        lax.psum_scatter(
            parts[5].astype(jnp.bfloat16), "blk", scatter_dimension=0, tiled=True
        ).astype(jnp.float32),
        lax.psum_scatter(
            parts[6].astype(jnp.bfloat16), "blk", scatter_dimension=0, tiled=True
        ).astype(jnp.float32),
        lax.psum_scatter(
            parts[7].astype(jnp.bfloat16), "blk", scatter_dimension=0, tiled=True
        ).astype(jnp.float32),
        lax.psum_scatter(
            parts[8].astype(jnp.bfloat16), "blk", scatter_dimension=0, tiled=True
        ).astype(jnp.float32),
        lax.psum_scatter(
            parts[9].astype(jnp.bfloat16), "blk", scatter_dimension=0, tiled=True
        ).astype(jnp.float32),
        lax.psum_scatter(
            parts[10].astype(jnp.bfloat16), "blk", scatter_dimension=0, tiled=True
        ).astype(jnp.float32),
        lax.psum_scatter(
            parts[11].astype(jnp.bfloat16), "blk", scatter_dimension=0, tiled=True
        ).astype(jnp.float32),
        lax.psum_scatter(
            parts[12].astype(jnp.bfloat16), "blk", scatter_dimension=0, tiled=True
        ).astype(jnp.float32),
    )
    summed = (
        lax.psum(split[0].astype(jnp.bfloat16), "dp").astype(jnp.float32),
        lax.psum(split[1].astype(jnp.bfloat16), "dp").astype(jnp.float32),
        lax.psum(split[2].astype(jnp.bfloat16), "dp").astype(jnp.float32),
        lax.psum(split[3].astype(jnp.bfloat16), "dp").astype(jnp.float32),
        lax.psum(split[4].astype(jnp.bfloat16), "dp").astype(jnp.float32),
        lax.psum(split[5].astype(jnp.bfloat16), "dp").astype(jnp.float32),
        lax.psum(split[6].astype(jnp.bfloat16), "dp").astype(jnp.float32),
        lax.psum(split[7].astype(jnp.bfloat16), "dp").astype(jnp.float32),
        lax.psum(split[8].astype(jnp.bfloat16), "dp").astype(jnp.float32),
        lax.psum(split[9].astype(jnp.bfloat16), "dp").astype(jnp.float32),
        lax.psum(split[10].astype(jnp.bfloat16), "dp").astype(jnp.float32),
        lax.psum(split[11].astype(jnp.bfloat16), "dp").astype(jnp.float32),
        lax.psum(split[12].astype(jnp.bfloat16), "dp").astype(jnp.float32),
    )
    return (
        lax.all_gather(summed[0].astype(jnp.bfloat16), "blk", axis=0, tiled=True).astype(
            jnp.float32
        ),
        lax.all_gather(summed[1].astype(jnp.bfloat16), "blk", axis=0, tiled=True).astype(
            jnp.float32
        ),
        lax.all_gather(summed[2].astype(jnp.bfloat16), "blk", axis=0, tiled=True).astype(
            jnp.float32
        ),
        lax.all_gather(summed[3].astype(jnp.bfloat16), "blk", axis=0, tiled=True).astype(
            jnp.float32
        ),
        lax.all_gather(summed[4].astype(jnp.bfloat16), "blk", axis=0, tiled=True).astype(
            jnp.float32
        ),
        lax.all_gather(summed[5].astype(jnp.bfloat16), "blk", axis=0, tiled=True).astype(
            jnp.float32
        ),
        lax.all_gather(summed[6].astype(jnp.bfloat16), "blk", axis=0, tiled=True).astype(
            jnp.float32
        ),
        lax.all_gather(summed[7].astype(jnp.bfloat16), "blk", axis=0, tiled=True).astype(
            jnp.float32
        ),
        lax.all_gather(summed[8].astype(jnp.bfloat16), "blk", axis=0, tiled=True).astype(
            jnp.float32
        ),
        lax.all_gather(summed[9].astype(jnp.bfloat16), "blk", axis=0, tiled=True).astype(
            jnp.float32
        ),
        lax.all_gather(summed[10].astype(jnp.bfloat16), "blk", axis=0, tiled=True).astype(
            jnp.float32
        ),
        lax.all_gather(summed[11].astype(jnp.bfloat16), "blk", axis=0, tiled=True).astype(
            jnp.float32
        ),
        lax.all_gather(summed[12].astype(jnp.bfloat16), "blk", axis=0, tiled=True).astype(
            jnp.float32
        ),
    )


def local(
    tokens,
    counts,
    ln1_gain,
    ln1_shift,
    w_qkv,
    bias_q,
    bias_v,
    w_out,
    bias_out,
    ln2_gain,
    ln2_shift,
    w_fc1,
    bias_fc1,
    w_fc2,
    bias_fc2,
    cotangent,
):
    cube_count, row_count, width = tokens.shape
    head_count = HEADS
    depth = HD
    score_scale = HD ** (-0.5)
    inputs = tokens.astype(jnp.float32)
    gain_one = ln1_gain.astype(jnp.float32)
    shift_one = ln1_shift.astype(jnp.float32)
    gain_two = ln2_gain.astype(jnp.float32)
    shift_two = ln2_shift.astype(jnp.float32)
    normed = norm_rows(inputs, gain_one, shift_one).astype(jnp.bfloat16)
    project = jnp.dot(normed, w_qkv, preferred_element_type=jnp.float32)
    queries = (project[..., :width] + bias_q.astype(jnp.float32)).astype(jnp.bfloat16)
    key_local = project[..., width : 2 * width].astype(jnp.bfloat16)
    value_local = (project[..., 2 * width :] + bias_v.astype(jnp.float32)).astype(jnp.bfloat16)
    key_all, value_all = (
        lax.all_gather(key_local, "blk", axis=1, tiled=True),
        lax.all_gather(value_local, "blk", axis=1, tiled=True),
    )
    seq_rows = key_all.shape[1]
    block_rows = math.gcd(seq_rows, 512)
    block_count = seq_rows // block_rows
    block_steps = jnp.arange(block_count, dtype=jnp.int32)
    query_heads = queries.reshape(cube_count, row_count, head_count, depth)

    def key_slices(offset):
        key_part = lax.dynamic_slice_in_dim(key_all, offset, block_rows, 1).reshape(
            cube_count, block_rows, head_count, depth
        )
        value_part = lax.dynamic_slice_in_dim(value_all, offset, block_rows, 1).reshape(
            cube_count, block_rows, head_count, depth
        )
        usable = cube_valid(counts, offset, block_rows)[:, None, None, :]
        return (key_part, value_part, usable)

    def forward_block(carry, step_index):
        row_top, row_total, accum = carry
        key_part, value_part, usable = key_slices(step_index * block_rows)
        scores = (
            jnp.einsum("cqhd,ckhd->chqk", query_heads, key_part, preferred_element_type=jnp.float32)
            * score_scale
        )
        masked = jnp.where(usable, scores, MASK_LOW)
        new_top = jnp.maximum(row_top, jnp.max(masked, axis=-1))
        factor = jnp.exp(row_top - new_top)
        weights = jnp.where(usable, jnp.exp(masked - new_top[..., None]), 0.0)
        row_total = row_total * factor + jnp.sum(weights, axis=-1)
        accum = accum * jnp.transpose(factor, (0, 2, 1))[..., None] + jnp.einsum(
            "chqk,ckhd->cqhd",
            weights.astype(jnp.bfloat16),
            value_part,
            preferred_element_type=jnp.float32,
        )
        return ((new_top, row_total, accum), None)

    start_carry = (
        jnp.full((cube_count, head_count, row_count), MASK_LOW, jnp.float32),
        jnp.zeros((cube_count, head_count, row_count), jnp.float32),
        jnp.zeros((cube_count, row_count, head_count, depth), jnp.float32),
    )
    (row_top, row_total, accum), _ = lax.scan(forward_block, start_carry, block_steps)
    attended_f = (accum / jnp.transpose(row_total, (0, 2, 1))[..., None]).reshape(
        cube_count, row_count, width
    )
    log_total = row_top + jnp.log(row_total)
    attended = attended_f.astype(jnp.bfloat16)
    middle = (
        inputs
        + jnp.dot(attended, w_out, preferred_element_type=jnp.float32)
        + bias_out.astype(jnp.float32)
    )
    normed_two = norm_rows(middle, gain_two, shift_two).astype(jnp.bfloat16)
    hidden = jnp.dot(normed_two, w_fc1, preferred_element_type=jnp.float32) + bias_fc1.astype(
        jnp.float32
    )
    active = gelu_exact(hidden).astype(jnp.bfloat16)
    output = (
        middle
        + jnp.dot(active, w_fc2, preferred_element_type=jnp.float32)
        + bias_fc2.astype(jnp.float32)
    ).astype(jnp.bfloat16)
    grad_bias_fc2 = jnp.sum(cotangent.astype(jnp.float32), axis=(0, 1))
    grad_w_fc2 = jnp.einsum("ctf,ctd->fd", active, cotangent, preferred_element_type=jnp.float32)
    back_active = jnp.einsum("ctd,fd->ctf", cotangent, w_fc2, preferred_element_type=jnp.float32)
    _, gelu_pull = jax.vjp(gelu_exact, hidden)
    back_hidden = gelu_pull(back_active)[0]
    grad_bias_fc1 = jnp.sum(back_hidden, axis=(0, 1))
    hidden_low = back_hidden.astype(jnp.bfloat16)
    grad_w_fc1 = jnp.einsum(
        "ctd,ctf->df", normed_two, hidden_low, preferred_element_type=jnp.float32
    )
    back_normed_two = jnp.einsum(
        "ctf,df->ctd", hidden_low, w_fc1, preferred_element_type=jnp.float32
    )
    _, norm_pull_two = jax.vjp(norm_rows, middle, gain_two, shift_two)
    back_middle_norm, grad_ln2_gain, grad_ln2_shift = norm_pull_two(back_normed_two)
    back_middle = cotangent.astype(jnp.float32) + back_middle_norm
    mlp_grads = (
        grad_ln2_gain,
        grad_ln2_shift,
        grad_w_fc1,
        grad_bias_fc1,
        grad_w_fc2,
        grad_bias_fc2,
    )
    grad_bias_out = jnp.sum(back_middle, axis=(0, 1))
    middle_low = back_middle.astype(jnp.bfloat16)
    grad_w_out = jnp.einsum("ctd,cte->de", attended, middle_low, preferred_element_type=jnp.float32)
    back_attended = jnp.einsum(
        "cte,de->ctd", middle_low, w_out, preferred_element_type=jnp.float32
    ).astype(jnp.bfloat16)
    back_heads = back_attended.reshape(cube_count, row_count, head_count, depth)
    delta = jnp.transpose(
        jnp.sum(
            (back_attended.astype(jnp.float32) * attended_f).reshape(
                cube_count, row_count, head_count, depth
            ),
            axis=-1,
        ),
        (0, 2, 1),
    )

    def block_grads(key_part, value_part, usable):
        scores = (
            jnp.einsum("cqhd,ckhd->chqk", query_heads, key_part, preferred_element_type=jnp.float32)
            * score_scale
        )
        probs = jnp.where(usable, jnp.exp(scores - log_total[..., None]), 0.0)
        back_probs = jnp.einsum(
            "cqhd,ckhd->chqk", back_heads, value_part, preferred_element_type=jnp.float32
        )
        back_scores = (probs * (back_probs - delta[..., None])).astype(jnp.bfloat16)
        return (probs, back_scores)

    query_zero = jnp.zeros((cube_count, row_count, head_count, depth), jnp.float32)

    def back_block(carry, step_index):
        back_query, key_grads, value_grads = carry
        offset = step_index * block_rows
        key_part, value_part, usable = key_slices(offset)
        probs, back_scores = block_grads(key_part, value_part, usable)
        back_query = (
            back_query
            + jnp.einsum(
                "chqk,ckhd->cqhd", back_scores, key_part, preferred_element_type=jnp.float32
            )
            * score_scale
        )
        key_block = (
            jnp.einsum(
                "chqk,cqhd->ckhd", back_scores, query_heads, preferred_element_type=jnp.float32
            )
            * score_scale
        )
        value_block = jnp.einsum(
            "chqk,cqhd->ckhd",
            probs.astype(jnp.bfloat16),
            back_heads,
            preferred_element_type=jnp.float32,
        )
        key_grads = lax.dynamic_update_slice_in_dim(
            key_grads, key_block.reshape(cube_count, block_rows, width), offset, 1
        )
        value_grads = lax.dynamic_update_slice_in_dim(
            value_grads, value_block.reshape(cube_count, block_rows, width), offset, 1
        )
        return ((back_query, key_grads, value_grads), None)

    full_zero = jnp.zeros((cube_count, seq_rows, width), jnp.float32)
    (back_query, key_grads, value_grads), _ = lax.scan(
        back_block, (query_zero, full_zero, full_zero), block_steps
    )
    key_back, value_back = (
        lax.psum_scatter(
            key_grads.astype(jnp.bfloat16), "blk", scatter_dimension=1, tiled=True
        ).astype(jnp.float32),
        lax.psum_scatter(
            value_grads.astype(jnp.bfloat16), "blk", scatter_dimension=1, tiled=True
        ).astype(jnp.float32),
    )
    query_low = back_query.reshape(cube_count, row_count, width).astype(jnp.bfloat16)
    key_low = key_back.astype(jnp.bfloat16)
    value_low = value_back.astype(jnp.bfloat16)
    grad_bias_q = jnp.sum(query_low.astype(jnp.float32), axis=(0, 1))
    grad_bias_v = jnp.sum(value_low.astype(jnp.float32), axis=(0, 1))
    back_project = jnp.concatenate([query_low, key_low, value_low], axis=-1)
    grad_w_qkv = jnp.einsum("ctd,cte->de", normed, back_project, preferred_element_type=jnp.float32)
    back_normed = jnp.einsum("cte,de->ctd", back_project, w_qkv, preferred_element_type=jnp.float32)
    _, norm_pull_one = jax.vjp(norm_rows, inputs, gain_one, shift_one)
    back_inputs, grad_ln1_gain, grad_ln1_shift = norm_pull_one(back_normed)
    input_grad = back_middle + back_inputs
    attn_grads = (
        grad_ln1_gain,
        grad_ln1_shift,
        grad_w_qkv,
        grad_bias_q,
        grad_bias_v,
        grad_w_out,
        grad_bias_out,
    )
    every_grad = total_every(attn_grads + mlp_grads)
    attn_grads = every_grad[:7]
    mlp_grads = every_grad[7:]
    return (
        output,
        input_grad,
        attn_grads[0],
        attn_grads[1],
        attn_grads[2],
        attn_grads[3],
        attn_grads[4],
        attn_grads[5],
        attn_grads[6],
        mlp_grads[0],
        mlp_grads[1],
        mlp_grads[2],
        mlp_grads[3],
        mlp_grads[4],
        mlp_grads[5],
    )


F32 = jnp.float32
BF16 = jnp.bfloat16
EXP_SCALE = math.log2(math.e) / 8
LANES = 128
VMEM = pl.BlockSpec(memory_space=pltpu.VMEM)


def shape_of(shape, dtype):
    return jax.ShapeDtypeStruct(shape, dtype)


def limits(mib):
    return pltpu.CompilerParams(vmem_limit_bytes=mib * 2**20)


def dot_nt(a, b):
    return lax.dot_general(a, b, (((1,), (1,)), ((), ())), preferred_element_type=F32)


def dot_nn(a, b):
    return lax.dot_general(a, b, (((1,), (0,)), ((), ())), preferred_element_type=F32)


def dot_tn(a, b):
    return lax.dot_general(a, b, (((0,), (0,)), ((), ())), preferred_element_type=F32)


def centred(values):
    centre = values - jnp.mean(values, axis=1, keepdims=True)
    spread = jnp.mean(centre * centre, axis=1, keepdims=True)
    return centre, lax.rsqrt(spread + NORM_EPS)


def norm_back(centre, recip, back, gain):
    unit = centre * recip
    grad = back * gain
    inner = jnp.mean(grad * unit, axis=1, keepdims=True)
    return unit, recip * (grad - jnp.mean(grad, axis=1, keepdims=True) - unit * inner)


def project_kernel(*refs, pieces):
    xs = refs[:pieces]
    vecs, w, q_ref, kv_ref = refs[pieces:]
    rows = xs[0].shape[0]
    gain, shift, bias_q, bias_v = (vecs[i : i + 1, :] for i in range(4))
    for i in range(pieces):
        centre, recip = centred(xs[i][...].astype(F32))
        normed = (centre * recip * gain + shift).astype(BF16)
        at = pl.ds(i * rows, rows)
        q_ref[at, :] = (dot_nn(normed, w[:, :768]) + bias_q).astype(BF16)
        kv_ref[0, at, :] = dot_nn(normed, w[:, 768:1536]).astype(BF16)
        kv_ref[1, at, :] = (dot_nn(normed, w[:, 1536:]) + bias_v).astype(BF16)


def project(xs, vecs, w):
    n = sum(x.shape[0] for x in xs)
    return pl.pallas_call(
        functools.partial(project_kernel, pieces=len(xs)),
        in_specs=[VMEM] * (len(xs) + 2),
        out_specs=[VMEM] * 2,
        out_shape=[shape_of((n, 768), BF16), shape_of((2, n, 768), BF16)],
        compiler_params=limits(40),
        cost_estimate=pl.CostEstimate(
            flops=2 * n * 768 * 2304, bytes_accessed=n * 768 * 8 + 768 * 2304 * 2, transcendentals=0
        ),
        name="project",
    )(*xs, vecs, w)


def three_parts(values, lane):
    high = values.astype(BF16)
    rest = values - high.astype(F32)
    middle = rest.astype(BF16)
    least = (rest - middle.astype(F32)).astype(BF16)
    zero = jnp.zeros((), BF16)
    return jnp.where(
        lane == 0, high, jnp.where(lane == 1, middle, jnp.where(lane == 2, least, zero))
    )


def lane_index(rows=1):
    return lax.broadcasted_iota(jnp.int32, (rows, LANES), 1)


def attend_kernel(*refs, pieces, valid, step):
    q_ref = refs[0]
    kvs = refs[1 : 1 + pieces]
    o_ref, t_ref = refs[1 + pieces :]
    lane = lane_index()
    low = lane < 64
    half = lane % 64
    total = sum(kv.shape[1] for kv in kvs)
    keys, values = [], []
    for h in range(2):
        own = low if h == 0 else ~low
        key_parts, value_parts, at = [], [], 0
        for kv in kvs:
            n = kv.shape[1]
            beside = jnp.zeros((n, LANES), BF16)
            if at + n > valid:
                place = lax.broadcasted_iota(jnp.int32, (n, LANES), 0) + at
                beside = jnp.where(
                    (place >= valid) & (lane_index(n) % 64 == 0), MASK_LOW, 0.0
                ).astype(BF16)
            key_parts.append(jnp.where(own, kv[0], beside))
            value_parts.append(jnp.where(own, kv[1], jnp.ones((), BF16)))
            at += n
        keys.append(key_parts)
        values.append(value_parts)
    for s in range(q_ref.shape[0] // step):
        at = pl.ds(s * step, step)
        q = q_ref[at, :]
        sums, tops = [], []
        for h in range(2):
            own = low if h == 0 else ~low
            q_own = q
            if total > valid:
                q_own = jnp.where(own, q, jnp.where(half == 0, 1.0, 0.0).astype(BF16))
            scores = [dot_nt(q_own, k) for k in keys[h]]
            top = functools.reduce(
                jnp.maximum, [jnp.max(x, axis=1, keepdims=True) for x in scores]
            )
            scaled_top = top * EXP_SCALE
            weights = [jnp.exp2(x * EXP_SCALE - scaled_top).astype(BF16) for x in scores]
            sums.append(
                functools.reduce(jnp.add, [dot_nn(p, v) for p, v in zip(weights, values[h])])
            )
            tops.append(top)
        above = jnp.where(low, sums[0], sums[1])
        below = jnp.where(low, sums[1], sums[0])
        o_ref[at, :] = above / pltpu.roll(below, 64, 1)
        log_total = -(jnp.where(low, tops[1], tops[0]) + 8.0 * jnp.log(below))
        t_ref[at, :] = jnp.where(half == 3, jnp.ones((), BF16), three_parts(log_total, half))


def attend(q, kvs, valid, rows, step):
    n = q.shape[0]
    keys = sum(kv.shape[1] for kv in kvs)
    block = pl.BlockSpec((rows, LANES), lambda p, i: (i, p))
    return pl.pallas_call(
        functools.partial(attend_kernel, pieces=len(kvs), valid=valid, step=step),
        out_shape=[shape_of((n, 768), F32), shape_of((n, 768), BF16)],
        grid=(6, n // rows),
        in_specs=[block]
        + [pl.BlockSpec((2, kv.shape[1], LANES), lambda p, i: (0, 0, p)) for kv in kvs],
        out_specs=[block, block],
        compiler_params=limits(56),
        cost_estimate=pl.CostEstimate(
            flops=16 * n * keys * 768, bytes_accessed=n * 768 * 8, transcendentals=n * keys * 12
        ),
        name="attend",
    )(q, *kvs)


def attend_back_kernel(*refs, pieces, valid, step):
    q_ref, do_ref, o_ref, t_ref = refs[:4]
    kvs = refs[4 : 4 + pieces]
    dq_ref = refs[4 + pieces]
    dkvs = refs[5 + pieces :]
    n = q_ref.shape[0]
    lane = lane_index()
    low = lane < 64
    half = lane % 64
    q, do, t = q_ref[...], do_ref[...], t_ref[...]
    product = do.astype(F32) * o_ref[...]
    delta = [
        jnp.sum(jnp.where(low, product, 0.0), axis=1, keepdims=True),
        jnp.sum(jnp.where(low, 0.0, product), axis=1, keepdims=True),
    ]
    d = three_parts(-jnp.where(low, delta[1], delta[0]), half)
    queries = [jnp.where(low, q, t), jnp.where(low, t, q)]
    backs = [jnp.where(low, do, d), jnp.where(low, d, do)]
    ones = jnp.where(half < 3, 1.0, 0.0).astype(BF16)
    sums = [jnp.zeros((LANES, n), F32), jnp.zeros((LANES, n), F32)]
    start = 0
    for kv, dkv in zip(kvs, dkvs):
        for first in range(0, kv.shape[1], step):
            size = min(step, kv.shape[1] - first)
            at = pl.ds(first, size)
            key_sums, value_sums = [], []
            for h in range(2):
                own = low if h == 0 else ~low
                beside = ones
                if start + first + size > valid:
                    place = lax.broadcasted_iota(jnp.int32, (size, LANES), 0) + (start + first)
                    wide = lane_index(size) % 64
                    beside = jnp.where(
                        wide < 3, 1.0, jnp.where((place >= valid) & (wide == 3), MASK_LOW, 0.0)
                    ).astype(BF16)
                key = jnp.where(own, kv[0, at, :], beside)
                value = jnp.where(own, kv[1, at, :], ones)
                probs = jnp.exp2(dot_nt(key, queries[h]) * EXP_SCALE)
                back_scores = (probs * dot_nt(value, backs[h])).astype(BF16)
                value_sums.append(dot_nn(probs.astype(BF16), backs[h]))
                key_sums.append(dot_nn(back_scores, queries[h]))
                sums[h] = sums[h] + dot_tn(key, back_scores)
            dkv[0, at, :] = (jnp.where(low, key_sums[0], key_sums[1]) * 0.125).astype(BF16)
            dkv[1, at, :] = jnp.where(low, value_sums[0], value_sums[1]).astype(BF16)
        start += kv.shape[1]
    both = jnp.concatenate([sums[0][:64], sums[1][64:]], axis=0)
    dq_ref[...] = (both.T * 0.125).astype(BF16)


def attend_back(q, do, o, t, kvs, valid, step):
    n = q.shape[0]
    keys = sum(kv.shape[1] for kv in kvs)
    block = pl.BlockSpec((n, LANES), lambda p: (0, p))
    wide = [pl.BlockSpec((2, kv.shape[1], LANES), lambda p: (0, 0, p)) for kv in kvs]
    return pl.pallas_call(
        functools.partial(attend_back_kernel, pieces=len(kvs), valid=valid, step=step),
        out_shape=[shape_of((n, 768), BF16)] + [shape_of(kv.shape, BF16) for kv in kvs],
        grid=(6,),
        in_specs=[block] * 4 + wide,
        out_specs=[block] + wide,
        compiler_params=limits(56),
        cost_estimate=pl.CostEstimate(
            flops=40 * n * keys * 768, bytes_accessed=n * 768 * 12, transcendentals=n * keys * 12
        ),
        name="attend_back",
    )(q, do, o, t, *kvs)


def feed_kernel(
    att_full, att_short, x1, x2, x3, c1, c2, c3, w_out, vecs, w1, b1, w2,
    o1, o2, o3, back_att, back_mid, gw1, gw2, gw_out, gb1, sums,
    mid, normed, normed_t, out_sum, back_sum, cot, active, hidden_low,
    *, steps, tile,
):
    j = pl.program_id(0)
    xs, cots, outs = (x1, x2, x3), (c1, c2, c3), (o1, o2, o3)
    rows = x1.shape[0]
    full = att_full.shape[0] // rows
    bias_out, gain, shift, b2 = (vecs[i : i + 1, :] for i in range(4))

    def at(i):
        return pl.ds(i * rows, rows)

    def attended(i):
        source = att_full[at(i), :] if i < full else att_short[at(i - full), :]
        return source.astype(BF16)

    @pl.when(j == 0)
    def _():
        for i in range(3):
            m = xs[i][...].astype(F32) + dot_nn(attended(i), w_out[...]) + bias_out
            mid[at(i), :] = m
            centre, recip = centred(m)
            low = (centre * recip * gain + shift).astype(BF16)
            normed[at(i), :] = low
            normed_t[:, at(i)] = low.T
            cot[at(i), :] = cots[i][...]
            out_sum[at(i), :] = m + b2
            back_sum[at(i), :] = jnp.zeros((rows, 768), F32)

    w1_tile, w2_tile = w1[...], w2[...]
    bias = b1[...]
    bias_sum = jnp.zeros((1, tile), F32)
    for i in range(3):
        h = dot_nn(normed[at(i), :], w1_tile) + bias
        back_active = dot_nt(cot[at(i), :], w2_tile)
        share = 0.5 + 0.5 * lax.erf(h * math.sqrt(0.5))
        act = (h * share).astype(BF16)
        slope = share + h * (math.sqrt(0.5 / math.pi) * jnp.exp(h * h * (-0.5)))
        back_hidden = back_active * slope
        low = back_hidden.astype(BF16)
        bias_sum = bias_sum + jnp.sum(back_hidden, axis=0, keepdims=True)
        active[at(i), :] = act
        hidden_low[at(i), :] = low
        out_sum[at(i), :] += dot_nn(act, w2_tile)
        back_sum[at(i), :] += dot_nt(low, w1_tile)
    gb1[...] = bias_sum
    gw1[...] = dot_nn(normed_t[...], hidden_low[...]).astype(BF16)
    gw2[...] = dot_tn(active[...], cot[...]).astype(BF16)

    @pl.when(j == steps - 1)
    def _():
        zero = jnp.zeros((1, 768), F32)
        grad_out, grad_gain, grad_shift, grad_b2 = zero, zero, zero, zero
        for i in range(3):
            outs[i][...] = out_sum[at(i), :].astype(BF16)
            centre, recip = centred(mid[at(i), :])
            back = back_sum[at(i), :]
            unit, through = norm_back(centre, recip, back, gain)
            c = cots[i][...].astype(F32)
            m = c + through
            grad_gain = grad_gain + jnp.sum(back * unit, axis=0, keepdims=True)
            grad_shift = grad_shift + jnp.sum(back, axis=0, keepdims=True)
            grad_out = grad_out + jnp.sum(m, axis=0, keepdims=True)
            grad_b2 = grad_b2 + jnp.sum(c, axis=0, keepdims=True)
            back_mid[at(i), :] = m
            low = m.astype(BF16)
            normed[at(i), :] = low
            back_att[at(i), :] = dot_nt(low, w_out[...]).astype(BF16)
            cot[at(i), :] = attended(i)
        gw_out[...] = dot_tn(cot[...], normed[...]).astype(BF16)
        sums[...] = jnp.concatenate(
            [grad_out, grad_gain, grad_shift, grad_b2, zero, zero, zero, zero], axis=0
        )


def feed(att_full, att_short, xs, cots, w_out, vecs, w1, b1, w2, tile):
    rows = xs[0].shape[0]
    n = rows * 3
    wide = w1.shape[1]
    steps = wide // tile
    across = pl.BlockSpec((768, tile), lambda j: (0, j))
    down = pl.BlockSpec((tile, 768), lambda j: (j, 0))
    line = pl.BlockSpec((1, tile), lambda j: (0, j))
    return pl.pallas_call(
        functools.partial(feed_kernel, steps=steps, tile=tile),
        grid=(steps,),
        in_specs=[VMEM] * 10 + [across, line, down],
        out_specs=[VMEM] * 5 + [across, down, VMEM, line, VMEM],
        out_shape=[shape_of((rows, 768), BF16)] * 3
        + [
            shape_of((n, 768), BF16),
            shape_of((n, 768), F32),
            shape_of((768, wide), BF16),
            shape_of((wide, 768), BF16),
            shape_of((768, 768), BF16),
            shape_of((1, wide), F32),
            shape_of((8, 768), F32),
        ],
        scratch_shapes=[
            pltpu.VMEM((n, 768), F32),
            pltpu.VMEM((n, 768), BF16),
            pltpu.VMEM((768, n), BF16),
            pltpu.VMEM((n, 768), F32),
            pltpu.VMEM((n, 768), F32),
            pltpu.VMEM((n, 768), BF16),
            pltpu.VMEM((n, tile), BF16),
            pltpu.VMEM((n, tile), BF16),
        ],
        compiler_params=limits(60),
        cost_estimate=pl.CostEstimate(
            flops=12 * n * 768 * wide + 6 * n * 768 * 768,
            bytes_accessed=40 * 2**20,
            transcendentals=2 * n * wide,
        ),
        name="feed",
    )(att_full, att_short, *xs, *cots, w_out, vecs, w1, b1, w2)


def project_grad_kernel(
    x1, x2, x3, vecs, dq_full, dq_short, own_full, got_full, own_short, got_short,
    back, gw, sums, normed,
):
    rows = x1.shape[0]
    full = dq_full.shape[0]
    gain, shift = vecs[0:1, :], vecs[1:2, :]
    for i, x in enumerate((x1, x2, x3)):
        centre, recip = centred(x[...].astype(F32))
        normed[pl.ds(i * rows, rows), :] = (centre * recip * gain + shift).astype(BF16)
    back[:full, :768] = dq_full[...]
    back[full:, :768] = dq_short[...]
    for k in range(2):
        at = pl.ds(768 * (k + 1), 768)
        back[:full, at] = (own_full[k].astype(F32) + got_full[k].astype(F32)).astype(BF16)
        back[full:, at] = (own_short[k].astype(F32) + got_short[k].astype(F32)).astype(BF16)
    zero = jnp.zeros((6, 768), F32)
    sums[...] = jnp.concatenate(
        [
            jnp.sum(back[:, :768].astype(F32), axis=0, keepdims=True),
            jnp.sum(back[:, 1536:].astype(F32), axis=0, keepdims=True),
            zero,
        ],
        axis=0,
    )
    flipped = normed[...].T
    for k in range(3):
        at = pl.ds(768 * k, 768)
        gw[:, at] = dot_nn(flipped, back[:, at]).astype(BF16)


def project_grad(xs, vecs, dq_full, dq_short, own_full, got_full, own_short, got_short):
    n = sum(x.shape[0] for x in xs)
    return pl.pallas_call(
        project_grad_kernel,
        in_specs=[VMEM] * 10,
        out_specs=[VMEM] * 3,
        out_shape=[shape_of((n, 2304), BF16), shape_of((768, 2304), BF16), shape_of((8, 768), F32)],
        scratch_shapes=[pltpu.VMEM((n, 768), BF16)],
        compiler_params=limits(56),
        cost_estimate=pl.CostEstimate(
            flops=2 * n * 768 * 2304, bytes_accessed=16 * 2**20, transcendentals=0
        ),
        name="project_grad",
    )(*xs, vecs, dq_full, dq_short, own_full, got_full, own_short, got_short)


def input_grad_kernel(x1, x2, x3, vecs, back, w, back_mid, o1, o2, o3, sums):
    rows = x1.shape[0]
    gain = vecs[0:1, :]
    zero = jnp.zeros((1, 768), F32)
    grad_gain, grad_shift = zero, zero
    for i, (x, out) in enumerate(((x1, o1), (x2, o2), (x3, o3))):
        at = pl.ds(i * rows, rows)
        centre, recip = centred(x[...].astype(F32))
        back_normed = dot_nt(back[at, :], w[...])
        unit, through = norm_back(centre, recip, back_normed, gain)
        grad_gain = grad_gain + jnp.sum(back_normed * unit, axis=0, keepdims=True)
        grad_shift = grad_shift + jnp.sum(back_normed, axis=0, keepdims=True)
        out[...] = (back_mid[at, :] + through).astype(BF16)
    sums[...] = jnp.concatenate([grad_gain, grad_shift, jnp.zeros((6, 768), F32)], axis=0)


def input_grad_of(xs, vecs, back, w, back_mid):
    n = back.shape[0]
    rows = xs[0].shape[0]
    return pl.pallas_call(
        input_grad_kernel,
        in_specs=[VMEM] * 7,
        out_specs=[VMEM] * 4,
        out_shape=[shape_of((rows, 768), BF16)] * 3 + [shape_of((8, 768), F32)],
        compiler_params=limits(56),
        cost_estimate=pl.CostEstimate(
            flops=2 * n * 768 * 2304, bytes_accessed=16 * 2**20, transcendentals=0
        ),
        name="input_grad",
    )(*xs, vecs, back, w, back_mid)


FIRST_TO = {
    (0, 0): (0, 0), (0, 1): (0, 1), (0, 2): (1, 0), (0, 3): (1, 1),
    (1, 0): (0, 2), (1, 1): (0, 3), (1, 2): (1, 2), (1, 3): (1, 3),
}
SECOND_TO = {
    (0, 0): (0, 1), (0, 1): (0, 0), (0, 2): (1, 1), (0, 3): (1, 0),
    (1, 0): (0, 3), (1, 1): (0, 2), (1, 2): (1, 3), (1, 3): (1, 2),
}


def column_pairs(table):
    pairs = []
    for chip in range(4):
        for (core, z), (core_to, z_to) in table.items():
            pairs.append(((chip * 2 + core) * 4 + z, (chip * 2 + core_to) * 4 + z_to))
    return pairs


def flip_pairs(size, mask):
    return [(i, i ^ mask) for i in range(size)]


def swap(array, axis, mask):
    return lax.ppermute(array, axis, flip_pairs(8 if axis == "dp" else 4, mask))


def add_low(*terms):
    return sum(term.astype(F32) for term in terms).astype(BF16)


def part_of(array, index, count):
    rows = array.shape[0] // count
    return lax.dynamic_slice_in_dim(array, index * rows, rows, 0)


class Place:
    def __init__(self):
        dp = lax.axis_index("dp")
        self.z = lax.axis_index("blk")
        self.core = dp % 2
        self.chip = dp // 2


def sum_apart(arrays, place):
    halves = []
    for a in arrays:
        got = swap(part_of(a, 1 - place.core, 2), "dp", 1)
        halves.append(add_low(part_of(a, place.core, 2), got))
    quarters = []
    for a in halves:
        got = [swap(part_of(a, place.chip ^ k, 4), "dp", 2 * k) for k in (1, 2, 3)]
        quarters.append(add_low(part_of(a, place.chip, 4), *got))
    parts = []
    for a in quarters:
        got = [swap(part_of(a, place.z ^ k, 4), "blk", k) for k in (1, 2, 3)]
        parts.append(add_low(part_of(a, place.z, 4), *got))
    return parts


def spread(piece, got, index):
    rows = piece.shape[0]
    whole = jnp.zeros((rows * 4,) + piece.shape[1:], piece.dtype)
    for k, array in enumerate([piece] + got):
        whole = lax.dynamic_update_slice_in_dim(whole, array, (index ^ k) * rows, 0)
    return whole


def join(parts, place):
    wholes = []
    for a in parts:
        a = spread(a, [swap(a, "blk", k) for k in (1, 2, 3)], place.z)
        a = spread(a, [swap(a, "dp", 2 * k) for k in (1, 2, 3)], place.chip)
        got = swap(a, "dp", 1)
        first = place.core == 0
        wholes.append(
            jnp.concatenate([jnp.where(first, a, got), jnp.where(first, got, a)]).astype(F32)
        )
    return wholes


def local_paired(
    tokens,
    counts,
    ln1_gain,
    ln1_shift,
    w_qkv,
    bias_q,
    bias_v,
    w_out,
    bias_out,
    ln2_gain,
    ln2_shift,
    w_fc1,
    bias_fc1,
    w_fc2,
    bias_fc2,
    cotangent,
):
    place = Place()
    odd = place.z % 2
    short = jnp.argmin(counts).astype(jnp.int32)
    full_one = jnp.where(short == 0, 1, 0)
    full_two = jnp.where(short == 2, 1, 2)
    slots = (jnp.where(odd == 0, full_one, full_two), jnp.where(odd == 0, full_two, full_one), short)
    tables = (FIRST_TO, SECOND_TO, FIRST_TO)

    def bring(array):
        return [
            lax.ppermute(
                lax.dynamic_index_in_dim(array, slot, 0, keepdims=False),
                ("dp", "blk"),
                column_pairs(table),
            )
            for slot, table in zip(slots, tables)
        ]

    def give_back(pieces):
        home = [
            lax.ppermute(
                piece, ("dp", "blk"), [(target, source) for source, target in column_pairs(table)]
            )
            for piece, table in zip(pieces, tables)
        ]
        return jnp.stack(
            [
                jnp.where(slots[0] == i, home[0], jnp.where(slots[1] == i, home[1], home[2]))
                for i in range(3)
            ]
        )

    vecs_one = jnp.stack([ln1_gain, ln1_shift, bias_q, bias_v]).astype(F32)
    vecs_two = jnp.stack([bias_out, ln2_gain, ln2_shift, bias_fc2]).astype(F32)
    b1 = bias_fc1.reshape(1, -1).astype(F32)

    xs = bring(tokens)
    cots = bring(cotangent)
    q_full, kv_full = project(xs[:2], vecs_one, w_qkv)
    kv_other = swap(kv_full, "dp", 1)
    q_short, kv_short = project(xs[2:], vecs_one, w_qkv)
    kv_near = swap(kv_short, "blk", 1)
    kv_pair = jnp.concatenate(
        [jnp.where(odd == 0, kv_short, kv_near), jnp.where(odd == 0, kv_near, kv_short)], axis=1
    )
    kv_far = swap(kv_pair, "dp", 1)
    first_core = place.core == 0
    kv_head = jnp.where(first_core, kv_pair, kv_far)
    spare = -(-(SHORT - kv_head.shape[1]) // LANES) * LANES
    kv_tail = jnp.where(first_core, kv_far[:, :spare], kv_pair[:, :spare])

    seq = 2 * kv_full.shape[1]
    att_full, t_full = attend(q_full, [kv_full, kv_other], seq, 768, 384)
    att_short, t_short = attend(q_short, [kv_head, kv_tail], SHORT, 384, 384)
    (o1, o2, o3, back_att, back_mid, gw1, gw2, gw_out, gb1, sums_two) = feed(
        att_full, att_short, xs, cots, w_out, vecs_two, w_fc1, b1, w_fc2, 512
    )
    output = give_back([o1, o2, o3])
    early = sum_apart([gw1, gw2, gw_out], place)

    n_full = q_full.shape[0]
    dq_full, own_full, sent_full = attend_back(
        q_full, back_att[:n_full], att_full, t_full, [kv_full, kv_other], seq, 768
    )
    got_full = swap(sent_full, "dp", 1)
    dq_short, d_head, d_tail = attend_back(
        q_short, back_att[n_full:], att_short, t_short, [kv_head, kv_tail], SHORT, 448
    )
    d_tail = jnp.pad(d_tail, ((0, 0), (0, d_head.shape[1] - spare), (0, 0)))
    got_pair = swap(jnp.where(first_core, d_tail, d_head), "dp", 1)
    d_pair = add_low(jnp.where(first_core, d_head, d_tail), got_pair)
    block = kv_short.shape[1]
    own_short = lax.dynamic_slice_in_dim(d_pair, odd * block, block, 1)
    got_short = swap(lax.dynamic_slice_in_dim(d_pair, (1 - odd) * block, block, 1), "blk", 1)
    back, gw_qkv, sums_one = project_grad(
        xs, vecs_one, dq_full, dq_short, own_full, got_full, own_short, got_short
    )
    late = sum_apart([gw_qkv], place)
    i1, i2, i3, sums_in = input_grad_of(xs, vecs_one, back, w_qkv, back_mid)
    input_grad = give_back([i1, i2, i3]).astype(F32)
    grad_w_fc1, grad_w_fc2, grad_w_out = join(early, place)
    (grad_w_qkv,) = join(late, place)
    lines = jnp.concatenate(
        [sums_two[:4], gb1.reshape(-1, 768), sums_one[:2], sums_in[:2]], axis=0
    )
    lines = lax.psum(lines, ("dp", "blk"))
    wide = w_fc1.shape[1] // 768
    return (
        output,
        input_grad,
        lines[6 + wide],
        lines[7 + wide],
        grad_w_qkv,
        lines[4 + wide],
        lines[5 + wide],
        grad_w_out,
        lines[0],
        lines[1],
        lines[2],
        grad_w_fc1,
        lines[4 : 4 + wide].reshape(-1),
        grad_w_fc2,
        lines[3],
    )


def solution(mesh):
    paired = mesh.shape["dp"] == 8 and mesh.shape["blk"] == 4
    chosen = local_paired if paired else local
    return jax.shard_map(
        chosen,
        mesh=mesh,
        in_specs=(
            P("dp", "blk", None),
            P("dp"),
            P(),
            P(),
            P(),
            P(),
            P(),
            P(),
            P(),
            P(),
            P(),
            P(),
            P(),
            P(),
            P(),
            P("dp", "blk", None),
        ),
        out_specs=(
            P("dp", "blk", None),
            P("dp", "blk", None),
            P(),
            P(),
            P(),
            P(),
            P(),
            P(),
            P(),
            P(),
            P(),
            P(),
            P(),
            P(),
            P(),
        ),
        check_vma=False,
    )
```

```python
import functools
import math

import jax
import jax.numpy as jnp
from jax import lax
from jax.experimental import pallas as pl
from jax.experimental.pallas import tpu as pltpu
from jax.sharding import PartitionSpec as P

HEADS = 12
HD = 64
SHORT = 864


NORM_EPS = 1e-06
MASK_LOW = -1e30


def norm_rows(values, gain, shift):
    centre = values - jnp.mean(values, axis=-1, keepdims=True)
    spread = jnp.mean(centre * centre, axis=-1, keepdims=True)
    return centre * lax.rsqrt(spread + NORM_EPS) * gain + shift


def gelu_exact(values):
    return jax.nn.gelu(values, approximate=False)


def cube_valid(counts, offset, length):
    places = offset + jnp.arange(length, dtype=jnp.int32)
    return places[None, :] < counts[:, None]


def total_every(parts):
    split = (
        lax.psum_scatter(
            parts[0].astype(jnp.bfloat16), "blk", scatter_dimension=0, tiled=True
        ).astype(jnp.float32),
        lax.psum_scatter(
            parts[1].astype(jnp.bfloat16), "blk", scatter_dimension=0, tiled=True
        ).astype(jnp.float32),
        lax.psum_scatter(
            parts[2].astype(jnp.bfloat16), "blk", scatter_dimension=0, tiled=True
        ).astype(jnp.float32),
        lax.psum_scatter(
            parts[3].astype(jnp.bfloat16), "blk", scatter_dimension=0, tiled=True
        ).astype(jnp.float32),
        lax.psum_scatter(
            parts[4].astype(jnp.bfloat16), "blk", scatter_dimension=0, tiled=True
        ).astype(jnp.float32),
        lax.psum_scatter(
            parts[5].astype(jnp.bfloat16), "blk", scatter_dimension=0, tiled=True
        ).astype(jnp.float32),
        lax.psum_scatter(
            parts[6].astype(jnp.bfloat16), "blk", scatter_dimension=0, tiled=True
        ).astype(jnp.float32),
        lax.psum_scatter(
            parts[7].astype(jnp.bfloat16), "blk", scatter_dimension=0, tiled=True
        ).astype(jnp.float32),
        lax.psum_scatter(
            parts[8].astype(jnp.bfloat16), "blk", scatter_dimension=0, tiled=True
        ).astype(jnp.float32),
        lax.psum_scatter(
            parts[9].astype(jnp.bfloat16), "blk", scatter_dimension=0, tiled=True
        ).astype(jnp.float32),
        lax.psum_scatter(
            parts[10].astype(jnp.bfloat16), "blk", scatter_dimension=0, tiled=True
        ).astype(jnp.float32),
        lax.psum_scatter(
            parts[11].astype(jnp.bfloat16), "blk", scatter_dimension=0, tiled=True
        ).astype(jnp.float32),
        lax.psum_scatter(
            parts[12].astype(jnp.bfloat16), "blk", scatter_dimension=0, tiled=True
        ).astype(jnp.float32),
    )
    summed = (
        lax.psum(split[0].astype(jnp.bfloat16), "dp").astype(jnp.float32),
        lax.psum(split[1].astype(jnp.bfloat16), "dp").astype(jnp.float32),
        lax.psum(split[2].astype(jnp.bfloat16), "dp").astype(jnp.float32),
        lax.psum(split[3].astype(jnp.bfloat16), "dp").astype(jnp.float32),
        lax.psum(split[4].astype(jnp.bfloat16), "dp").astype(jnp.float32),
        lax.psum(split[5].astype(jnp.bfloat16), "dp").astype(jnp.float32),
        lax.psum(split[6].astype(jnp.bfloat16), "dp").astype(jnp.float32),
        lax.psum(split[7].astype(jnp.bfloat16), "dp").astype(jnp.float32),
        lax.psum(split[8].astype(jnp.bfloat16), "dp").astype(jnp.float32),
        lax.psum(split[9].astype(jnp.bfloat16), "dp").astype(jnp.float32),
        lax.psum(split[10].astype(jnp.bfloat16), "dp").astype(jnp.float32),
        lax.psum(split[11].astype(jnp.bfloat16), "dp").astype(jnp.float32),
        lax.psum(split[12].astype(jnp.bfloat16), "dp").astype(jnp.float32),
    )
    return (
        lax.all_gather(summed[0].astype(jnp.bfloat16), "blk", axis=0, tiled=True).astype(
            jnp.float32
        ),
        lax.all_gather(summed[1].astype(jnp.bfloat16), "blk", axis=0, tiled=True).astype(
            jnp.float32
        ),
        lax.all_gather(summed[2].astype(jnp.bfloat16), "blk", axis=0, tiled=True).astype(
            jnp.float32
        ),
        lax.all_gather(summed[3].astype(jnp.bfloat16), "blk", axis=0, tiled=True).astype(
            jnp.float32
        ),
        lax.all_gather(summed[4].astype(jnp.bfloat16), "blk", axis=0, tiled=True).astype(
            jnp.float32
        ),
        lax.all_gather(summed[5].astype(jnp.bfloat16), "blk", axis=0, tiled=True).astype(
            jnp.float32
        ),
        lax.all_gather(summed[6].astype(jnp.bfloat16), "blk", axis=0, tiled=True).astype(
            jnp.float32
        ),
        lax.all_gather(summed[7].astype(jnp.bfloat16), "blk", axis=0, tiled=True).astype(
            jnp.float32
        ),
        lax.all_gather(summed[8].astype(jnp.bfloat16), "blk", axis=0, tiled=True).astype(
            jnp.float32
        ),
        lax.all_gather(summed[9].astype(jnp.bfloat16), "blk", axis=0, tiled=True).astype(
            jnp.float32
        ),
        lax.all_gather(summed[10].astype(jnp.bfloat16), "blk", axis=0, tiled=True).astype(
            jnp.float32
        ),
        lax.all_gather(summed[11].astype(jnp.bfloat16), "blk", axis=0, tiled=True).astype(
            jnp.float32
        ),
        lax.all_gather(summed[12].astype(jnp.bfloat16), "blk", axis=0, tiled=True).astype(
            jnp.float32
        ),
    )


def local(
    tokens,
    counts,
    ln1_gain,
    ln1_shift,
    w_qkv,
    bias_q,
    bias_v,
    w_out,
    bias_out,
    ln2_gain,
    ln2_shift,
    w_fc1,
    bias_fc1,
    w_fc2,
    bias_fc2,
    cotangent,
):
    cube_count, row_count, width = tokens.shape
    head_count = HEADS
    depth = HD
    score_scale = HD ** (-0.5)
    inputs = tokens.astype(jnp.float32)
    gain_one = ln1_gain.astype(jnp.float32)
    shift_one = ln1_shift.astype(jnp.float32)
    gain_two = ln2_gain.astype(jnp.float32)
    shift_two = ln2_shift.astype(jnp.float32)
    normed = norm_rows(inputs, gain_one, shift_one).astype(jnp.bfloat16)
    project = jnp.dot(normed, w_qkv, preferred_element_type=jnp.float32)
    queries = (project[..., :width] + bias_q.astype(jnp.float32)).astype(jnp.bfloat16)
    key_local = project[..., width : 2 * width].astype(jnp.bfloat16)
    value_local = (project[..., 2 * width :] + bias_v.astype(jnp.float32)).astype(jnp.bfloat16)
    key_all, value_all = (
        lax.all_gather(key_local, "blk", axis=1, tiled=True),
        lax.all_gather(value_local, "blk", axis=1, tiled=True),
    )
    seq_rows = key_all.shape[1]
    block_rows = math.gcd(seq_rows, 512)
    block_count = seq_rows // block_rows
    block_steps = jnp.arange(block_count, dtype=jnp.int32)
    query_heads = queries.reshape(cube_count, row_count, head_count, depth)

    def key_slices(offset):
        key_part = lax.dynamic_slice_in_dim(key_all, offset, block_rows, 1).reshape(
            cube_count, block_rows, head_count, depth
        )
        value_part = lax.dynamic_slice_in_dim(value_all, offset, block_rows, 1).reshape(
            cube_count, block_rows, head_count, depth
        )
        usable = cube_valid(counts, offset, block_rows)[:, None, None, :]
        return (key_part, value_part, usable)

    def forward_block(carry, step_index):
        row_top, row_total, accum = carry
        key_part, value_part, usable = key_slices(step_index * block_rows)
        scores = (
            jnp.einsum("cqhd,ckhd->chqk", query_heads, key_part, preferred_element_type=jnp.float32)
            * score_scale
        )
        masked = jnp.where(usable, scores, MASK_LOW)
        new_top = jnp.maximum(row_top, jnp.max(masked, axis=-1))
        factor = jnp.exp(row_top - new_top)
        weights = jnp.where(usable, jnp.exp(masked - new_top[..., None]), 0.0)
        row_total = row_total * factor + jnp.sum(weights, axis=-1)
        accum = accum * jnp.transpose(factor, (0, 2, 1))[..., None] + jnp.einsum(
            "chqk,ckhd->cqhd",
            weights.astype(jnp.bfloat16),
            value_part,
            preferred_element_type=jnp.float32,
        )
        return ((new_top, row_total, accum), None)

    start_carry = (
        jnp.full((cube_count, head_count, row_count), MASK_LOW, jnp.float32),
        jnp.zeros((cube_count, head_count, row_count), jnp.float32),
        jnp.zeros((cube_count, row_count, head_count, depth), jnp.float32),
    )
    (row_top, row_total, accum), _ = lax.scan(forward_block, start_carry, block_steps)
    attended_f = (accum / jnp.transpose(row_total, (0, 2, 1))[..., None]).reshape(
        cube_count, row_count, width
    )
    log_total = row_top + jnp.log(row_total)
    attended = attended_f.astype(jnp.bfloat16)
    middle = (
        inputs
        + jnp.dot(attended, w_out, preferred_element_type=jnp.float32)
        + bias_out.astype(jnp.float32)
    )
    normed_two = norm_rows(middle, gain_two, shift_two).astype(jnp.bfloat16)
    hidden = jnp.dot(normed_two, w_fc1, preferred_element_type=jnp.float32) + bias_fc1.astype(
        jnp.float32
    )
    active = gelu_exact(hidden).astype(jnp.bfloat16)
    output = (
        middle
        + jnp.dot(active, w_fc2, preferred_element_type=jnp.float32)
        + bias_fc2.astype(jnp.float32)
    ).astype(jnp.bfloat16)
    grad_bias_fc2 = jnp.sum(cotangent.astype(jnp.float32), axis=(0, 1))
    grad_w_fc2 = jnp.einsum("ctf,ctd->fd", active, cotangent, preferred_element_type=jnp.float32)
    back_active = jnp.einsum("ctd,fd->ctf", cotangent, w_fc2, preferred_element_type=jnp.float32)
    _, gelu_pull = jax.vjp(gelu_exact, hidden)
    back_hidden = gelu_pull(back_active)[0]
    grad_bias_fc1 = jnp.sum(back_hidden, axis=(0, 1))
    hidden_low = back_hidden.astype(jnp.bfloat16)
    grad_w_fc1 = jnp.einsum(
        "ctd,ctf->df", normed_two, hidden_low, preferred_element_type=jnp.float32
    )
    back_normed_two = jnp.einsum(
        "ctf,df->ctd", hidden_low, w_fc1, preferred_element_type=jnp.float32
    )
    _, norm_pull_two = jax.vjp(norm_rows, middle, gain_two, shift_two)
    back_middle_norm, grad_ln2_gain, grad_ln2_shift = norm_pull_two(back_normed_two)
    back_middle = cotangent.astype(jnp.float32) + back_middle_norm
    mlp_grads = (
        grad_ln2_gain,
        grad_ln2_shift,
        grad_w_fc1,
        grad_bias_fc1,
        grad_w_fc2,
        grad_bias_fc2,
    )
    grad_bias_out = jnp.sum(back_middle, axis=(0, 1))
    middle_low = back_middle.astype(jnp.bfloat16)
    grad_w_out = jnp.einsum("ctd,cte->de", attended, middle_low, preferred_element_type=jnp.float32)
    back_attended = jnp.einsum(
        "cte,de->ctd", middle_low, w_out, preferred_element_type=jnp.float32
    ).astype(jnp.bfloat16)
    back_heads = back_attended.reshape(cube_count, row_count, head_count, depth)
    delta = jnp.transpose(
        jnp.sum(
            (back_attended.astype(jnp.float32) * attended_f).reshape(
                cube_count, row_count, head_count, depth
            ),
            axis=-1,
        ),
        (0, 2, 1),
    )

    def block_grads(key_part, value_part, usable):
        scores = (
            jnp.einsum("cqhd,ckhd->chqk", query_heads, key_part, preferred_element_type=jnp.float32)
            * score_scale
        )
        probs = jnp.where(usable, jnp.exp(scores - log_total[..., None]), 0.0)
        back_probs = jnp.einsum(
            "cqhd,ckhd->chqk", back_heads, value_part, preferred_element_type=jnp.float32
        )
        back_scores = (probs * (back_probs - delta[..., None])).astype(jnp.bfloat16)
        return (probs, back_scores)

    query_zero = jnp.zeros((cube_count, row_count, head_count, depth), jnp.float32)

    def back_block(carry, step_index):
        back_query, key_grads, value_grads = carry
        offset = step_index * block_rows
        key_part, value_part, usable = key_slices(offset)
        probs, back_scores = block_grads(key_part, value_part, usable)
        back_query = (
            back_query
            + jnp.einsum(
                "chqk,ckhd->cqhd", back_scores, key_part, preferred_element_type=jnp.float32
            )
            * score_scale
        )
        key_block = (
            jnp.einsum(
                "chqk,cqhd->ckhd", back_scores, query_heads, preferred_element_type=jnp.float32
            )
            * score_scale
        )
        value_block = jnp.einsum(
            "chqk,cqhd->ckhd",
            probs.astype(jnp.bfloat16),
            back_heads,
            preferred_element_type=jnp.float32,
        )
        key_grads = lax.dynamic_update_slice_in_dim(
            key_grads, key_block.reshape(cube_count, block_rows, width), offset, 1
        )
        value_grads = lax.dynamic_update_slice_in_dim(
            value_grads, value_block.reshape(cube_count, block_rows, width), offset, 1
        )
        return ((back_query, key_grads, value_grads), None)

    full_zero = jnp.zeros((cube_count, seq_rows, width), jnp.float32)
    (back_query, key_grads, value_grads), _ = lax.scan(
        back_block, (query_zero, full_zero, full_zero), block_steps
    )
    key_back, value_back = (
        lax.psum_scatter(
            key_grads.astype(jnp.bfloat16), "blk", scatter_dimension=1, tiled=True
        ).astype(jnp.float32),
        lax.psum_scatter(
            value_grads.astype(jnp.bfloat16), "blk", scatter_dimension=1, tiled=True
        ).astype(jnp.float32),
    )
    query_low = back_query.reshape(cube_count, row_count, width).astype(jnp.bfloat16)
    key_low = key_back.astype(jnp.bfloat16)
    value_low = value_back.astype(jnp.bfloat16)
    grad_bias_q = jnp.sum(query_low.astype(jnp.float32), axis=(0, 1))
    grad_bias_v = jnp.sum(value_low.astype(jnp.float32), axis=(0, 1))
    back_project = jnp.concatenate([query_low, key_low, value_low], axis=-1)
    grad_w_qkv = jnp.einsum("ctd,cte->de", normed, back_project, preferred_element_type=jnp.float32)
    back_normed = jnp.einsum("cte,de->ctd", back_project, w_qkv, preferred_element_type=jnp.float32)
    _, norm_pull_one = jax.vjp(norm_rows, inputs, gain_one, shift_one)
    back_inputs, grad_ln1_gain, grad_ln1_shift = norm_pull_one(back_normed)
    input_grad = back_middle + back_inputs
    attn_grads = (
        grad_ln1_gain,
        grad_ln1_shift,
        grad_w_qkv,
        grad_bias_q,
        grad_bias_v,
        grad_w_out,
        grad_bias_out,
    )
    every_grad = total_every(attn_grads + mlp_grads)
    attn_grads = every_grad[:7]
    mlp_grads = every_grad[7:]
    return (
        output,
        input_grad,
        attn_grads[0],
        attn_grads[1],
        attn_grads[2],
        attn_grads[3],
        attn_grads[4],
        attn_grads[5],
        attn_grads[6],
        mlp_grads[0],
        mlp_grads[1],
        mlp_grads[2],
        mlp_grads[3],
        mlp_grads[4],
        mlp_grads[5],
    )


F32 = jnp.float32
BF16 = jnp.bfloat16
EXP_SCALE = math.log2(math.e) / 8
LANES = 128
VMEM = pl.BlockSpec(memory_space=pltpu.VMEM)
SMEM = pl.BlockSpec(memory_space=pltpu.SMEM)


def lasting(micros):
    return pl.CostEstimate(flops=micros * 10**9, bytes_accessed=2**20, transcendentals=0)


def shape_of(shape, dtype):
    return jax.ShapeDtypeStruct(shape, dtype)


def limits(mib):
    return pltpu.CompilerParams(vmem_limit_bytes=mib * 2**20)


def dot_nt(a, b):
    return lax.dot_general(a, b, (((1,), (1,)), ((), ())), preferred_element_type=F32)


def dot_nn(a, b):
    return lax.dot_general(a, b, (((1,), (0,)), ((), ())), preferred_element_type=F32)


def dot_tn(a, b):
    return lax.dot_general(a, b, (((0,), (0,)), ((), ())), preferred_element_type=F32)


def centred(values):
    centre = values - jnp.mean(values, axis=1, keepdims=True)
    spread = jnp.mean(centre * centre, axis=1, keepdims=True)
    return centre, lax.rsqrt(spread + NORM_EPS)


def norm_back(centre, recip, back, gain):
    unit = centre * recip
    grad = back * gain
    inner = jnp.mean(grad * unit, axis=1, keepdims=True)
    return unit, recip * (grad - jnp.mean(grad, axis=1, keepdims=True) - unit * inner)


def prepare_kernel(a, b, out_a, out_b, *, counts):
    out_a[...] = a[...].astype(F32)
    out_b[...] = b[...].astype(F32)


def prepare(a, b):
    return pl.pallas_call(
        functools.partial(prepare_kernel, counts=None),
        in_specs=[VMEM] * 2,
        out_specs=[VMEM] * 2,
        out_shape=[shape_of(a.shape, F32), shape_of(b.shape, F32)],
        cost_estimate=lasting(1),
        name="prepare",
    )(a, b)


def project_kernel(x13, x2, vecs, w, q_ref, kv_ref, *, which):
    gain, shift, bias_q, bias_v = (vecs[i : i + 1, :] for i in range(4))
    for i in range(2):
        x = x2[...] if which == "full" and i == 1 else x13[i]
        rows = x.shape[0]
        centre, recip = centred(x.astype(F32))
        normed = (centre * recip * gain + shift).astype(BF16)
        at = pl.ds(i * rows, rows)
        q_ref[at, :] = (dot_nn(normed, w[:, :768]) + bias_q).astype(BF16)
        kv_ref[0, at, :] = dot_nn(normed, w[:, 768:1536]).astype(BF16)
        kv_ref[1, at, :] = (dot_nn(normed, w[:, 1536:]) + bias_v).astype(BF16)


def project(x13, x2, vecs, w, which):
    n = 2 * x2.shape[0]
    return pl.pallas_call(
        functools.partial(project_kernel, which=which),
        in_specs=[VMEM] * 4,
        out_specs=[VMEM] * 2,
        out_shape=[shape_of((n, 768), BF16), shape_of((2, n, 768), BF16)],
        compiler_params=limits(40),
        cost_estimate=lasting(n // 160),
        name="project",
    )(x13, x2, vecs, w)


def three_parts(values, lane):
    high = values.astype(BF16)
    rest = values - high.astype(F32)
    middle = rest.astype(BF16)
    least = (rest - middle.astype(F32)).astype(BF16)
    zero = jnp.zeros((), BF16)
    return jnp.where(
        lane == 0, high, jnp.where(lane == 1, middle, jnp.where(lane == 2, least, zero))
    )


def lane_index(rows=1):
    return lax.broadcasted_iota(jnp.int32, (rows, LANES), 1)


def attend_kernel(*refs, pieces, valid, step):
    q_ref = refs[0]
    kvs = refs[1 : 1 + pieces]
    o_ref, t_ref = refs[1 + pieces :]
    lane = lane_index()
    low = lane < 64
    half = lane % 64
    total = sum(kv.shape[1] for kv in kvs)
    keys, values = [], []
    for h in range(2):
        own = low if h == 0 else ~low
        key_parts, value_parts, at = [], [], 0
        for kv in kvs:
            n = kv.shape[1]
            beside = jnp.zeros((n, LANES), BF16)
            if at + n > valid:
                place = lax.broadcasted_iota(jnp.int32, (n, LANES), 0) + at
                beside = jnp.where(
                    (place >= valid) & (lane_index(n) % 64 == 0), MASK_LOW, 0.0
                ).astype(BF16)
            key_parts.append(jnp.where(own, kv[0], beside))
            value_parts.append(jnp.where(own, kv[1], jnp.ones((), BF16)))
            at += n
        keys.append(key_parts)
        values.append(value_parts)
    for s in range(q_ref.shape[0] // step):
        at = pl.ds(s * step, step)
        q = q_ref[at, :]
        sums, tops = [], []
        for h in range(2):
            own = low if h == 0 else ~low
            q_own = q
            if total > valid:
                q_own = jnp.where(own, q, jnp.where(half == 0, 1.0, 0.0).astype(BF16))
            scores = [dot_nt(q_own, k) for k in keys[h]]
            top = functools.reduce(
                jnp.maximum, [jnp.max(x, axis=1, keepdims=True) for x in scores]
            )
            scaled_top = top * EXP_SCALE
            weights = [jnp.exp2(x * EXP_SCALE - scaled_top).astype(BF16) for x in scores]
            sums.append(
                functools.reduce(jnp.add, [dot_nn(p, v) for p, v in zip(weights, values[h])])
            )
            tops.append(top)
        above = jnp.where(low, sums[0], sums[1])
        below = jnp.where(low, sums[1], sums[0])
        o_ref[at, :] = above / pltpu.roll(below, 64, 1)
        log_total = -(jnp.where(low, tops[1], tops[0]) + 8.0 * jnp.log(below))
        t_ref[at, :] = jnp.where(half == 3, jnp.ones((), BF16), three_parts(log_total, half))


def attend(q, kvs, valid, rows, step, first=0, count=6):
    n = q.shape[0]
    keys = sum(kv.shape[1] for kv in kvs)
    block = pl.BlockSpec((rows, LANES), lambda p, i: (i, p))
    return pl.pallas_call(
        functools.partial(attend_kernel, pieces=len(kvs), valid=valid, step=step),
        out_shape=[shape_of((n, LANES * count), F32), shape_of((n, LANES * count), BF16)],
        grid=(count, n // rows),
        in_specs=[pl.BlockSpec((rows, LANES), lambda p, i: (i, first + p))]
        + [pl.BlockSpec((2, kv.shape[1], LANES), lambda p, i: (0, 0, first + p)) for kv in kvs],
        out_specs=[block, block],
        compiler_params=limits(56),
        cost_estimate=lasting(n * keys * count // 280000),
        name="attend",
    )(q, *kvs)


def attend_back_kernel(*refs, pieces, valid, step):
    q_ref, do_ref, o_ref, t_ref = refs[:4]
    kvs = refs[4 : 4 + pieces]
    dq_ref = refs[4 + pieces]
    dkvs = refs[5 + pieces :]
    n = q_ref.shape[0]
    lane = lane_index()
    low = lane < 64
    half = lane % 64
    q, do, t = q_ref[...], do_ref[...], t_ref[...]
    product = do.astype(F32) * o_ref[...]
    delta = [
        jnp.sum(jnp.where(low, product, 0.0), axis=1, keepdims=True),
        jnp.sum(jnp.where(low, 0.0, product), axis=1, keepdims=True),
    ]
    d = three_parts(-jnp.where(low, delta[1], delta[0]), half)
    queries = [jnp.where(low, q, t), jnp.where(low, t, q)]
    backs = [jnp.where(low, do, d), jnp.where(low, d, do)]
    ones = jnp.where(half < 3, 1.0, 0.0).astype(BF16)
    sums = [jnp.zeros((LANES, n), F32), jnp.zeros((LANES, n), F32)]
    start = 0
    for kv, dkv in zip(kvs, dkvs):
        for first in range(0, kv.shape[1], step):
            size = min(step, kv.shape[1] - first)
            at = pl.ds(first, size)
            key_sums, value_sums = [], []
            for h in range(2):
                own = low if h == 0 else ~low
                beside = ones
                if start + first + size > valid:
                    place = lax.broadcasted_iota(jnp.int32, (size, LANES), 0) + (start + first)
                    wide = lane_index(size) % 64
                    beside = jnp.where(
                        wide < 3, 1.0, jnp.where((place >= valid) & (wide == 3), MASK_LOW, 0.0)
                    ).astype(BF16)
                key = jnp.where(own, kv[0, at, :], beside)
                value = jnp.where(own, kv[1, at, :], ones)
                probs = jnp.exp2(dot_nt(key, queries[h]) * EXP_SCALE)
                back_scores = (probs * dot_nt(value, backs[h])).astype(BF16)
                value_sums.append(dot_nn(probs.astype(BF16), backs[h]))
                key_sums.append(dot_nn(back_scores, queries[h]))
                sums[h] = sums[h] + dot_tn(key, back_scores)
            dkv[0, at, :] = (jnp.where(low, key_sums[0], key_sums[1]) * 0.125).astype(BF16)
            dkv[1, at, :] = jnp.where(low, value_sums[0], value_sums[1]).astype(BF16)
        start += kv.shape[1]
    both = jnp.concatenate([sums[0][:64], sums[1][64:]], axis=0)
    dq_ref[...] = (both.T * 0.125).astype(BF16)


def attend_back(q, do, first_row, o, t, kvs, valid, step, first, count):
    n = q.shape[0]
    keys = sum(kv.shape[1] for kv in kvs)
    row = first_row // n
    block = pl.BlockSpec((n, LANES), lambda p: (0, first + p))
    back_block = pl.BlockSpec((n, LANES), lambda p: (row, first + p))
    wide = [pl.BlockSpec((2, kv.shape[1], LANES), lambda p: (0, 0, first + p)) for kv in kvs]
    out = pl.BlockSpec((n, LANES), lambda p: (0, p))
    out_wide = [pl.BlockSpec((2, kv.shape[1], LANES), lambda p: (0, 0, p)) for kv in kvs]
    return pl.pallas_call(
        functools.partial(attend_back_kernel, pieces=len(kvs), valid=valid, step=step),
        out_shape=[shape_of((n, LANES * count), BF16)]
        + [shape_of((2, kv.shape[1], LANES * count), BF16) for kv in kvs],
        grid=(count,),
        in_specs=[block, back_block, out, out] + wide,
        out_specs=[out] + out_wide,
        compiler_params=limits(56),
        cost_estimate=lasting(n * keys * count // 180000),
        name="attend_back",
    )(q, do, o, t, *kvs)


def fill_part(where, send, keep, j, block):
    left, right = block[:, :384], block[:, 384:]
    first = where[0] == 0
    for ref, half in (
        (keep, jnp.where(first, left, right)),
        (send, jnp.where(first, right, left)),
    ):
        for p in range(16):
            ref[p ^ where[1], pl.ds(j * 48, 48), :] = half[p * 48 : (p + 1) * 48]


def fill_lines(where, send, keep, start, lines):
    left, right = lines[:, :384], lines[:, 384:]
    first = where[0] == 0
    for ref, half in (
        (keep, jnp.where(first, left, right)),
        (send, jnp.where(first, right, left)),
    ):
        for p in range(16):
            row = half[p : p + 1] if p < lines.shape[0] else jnp.zeros((1, 384), F32)
            ref[p ^ where[1], pl.ds(start, 16), :] = jnp.concatenate(
                [row, jnp.zeros((15, 384), F32)], axis=0
            ).astype(BF16)


def attended_rows(att_one, att_two, att_short, i, rows):
    if i == 2:
        return att_short[...].astype(BF16)
    at = pl.ds(i * rows, rows)
    return jnp.concatenate([att_one[at, :].astype(BF16), att_two[at, :].astype(BF16)], axis=1)


def feed_kernel(
    where, att_one, att_two, att_short, x13, x2, c13, c2, w_out, vecs, w1, b1, w2,
    o13, o2, mid, normed, hidden_low, send, keep, gb1,
    out_sum, cot, active,
    *, steps, tile,
):
    j = pl.program_id(0)
    xs, cots, outs = (x13.at[0], x2, x13.at[1]), (c13.at[0], c2, c13.at[1]), (o13.at[0], o2, o13.at[1])
    rows = x2.shape[0]
    bias_out, gain, shift, b2 = (vecs[i : i + 1, :] for i in range(4))

    def at(i):
        return pl.ds(i * rows, rows)

    @pl.when(j == 0)
    def _():
        for i in range(3):
            att = attended_rows(att_one, att_two, att_short, i, rows)
            m = xs[i][...].astype(F32) + dot_nn(att, w_out[...]) + bias_out
            mid[at(i), :] = m
            centre, recip = centred(m)
            normed[at(i), :] = (centre * recip * gain + shift).astype(BF16)
            cot[at(i), :] = cots[i][...]
            out_sum[at(i), :] = m + b2

    w1_tile, w2_tile = w1[...], w2[...]
    bias = b1[...]
    bias_sum = jnp.zeros((1, tile), F32)
    for i in range(3):
        h = dot_nn(normed[at(i), :], w1_tile) + bias
        back_active = dot_nt(cot[at(i), :], w2_tile)
        share = 0.5 + 0.5 * lax.erf(h * math.sqrt(0.5))
        act = (h * share).astype(BF16)
        slope = share + h * (math.sqrt(0.5 / math.pi) * jnp.exp(h * h * (-0.5)))
        back_hidden = back_active * slope
        bias_sum = bias_sum + jnp.sum(back_hidden, axis=0, keepdims=True)
        active[at(i), :] = act
        hidden_low[at(i), :] = back_hidden.astype(BF16)
        out_sum[at(i), :] += dot_nn(act, w2_tile)
    gb1[...] = bias_sum
    grad = dot_tn(active[...], cot[...]).astype(BF16)
    fill_part(where, send, keep, 0, grad)

    @pl.when(j == steps - 1)
    def _():
        for i in range(3):
            outs[i][...] = out_sum[at(i), :].astype(BF16)


def feed(where, att_one, att_two, att_short, xs, cots, w_out, vecs, w1, b1, w2):
    rows = xs[1].shape[0]
    n = rows * 3
    wide = w1.shape[1]
    tile = 768
    steps = wide // tile
    across = pl.BlockSpec((768, tile), lambda j: (0, j))
    down = pl.BlockSpec((tile, 768), lambda j: (j, 0))
    line = pl.BlockSpec((1, tile), lambda j: (0, j))
    return pl.pallas_call(
        functools.partial(feed_kernel, steps=steps, tile=tile),
        grid=(steps,),
        in_specs=[SMEM] + [VMEM] * 9 + [across, line, down],
        out_specs=[VMEM] * 4
        + [pl.BlockSpec((n, tile), lambda j: (0, j))]
        + [pl.BlockSpec((16, 48, 384), lambda j: (0, j, 0))] * 2
        + [line],
        out_shape=[shape_of((2, rows, 768), BF16), shape_of((rows, 768), BF16)]
        + [
            shape_of((n, 768), F32),
            shape_of((n, 768), BF16),
            shape_of((n, wide), BF16),
            shape_of((16, 48 * steps, 384), BF16),
            shape_of((16, 48 * steps, 384), BF16),
            shape_of((1, wide), F32),
        ],
        scratch_shapes=[
            pltpu.VMEM((n, 768), F32),
            pltpu.VMEM((n, 768), BF16),
            pltpu.VMEM((n, tile), BF16),
        ],
        compiler_params=limits(60),
        cost_estimate=lasting(36),
        name="feed",
    )(where, att_one, att_two, att_short, *xs, *cots, w_out, vecs, w1, b1, w2)


def feed_back_kernel(
    where, att_one, att_two, att_short, c13, c2, w_out, vecs, mid, normed, hidden_low, w1,
    back_att, back_mid, send, keep, sums,
    back_sum, flipped, low_mid, att,
    *, steps,
):
    j = pl.program_id(0)
    cots = (c13.at[0], c2, c13.at[1])
    rows = c2.shape[0]
    gain = vecs[1:2, :]

    def at(i):
        return pl.ds(i * rows, rows)

    @pl.when(j == 0)
    def _():
        flipped[...] = normed[...].T
        for i in range(3):
            back_sum[at(i), :] = jnp.zeros((rows, 768), F32)

    @pl.when(j < steps)
    def _():
        for i in range(3):
            back_sum[at(i), :] += dot_nt(hidden_low[at(i), :], w1[...])
        fill_part(where, send, keep, 0, dot_nn(flipped[...], hidden_low[...]).astype(BF16))

    @pl.when(j == steps)
    def _():
        zero = jnp.zeros((1, 768), F32)
        grad_out, grad_gain, grad_shift, grad_b2 = zero, zero, zero, zero
        for i in range(3):
            centre, recip = centred(mid[at(i), :])
            back = back_sum[at(i), :]
            unit, through = norm_back(centre, recip, back, gain)
            c = cots[i][...].astype(F32)
            m = c + through
            grad_gain = grad_gain + jnp.sum(back * unit, axis=0, keepdims=True)
            grad_shift = grad_shift + jnp.sum(back, axis=0, keepdims=True)
            grad_out = grad_out + jnp.sum(m, axis=0, keepdims=True)
            grad_b2 = grad_b2 + jnp.sum(c, axis=0, keepdims=True)
            back_mid[at(i), :] = m
            low = m.astype(BF16)
            low_mid[at(i), :] = low
            back_att[at(i), :] = dot_nt(low, w_out[...]).astype(BF16)
            att[at(i), :] = attended_rows(att_one, att_two, att_short, i, rows)
        fill_part(where, send, keep, 0, dot_tn(att[...], low_mid[...]).astype(BF16))
        sums[...] = jnp.concatenate(
            [grad_out, grad_gain, grad_shift, grad_b2, zero, zero, zero, zero], axis=0
        )


def feed_back(where, att_one, att_two, att_short, cots, w_out, vecs, mid, normed, hidden_low, w1):
    rows = cots[1].shape[0]
    n = rows * 3
    wide = w1.shape[1]
    tile = 768
    steps = wide // tile
    part = pl.BlockSpec((16, 48, 384), lambda j: (0, j, 0))
    return pl.pallas_call(
        functools.partial(feed_back_kernel, steps=steps),
        grid=(steps + 1,),
        in_specs=[SMEM]
        + [VMEM] * 9
        + [
            pl.BlockSpec((n, tile), lambda j: (0, jnp.minimum(j, steps - 1))),
            pl.BlockSpec((768, tile), lambda j: (0, jnp.minimum(j, steps - 1))),
        ],
        out_specs=[VMEM, VMEM, part, part, VMEM],
        out_shape=[
            shape_of((n, 768), BF16),
            shape_of((n, 768), F32),
            shape_of((16, 48 * (steps + 1), 384), BF16),
            shape_of((16, 48 * (steps + 1), 384), BF16),
            shape_of((8, 768), F32),
        ],
        scratch_shapes=[
            pltpu.VMEM((n, 768), F32),
            pltpu.VMEM((768, n), BF16),
            pltpu.VMEM((n, 768), BF16),
            pltpu.VMEM((n, 768), BF16),
        ],
        compiler_params=limits(60),
        cost_estimate=lasting(26),
        name="feed_back",
    )(where, att_one, att_two, att_short, *cots, w_out, vecs, mid, normed, hidden_low, w1)


def last_kernel(
    where, x13, x2, vecs, w, back_mid, dq_one, dq_two, dq_short, own_one, own_two, got_one, got_two,
    own_short, got_short, sums, gb1, o13, o2, send, keep,
    back, normed,
):
    rows = x2.shape[0]
    full = dq_one.shape[0]
    gain, shift = vecs[0:1, :], vecs[1:2, :]
    back[:full, :384] = dq_one[...]
    back[:full, 384:768] = dq_two[...]
    back[full:, :768] = dq_short[...]
    for k in range(2):
        start = 768 * (k + 1)
        for i, (own, got) in enumerate(((own_one, got_one), (own_two, got_two))):
            at = pl.ds(start + 384 * i, 384)
            back[:full, at] = (own[k].astype(F32) + got[k].astype(F32)).astype(BF16)
        at = pl.ds(start, 768)
        back[full:, at] = (own_short[k].astype(F32) + got_short[k].astype(F32)).astype(BF16)
    zero = jnp.zeros((1, 768), F32)
    grad_gain, grad_shift = zero, zero
    for i, (x, out) in enumerate(((x13.at[0], o13.at[0]), (x2, o2), (x13.at[1], o13.at[1]))):
        at = pl.ds(i * rows, rows)
        centre, recip = centred(x[...].astype(F32))
        normed[at, :] = (centre * recip * gain + shift).astype(BF16)
        back_normed = dot_nt(back[at, :], w[...])
        unit, through = norm_back(centre, recip, back_normed, gain)
        grad_gain = grad_gain + jnp.sum(back_normed * unit, axis=0, keepdims=True)
        grad_shift = grad_shift + jnp.sum(back_normed, axis=0, keepdims=True)
        out[...] = (back_mid[at, :] + through).astype(BF16)
    flipped = normed[...].T
    for k in range(3):
        fill_part(where, send, keep, k, dot_nn(flipped, back[:, k * 768 : (k + 1) * 768]).astype(BF16))
    lines = [
        grad_gain,
        grad_shift,
        jnp.sum(back[:, :768].astype(F32), axis=0, keepdims=True),
        jnp.sum(back[:, 1536:].astype(F32), axis=0, keepdims=True),
    ]
    lines += [gb1[:, k * 768 : (k + 1) * 768] for k in range(gb1.shape[1] // 768)]
    fill_lines(where, send, keep, 144, jnp.concatenate([sums[:4, :]] + lines, axis=0))


def last(where, xs, vecs, w, back_mid, *backs):
    rows = xs[1].shape[0]
    n = rows * 3
    return pl.pallas_call(
        last_kernel,
        in_specs=[SMEM] + [VMEM] * 16,
        out_specs=[VMEM] * 4,
        out_shape=[shape_of((2, rows, 768), BF16), shape_of((rows, 768), BF16)] + [shape_of((16, 160, 384), BF16)] * 2,
        scratch_shapes=[pltpu.VMEM((n, 2304), BF16), pltpu.VMEM((n, 768), BF16)],
        compiler_params=limits(60),
        cost_estimate=lasting(18),
        name="last",
    )(where, *xs, vecs, w, back_mid, *backs)


def finish_kernel(source, out):
    for chip in range(4):
        for core in range(2):
            for z in range(4):
                out[pl.ds((chip * 4 + z) * 48, 48), pl.ds(core * 384, 384)] = source[
                    chip, core, z
                ].astype(F32)


def finish(source, count, across):
    shape = (768, 768 * count) if across else (768 * count, 768)
    return pl.pallas_call(
        finish_kernel,
        grid=(count,),
        in_specs=[pl.BlockSpec((4, 2, 4, 48, 384), lambda j: (0, 0, 0, j, 0))],
        out_specs=pl.BlockSpec((768, 768), (lambda j: (0, j)) if across else (lambda j: (j, 0))),
        out_shape=shape_of(shape, F32),
        compiler_params=limits(40),
        cost_estimate=lasting(4),
        name="finish",
    )(source)


def finish_one(source, index):
    return pl.pallas_call(
        finish_kernel,
        grid=(1,),
        in_specs=[pl.BlockSpec((4, 2, 4, 48, 384), lambda j: (0, 0, 0, index, 0))],
        out_specs=pl.BlockSpec((768, 768), lambda j: (0, 0)),
        out_shape=shape_of((768, 768), F32),
        compiler_params=limits(40),
        cost_estimate=lasting(4),
        name="finish",
    )(source)


def finish_near_kernel(where, mine, other, mine_rows, other_rows, out, lines):
    first = where[0] == 0
    for q in range(16):
        a, b = mine[q // 4, q % 4].astype(F32), other[q // 4, q % 4].astype(F32)
        at = pl.ds(pl.multiple_of((q ^ where[1]) * 48, 48), 48)
        out[at, :384] = jnp.where(first, a, b)
        out[at, 384:] = jnp.where(first, b, a)

    @pl.when(pl.program_id(0) == 0)
    def _():
        for q in range(16):
            a = mine_rows[q // 4, q % 4, 0:1, :].astype(F32)
            b = other_rows[q // 4, q % 4, 0:1, :].astype(F32)
            lines[pl.ds(q ^ where[1], 1), :] = jnp.concatenate(
                [jnp.where(first, a, b), jnp.where(first, b, a)], axis=1
            )


def finish_near(where, mine, other, count):
    block = pl.BlockSpec((4, 4, 48, 384), lambda j: (0, 0, j, 0))
    spare = pl.BlockSpec((4, 4, 16, 384), lambda j: (0, 0, 3 * count, 0))
    return pl.pallas_call(
        finish_near_kernel,
        grid=(count,),
        in_specs=[SMEM, block, block, spare, spare],
        out_specs=[
            pl.BlockSpec((768, 768), lambda j: (0, j)),
            pl.BlockSpec((16, 768), lambda j: (0, 0)),
        ],
        out_shape=[shape_of((768, 768 * count), F32), shape_of((16, 768), F32)],
        compiler_params=limits(40),
        cost_estimate=lasting(4),
        name="finish_near",
    )(where, mine, other, mine, other)


FIRST_TO = {
    (0, 0): (0, 0), (0, 1): (0, 1), (0, 2): (1, 0), (0, 3): (1, 1),
    (1, 0): (0, 2), (1, 1): (0, 3), (1, 2): (1, 2), (1, 3): (1, 3),
}
SECOND_TO = {
    (0, 0): (0, 1), (0, 1): (0, 0), (0, 2): (1, 1), (0, 3): (1, 0),
    (1, 0): (0, 3), (1, 1): (0, 2), (1, 2): (1, 3), (1, 3): (1, 2),
}


def column_pairs(table):
    pairs = []
    for chip in range(4):
        for (core, z), (core_to, z_to) in table.items():
            pairs.append(((chip * 2 + core) * 4 + z, (chip * 2 + core_to) * 4 + z_to))
    return pairs


def flip_pairs(size, mask):
    return [(i, i ^ mask) for i in range(size)]


def swap(array, axis, mask):
    return lax.ppermute(array, axis, flip_pairs(8 if axis == "dp" else 4, mask))


def add_low(*terms):
    return sum(term.astype(F32) for term in terms).astype(BF16)


class Place:
    def __init__(self):
        dp = lax.axis_index("dp")
        self.z = lax.axis_index("blk")
        self.core = dp % 2
        self.chip = dp // 2


def after(value, *others):
    return lax.optimization_barrier((value,) + others)[0]


def by_chip(keep, got):
    return [add_low(keep[4 * k : 4 * k + 4], got[4 * k : 4 * k + 4]) for k in range(4)]


def over_chips(sums):
    return [swap(sums[k], "dp", 2 * k) for k in (1, 2, 3)]


def over_line(quarter):
    return [swap(quarter[k], "blk", k) for k in (1, 2, 3)]


def gather_all(part):
    every = lax.all_gather(part, ("dp", "blk"), axis=0)
    return every.reshape((4, 2, 4) + every.shape[1:])


def local_paired(
    tokens,
    counts,
    ln1_gain,
    ln1_shift,
    w_qkv,
    bias_q,
    bias_v,
    w_out,
    bias_out,
    ln2_gain,
    ln2_shift,
    w_fc1,
    bias_fc1,
    w_fc2,
    bias_fc2,
    cotangent,
):
    place = Place()
    odd = place.z % 2
    short = jnp.argmin(counts).astype(jnp.int32)
    full_one = jnp.where(short == 0, 1, 0)
    full_two = jnp.where(short == 2, 1, 2)
    slots = (jnp.where(odd == 0, full_one, full_two), jnp.where(odd == 0, full_two, full_one), short)
    tables = (FIRST_TO, SECOND_TO, FIRST_TO)

    def arrange(pieces):
        (one, three), two = pieces
        return jnp.stack(
            [
                jnp.where(slots[0] == i, one, jnp.where(slots[1] == i, two, three))
                for i in range(3)
            ]
        )

    first_core = place.core == 0
    where = jnp.stack([place.core, place.chip * 4 + place.z]).astype(jnp.int32)

    def leaving(array):
        pieces = [lax.dynamic_index_in_dim(array, slot, 0, keepdims=False) for slot in slots]
        return jnp.stack([pieces[0], pieces[2]]), pieces[1]

    def move(pieces):
        return tuple(
            lax.ppermute(piece, ("dp", "blk"), column_pairs(table))
            for piece, table in zip(pieces, (FIRST_TO, SECOND_TO))
        )

    def give(pieces):
        return tuple(
            lax.ppermute(piece, ("dp", "blk"), [pair[::-1] for pair in column_pairs(table)])
            for piece, table in zip(pieces, (FIRST_TO, SECOND_TO))
        )

    wide = w_fc1.shape[1] // 768
    rows = tokens.shape[1]
    vectors = [ln1_gain, ln1_shift, bias_q, bias_v, bias_out, ln2_gain, ln2_shift, bias_fc2]
    vecs, b1 = prepare(jnp.stack(vectors), bias_fc1.reshape(1, -1))
    vecs_one, vecs_two = vecs[:4], vecs[4:]
    token_sends = leaving(tokens)
    x13, x2 = move(token_sends)
    xs = (x13, x2)
    cot_sends = leaving(after(cotangent, *token_sends))
    x3 = after(x13[1], x2, vecs, *cot_sends)
    x_near = swap(x3, "blk", 1)
    q_full, kv_full = project(x13, after(x2, x3), vecs_one, w_qkv, "full")
    kv_other = swap(kv_full, "dp", 1)
    cots = move(after(cot_sends, kv_full))
    seq = 2 * kv_full.shape[1]
    kv_both = [kv_full, kv_other]
    att_one, t_one = attend(q_full, kv_both, seq, 768, 384, 0, 3)
    x_near = after(x_near, att_one)
    x_pair = jnp.stack([jnp.where(odd == 0, x3, x_near), jnp.where(odd == 0, x_near, x3)])
    q_pair, kv_pair = project(x_pair, x2, vecs_one, w_qkv, "pair")
    q_short = lax.dynamic_slice_in_dim(q_pair, odd * rows, rows, 0)
    kv_far = swap(kv_pair, "dp", 1)
    att_two, t_two = attend(after(q_full, kv_pair, q_short), kv_both, seq, 768, 384, 3, 3)
    kv_far = after(kv_far, att_two)
    kv_head = jnp.where(first_core, kv_pair, kv_far)
    spare = -(-(SHORT - kv_head.shape[1]) // LANES) * LANES
    kv_tail = jnp.where(first_core, kv_far[:, :spare], kv_pair[:, :spare])
    kv_short = [kv_head, kv_tail]
    att_short, t_short = attend(q_short, kv_short, SHORT, 384, 384)
    cots = after(cots, att_short)
    o13, o2, mid, normed_two, hidden_low, send_a, keep_a, gb1 = feed(
        where, att_one, att_two, att_short, xs, cots, w_out, vecs_two, w_fc1, b1, w_fc2
    )
    got_a = swap(send_a, "dp", 1)
    home = give((o13, o2))
    sums_a = by_chip(keep_a, got_a)
    chips_a = over_chips(sums_a)
    back_att, back_mid, send_b, keep_b, feed_sums = feed_back(
        where, att_one, att_two, att_short, cots, w_out, vecs_two, after(mid, *sums_a), normed_two,
        hidden_low, w_fc1,
    )
    home = after(home, back_mid)
    quarter_a = add_low(after(sums_a[0], back_mid, *home), *chips_a)
    line_a = over_line(quarter_a)
    got_b = swap(after(send_b, quarter_a), "dp", 1)

    n_full = q_full.shape[0]
    dq_short, d_head, d_tail = attend_back(
        after(q_short, quarter_a), back_att, n_full, att_short, t_short, kv_short, SHORT, 448, 0, 6
    )
    d_tail = jnp.pad(d_tail, ((0, 0), (0, d_head.shape[1] - spare), (0, 0)))
    d_send = jnp.where(first_core, d_tail, d_head)
    part_a = add_low(after(quarter_a[0], dq_short), *line_a)
    all_a = gather_all(part_a)
    sums_b = by_chip(after(keep_b, dq_short, part_a), got_b)
    chips_b = over_chips(sums_b)
    got_pair = swap(after(d_send, sums_b[0]), "dp", 1)
    d_pair = add_low(jnp.where(first_core, d_head, d_tail), got_pair)
    own_short = lax.dynamic_slice_in_dim(d_pair, odd * rows, rows, 1)
    send_short = lax.dynamic_slice_in_dim(d_pair, (1 - odd) * rows, rows, 1)
    got_short = swap(send_short, "blk", 1)
    dq_one, own_one, sent_one = attend_back(
        after(q_full, send_short), back_att, 0, att_one, t_one, kv_both, seq, 768, 0, 3
    )
    dq_two, own_two, sent_two = attend_back(
        after(q_full, dq_one), back_att, 0, att_two, t_two, kv_both, seq, 768, 3, 3
    )
    got_short = after(got_short, dq_two)
    quarter_b = add_low(after(sums_b[0], dq_two, got_short), *chips_b)
    line_b = over_line(quarter_b)
    got_one = swap(after(sent_one, quarter_b), "dp", 1)
    got_two = swap(after(sent_two, quarter_b), "dp", 1)
    i13, i2, send_c, keep_c = last(
        where, xs, vecs_one, w_qkv, back_mid, dq_one, dq_two, dq_short, own_one, own_two,
        got_one, got_two, own_short, got_short, feed_sums, gb1,
    )
    part_b = add_low(after(quarter_b[0], i2), *line_b)
    got_c = swap(after(send_c, part_b), "dp", 1)
    all_b = gather_all(part_b)
    grads_home = give(after((i13, i2), part_b))
    output = arrange(after(home, i2))
    sums_c = by_chip(after(keep_c, part_b, output), got_c)
    chips_c = over_chips(sums_c)
    grad_w_fc2 = finish(after(all_a, *sums_c), wide, False)
    grads_home = after(grads_home, grad_w_fc2)
    quarter_c = add_low(after(sums_c[0], grad_w_fc2, *grads_home), *chips_c)
    line_c = over_line(quarter_c)
    part_c = add_low(quarter_c[0], *line_c)
    near_c = jnp.stack([part_c] + over_line([part_c] * 4))
    whole_c = jnp.stack([near_c] + over_chips([near_c] * 4))
    other_c = swap(whole_c, "dp", 1)
    input_grad = arrange(after(grads_home, near_c)).astype(F32)
    all_b = after(all_b, input_grad)
    grad_w_fc1 = finish(all_b, wide, True)
    grad_w_out = finish_one(all_b, wide)
    grad_w_qkv, lines = finish_near(where, whole_c, other_c, 3)
    return (
        output,
        input_grad,
        lines[4],
        lines[5],
        grad_w_qkv,
        lines[6],
        lines[7],
        grad_w_out,
        lines[0],
        lines[1],
        lines[2],
        grad_w_fc1,
        lines[8 : 8 + wide].reshape(-1),
        grad_w_fc2,
        lines[3],
    )


def solution(mesh):
    paired = mesh.shape["dp"] == 8 and mesh.shape["blk"] == 4
    chosen = local_paired if paired else local
    return jax.shard_map(
        chosen,
        mesh=mesh,
        in_specs=(
            P("dp", "blk", None),
            P("dp"),
            P(),
            P(),
            P(),
            P(),
            P(),
            P(),
            P(),
            P(),
            P(),
            P(),
            P(),
            P(),
            P(),
            P("dp", "blk", None),
        ),
        out_specs=(
            P("dp", "blk", None),
            P("dp", "blk", None),
            P(),
            P(),
            P(),
            P(),
            P(),
            P(),
            P(),
            P(),
            P(),
            P(),
            P(),
            P(),
            P(),
        ),
        check_vma=False,
    )
```

```python
import functools
import math

import jax
import jax.numpy as jnp
from jax import lax
from jax.experimental import pallas as pl
from jax.experimental.pallas import tpu as pltpu
from jax.sharding import PartitionSpec as P

HEADS = 12
HD = 64
SHORT = 864


NORM_EPS = 1e-06
MASK_LOW = -1e30


def norm_rows(values, gain, shift):
    centre = values - jnp.mean(values, axis=-1, keepdims=True)
    spread = jnp.mean(centre * centre, axis=-1, keepdims=True)
    return centre * lax.rsqrt(spread + NORM_EPS) * gain + shift


def gelu_exact(values):
    return jax.nn.gelu(values, approximate=False)


def cube_valid(counts, offset, length):
    places = offset + jnp.arange(length, dtype=jnp.int32)
    return places[None, :] < counts[:, None]


def total_every(parts):
    split = (
        lax.psum_scatter(
            parts[0].astype(jnp.bfloat16), "blk", scatter_dimension=0, tiled=True
        ).astype(jnp.float32),
        lax.psum_scatter(
            parts[1].astype(jnp.bfloat16), "blk", scatter_dimension=0, tiled=True
        ).astype(jnp.float32),
        lax.psum_scatter(
            parts[2].astype(jnp.bfloat16), "blk", scatter_dimension=0, tiled=True
        ).astype(jnp.float32),
        lax.psum_scatter(
            parts[3].astype(jnp.bfloat16), "blk", scatter_dimension=0, tiled=True
        ).astype(jnp.float32),
        lax.psum_scatter(
            parts[4].astype(jnp.bfloat16), "blk", scatter_dimension=0, tiled=True
        ).astype(jnp.float32),
        lax.psum_scatter(
            parts[5].astype(jnp.bfloat16), "blk", scatter_dimension=0, tiled=True
        ).astype(jnp.float32),
        lax.psum_scatter(
            parts[6].astype(jnp.bfloat16), "blk", scatter_dimension=0, tiled=True
        ).astype(jnp.float32),
        lax.psum_scatter(
            parts[7].astype(jnp.bfloat16), "blk", scatter_dimension=0, tiled=True
        ).astype(jnp.float32),
        lax.psum_scatter(
            parts[8].astype(jnp.bfloat16), "blk", scatter_dimension=0, tiled=True
        ).astype(jnp.float32),
        lax.psum_scatter(
            parts[9].astype(jnp.bfloat16), "blk", scatter_dimension=0, tiled=True
        ).astype(jnp.float32),
        lax.psum_scatter(
            parts[10].astype(jnp.bfloat16), "blk", scatter_dimension=0, tiled=True
        ).astype(jnp.float32),
        lax.psum_scatter(
            parts[11].astype(jnp.bfloat16), "blk", scatter_dimension=0, tiled=True
        ).astype(jnp.float32),
        lax.psum_scatter(
            parts[12].astype(jnp.bfloat16), "blk", scatter_dimension=0, tiled=True
        ).astype(jnp.float32),
    )
    summed = (
        lax.psum(split[0].astype(jnp.bfloat16), "dp").astype(jnp.float32),
        lax.psum(split[1].astype(jnp.bfloat16), "dp").astype(jnp.float32),
        lax.psum(split[2].astype(jnp.bfloat16), "dp").astype(jnp.float32),
        lax.psum(split[3].astype(jnp.bfloat16), "dp").astype(jnp.float32),
        lax.psum(split[4].astype(jnp.bfloat16), "dp").astype(jnp.float32),
        lax.psum(split[5].astype(jnp.bfloat16), "dp").astype(jnp.float32),
        lax.psum(split[6].astype(jnp.bfloat16), "dp").astype(jnp.float32),
        lax.psum(split[7].astype(jnp.bfloat16), "dp").astype(jnp.float32),
        lax.psum(split[8].astype(jnp.bfloat16), "dp").astype(jnp.float32),
        lax.psum(split[9].astype(jnp.bfloat16), "dp").astype(jnp.float32),
        lax.psum(split[10].astype(jnp.bfloat16), "dp").astype(jnp.float32),
        lax.psum(split[11].astype(jnp.bfloat16), "dp").astype(jnp.float32),
        lax.psum(split[12].astype(jnp.bfloat16), "dp").astype(jnp.float32),
    )
    return (
        lax.all_gather(summed[0].astype(jnp.bfloat16), "blk", axis=0, tiled=True).astype(
            jnp.float32
        ),
        lax.all_gather(summed[1].astype(jnp.bfloat16), "blk", axis=0, tiled=True).astype(
            jnp.float32
        ),
        lax.all_gather(summed[2].astype(jnp.bfloat16), "blk", axis=0, tiled=True).astype(
            jnp.float32
        ),
        lax.all_gather(summed[3].astype(jnp.bfloat16), "blk", axis=0, tiled=True).astype(
            jnp.float32
        ),
        lax.all_gather(summed[4].astype(jnp.bfloat16), "blk", axis=0, tiled=True).astype(
            jnp.float32
        ),
        lax.all_gather(summed[5].astype(jnp.bfloat16), "blk", axis=0, tiled=True).astype(
            jnp.float32
        ),
        lax.all_gather(summed[6].astype(jnp.bfloat16), "blk", axis=0, tiled=True).astype(
            jnp.float32
        ),
        lax.all_gather(summed[7].astype(jnp.bfloat16), "blk", axis=0, tiled=True).astype(
            jnp.float32
        ),
        lax.all_gather(summed[8].astype(jnp.bfloat16), "blk", axis=0, tiled=True).astype(
            jnp.float32
        ),
        lax.all_gather(summed[9].astype(jnp.bfloat16), "blk", axis=0, tiled=True).astype(
            jnp.float32
        ),
        lax.all_gather(summed[10].astype(jnp.bfloat16), "blk", axis=0, tiled=True).astype(
            jnp.float32
        ),
        lax.all_gather(summed[11].astype(jnp.bfloat16), "blk", axis=0, tiled=True).astype(
            jnp.float32
        ),
        lax.all_gather(summed[12].astype(jnp.bfloat16), "blk", axis=0, tiled=True).astype(
            jnp.float32
        ),
    )


def local(
    tokens,
    counts,
    ln1_gain,
    ln1_shift,
    w_qkv,
    bias_q,
    bias_v,
    w_out,
    bias_out,
    ln2_gain,
    ln2_shift,
    w_fc1,
    bias_fc1,
    w_fc2,
    bias_fc2,
    cotangent,
):
    cube_count, row_count, width = tokens.shape
    head_count = HEADS
    depth = HD
    score_scale = HD ** (-0.5)
    inputs = tokens.astype(jnp.float32)
    gain_one = ln1_gain.astype(jnp.float32)
    shift_one = ln1_shift.astype(jnp.float32)
    gain_two = ln2_gain.astype(jnp.float32)
    shift_two = ln2_shift.astype(jnp.float32)
    normed = norm_rows(inputs, gain_one, shift_one).astype(jnp.bfloat16)
    project = jnp.dot(normed, w_qkv, preferred_element_type=jnp.float32)
    queries = (project[..., :width] + bias_q.astype(jnp.float32)).astype(jnp.bfloat16)
    key_local = project[..., width : 2 * width].astype(jnp.bfloat16)
    value_local = (project[..., 2 * width :] + bias_v.astype(jnp.float32)).astype(jnp.bfloat16)
    key_all, value_all = (
        lax.all_gather(key_local, "blk", axis=1, tiled=True),
        lax.all_gather(value_local, "blk", axis=1, tiled=True),
    )
    seq_rows = key_all.shape[1]
    block_rows = math.gcd(seq_rows, 512)
    block_count = seq_rows // block_rows
    block_steps = jnp.arange(block_count, dtype=jnp.int32)
    query_heads = queries.reshape(cube_count, row_count, head_count, depth)

    def key_slices(offset):
        key_part = lax.dynamic_slice_in_dim(key_all, offset, block_rows, 1).reshape(
            cube_count, block_rows, head_count, depth
        )
        value_part = lax.dynamic_slice_in_dim(value_all, offset, block_rows, 1).reshape(
            cube_count, block_rows, head_count, depth
        )
        usable = cube_valid(counts, offset, block_rows)[:, None, None, :]
        return (key_part, value_part, usable)

    def forward_block(carry, step_index):
        row_top, row_total, accum = carry
        key_part, value_part, usable = key_slices(step_index * block_rows)
        scores = (
            jnp.einsum("cqhd,ckhd->chqk", query_heads, key_part, preferred_element_type=jnp.float32)
            * score_scale
        )
        masked = jnp.where(usable, scores, MASK_LOW)
        new_top = jnp.maximum(row_top, jnp.max(masked, axis=-1))
        factor = jnp.exp(row_top - new_top)
        weights = jnp.where(usable, jnp.exp(masked - new_top[..., None]), 0.0)
        row_total = row_total * factor + jnp.sum(weights, axis=-1)
        accum = accum * jnp.transpose(factor, (0, 2, 1))[..., None] + jnp.einsum(
            "chqk,ckhd->cqhd",
            weights.astype(jnp.bfloat16),
            value_part,
            preferred_element_type=jnp.float32,
        )
        return ((new_top, row_total, accum), None)

    start_carry = (
        jnp.full((cube_count, head_count, row_count), MASK_LOW, jnp.float32),
        jnp.zeros((cube_count, head_count, row_count), jnp.float32),
        jnp.zeros((cube_count, row_count, head_count, depth), jnp.float32),
    )
    (row_top, row_total, accum), _ = lax.scan(forward_block, start_carry, block_steps)
    attended_f = (accum / jnp.transpose(row_total, (0, 2, 1))[..., None]).reshape(
        cube_count, row_count, width
    )
    log_total = row_top + jnp.log(row_total)
    attended = attended_f.astype(jnp.bfloat16)
    middle = (
        inputs
        + jnp.dot(attended, w_out, preferred_element_type=jnp.float32)
        + bias_out.astype(jnp.float32)
    )
    normed_two = norm_rows(middle, gain_two, shift_two).astype(jnp.bfloat16)
    hidden = jnp.dot(normed_two, w_fc1, preferred_element_type=jnp.float32) + bias_fc1.astype(
        jnp.float32
    )
    active = gelu_exact(hidden).astype(jnp.bfloat16)
    output = (
        middle
        + jnp.dot(active, w_fc2, preferred_element_type=jnp.float32)
        + bias_fc2.astype(jnp.float32)
    ).astype(jnp.bfloat16)
    grad_bias_fc2 = jnp.sum(cotangent.astype(jnp.float32), axis=(0, 1))
    grad_w_fc2 = jnp.einsum("ctf,ctd->fd", active, cotangent, preferred_element_type=jnp.float32)
    back_active = jnp.einsum("ctd,fd->ctf", cotangent, w_fc2, preferred_element_type=jnp.float32)
    _, gelu_pull = jax.vjp(gelu_exact, hidden)
    back_hidden = gelu_pull(back_active)[0]
    grad_bias_fc1 = jnp.sum(back_hidden, axis=(0, 1))
    hidden_low = back_hidden.astype(jnp.bfloat16)
    grad_w_fc1 = jnp.einsum(
        "ctd,ctf->df", normed_two, hidden_low, preferred_element_type=jnp.float32
    )
    back_normed_two = jnp.einsum(
        "ctf,df->ctd", hidden_low, w_fc1, preferred_element_type=jnp.float32
    )
    _, norm_pull_two = jax.vjp(norm_rows, middle, gain_two, shift_two)
    back_middle_norm, grad_ln2_gain, grad_ln2_shift = norm_pull_two(back_normed_two)
    back_middle = cotangent.astype(jnp.float32) + back_middle_norm
    mlp_grads = (
        grad_ln2_gain,
        grad_ln2_shift,
        grad_w_fc1,
        grad_bias_fc1,
        grad_w_fc2,
        grad_bias_fc2,
    )
    grad_bias_out = jnp.sum(back_middle, axis=(0, 1))
    middle_low = back_middle.astype(jnp.bfloat16)
    grad_w_out = jnp.einsum("ctd,cte->de", attended, middle_low, preferred_element_type=jnp.float32)
    back_attended = jnp.einsum(
        "cte,de->ctd", middle_low, w_out, preferred_element_type=jnp.float32
    ).astype(jnp.bfloat16)
    back_heads = back_attended.reshape(cube_count, row_count, head_count, depth)
    delta = jnp.transpose(
        jnp.sum(
            (back_attended.astype(jnp.float32) * attended_f).reshape(
                cube_count, row_count, head_count, depth
            ),
            axis=-1,
        ),
        (0, 2, 1),
    )

    def block_grads(key_part, value_part, usable):
        scores = (
            jnp.einsum("cqhd,ckhd->chqk", query_heads, key_part, preferred_element_type=jnp.float32)
            * score_scale
        )
        probs = jnp.where(usable, jnp.exp(scores - log_total[..., None]), 0.0)
        back_probs = jnp.einsum(
            "cqhd,ckhd->chqk", back_heads, value_part, preferred_element_type=jnp.float32
        )
        back_scores = (probs * (back_probs - delta[..., None])).astype(jnp.bfloat16)
        return (probs, back_scores)

    query_zero = jnp.zeros((cube_count, row_count, head_count, depth), jnp.float32)

    def back_block(carry, step_index):
        back_query, key_grads, value_grads = carry
        offset = step_index * block_rows
        key_part, value_part, usable = key_slices(offset)
        probs, back_scores = block_grads(key_part, value_part, usable)
        back_query = (
            back_query
            + jnp.einsum(
                "chqk,ckhd->cqhd", back_scores, key_part, preferred_element_type=jnp.float32
            )
            * score_scale
        )
        key_block = (
            jnp.einsum(
                "chqk,cqhd->ckhd", back_scores, query_heads, preferred_element_type=jnp.float32
            )
            * score_scale
        )
        value_block = jnp.einsum(
            "chqk,cqhd->ckhd",
            probs.astype(jnp.bfloat16),
            back_heads,
            preferred_element_type=jnp.float32,
        )
        key_grads = lax.dynamic_update_slice_in_dim(
            key_grads, key_block.reshape(cube_count, block_rows, width), offset, 1
        )
        value_grads = lax.dynamic_update_slice_in_dim(
            value_grads, value_block.reshape(cube_count, block_rows, width), offset, 1
        )
        return ((back_query, key_grads, value_grads), None)

    full_zero = jnp.zeros((cube_count, seq_rows, width), jnp.float32)
    (back_query, key_grads, value_grads), _ = lax.scan(
        back_block, (query_zero, full_zero, full_zero), block_steps
    )
    key_back, value_back = (
        lax.psum_scatter(
            key_grads.astype(jnp.bfloat16), "blk", scatter_dimension=1, tiled=True
        ).astype(jnp.float32),
        lax.psum_scatter(
            value_grads.astype(jnp.bfloat16), "blk", scatter_dimension=1, tiled=True
        ).astype(jnp.float32),
    )
    query_low = back_query.reshape(cube_count, row_count, width).astype(jnp.bfloat16)
    key_low = key_back.astype(jnp.bfloat16)
    value_low = value_back.astype(jnp.bfloat16)
    grad_bias_q = jnp.sum(query_low.astype(jnp.float32), axis=(0, 1))
    grad_bias_v = jnp.sum(value_low.astype(jnp.float32), axis=(0, 1))
    back_project = jnp.concatenate([query_low, key_low, value_low], axis=-1)
    grad_w_qkv = jnp.einsum("ctd,cte->de", normed, back_project, preferred_element_type=jnp.float32)
    back_normed = jnp.einsum("cte,de->ctd", back_project, w_qkv, preferred_element_type=jnp.float32)
    _, norm_pull_one = jax.vjp(norm_rows, inputs, gain_one, shift_one)
    back_inputs, grad_ln1_gain, grad_ln1_shift = norm_pull_one(back_normed)
    input_grad = back_middle + back_inputs
    attn_grads = (
        grad_ln1_gain,
        grad_ln1_shift,
        grad_w_qkv,
        grad_bias_q,
        grad_bias_v,
        grad_w_out,
        grad_bias_out,
    )
    every_grad = total_every(attn_grads + mlp_grads)
    attn_grads = every_grad[:7]
    mlp_grads = every_grad[7:]
    return (
        output,
        input_grad,
        attn_grads[0],
        attn_grads[1],
        attn_grads[2],
        attn_grads[3],
        attn_grads[4],
        attn_grads[5],
        attn_grads[6],
        mlp_grads[0],
        mlp_grads[1],
        mlp_grads[2],
        mlp_grads[3],
        mlp_grads[4],
        mlp_grads[5],
    )


F32 = jnp.float32
BF16 = jnp.bfloat16
EXP_SCALE = math.log2(math.e) / 8
LANES = 128
VMEM = pl.BlockSpec(memory_space=pltpu.VMEM)
SMEM = pl.BlockSpec(memory_space=pltpu.SMEM)
ANY = pl.BlockSpec(memory_space=pl.ANY)


def lasting(micros):
    return pl.CostEstimate(flops=micros * 10**9, bytes_accessed=2**20, transcendentals=0)


def shape_of(shape, dtype):
    return jax.ShapeDtypeStruct(shape, dtype)


def limits(mib):
    return pltpu.CompilerParams(vmem_limit_bytes=mib * 2**20)


def dot_nt(a, b):
    return lax.dot_general(a, b, (((1,), (1,)), ((), ())), preferred_element_type=F32)


def dot_nn(a, b):
    return lax.dot_general(a, b, (((1,), (0,)), ((), ())), preferred_element_type=F32)


def dot_tn(a, b):
    return lax.dot_general(a, b, (((0,), (0,)), ((), ())), preferred_element_type=F32)


def centred(values):
    centre = values - jnp.mean(values, axis=1, keepdims=True)
    spread = jnp.mean(centre * centre, axis=1, keepdims=True)
    return centre, lax.rsqrt(spread + NORM_EPS)


def norm_back(centre, recip, back, gain):
    unit = centre * recip
    grad = back * gain
    inner = jnp.mean(grad * unit, axis=1, keepdims=True)
    return unit, recip * (grad - jnp.mean(grad, axis=1, keepdims=True) - unit * inner)


def prepare_kernel(a, b, out_a, out_b, *, counts):
    out_a[...] = a[...].astype(F32)
    out_b[...] = b[...].astype(F32)


def prepare(a, b):
    return pl.pallas_call(
        functools.partial(prepare_kernel, counts=None),
        in_specs=[VMEM] * 2,
        out_specs=[VMEM] * 2,
        out_shape=[shape_of(a.shape, F32), shape_of(b.shape, F32)],
        cost_estimate=lasting(1),
        name="prepare",
    )(a, b)


def project_rows(x, vecs, w, q_ref, kv_ref, at, q_at=None):
    gain, shift, bias_q, bias_v = (vecs[i : i + 1, :] for i in range(4))
    centre, recip = centred(x.astype(F32))
    normed = (centre * recip * gain + shift).astype(BF16)
    kv_ref[0, at, :] = dot_nn(normed, w[:, 768:1536]).astype(BF16)
    kv_ref[1, at, :] = (dot_nn(normed, w[:, 1536:]) + bias_v).astype(BF16)
    if q_at is not None:
        q_ref[q_at, :] = (dot_nn(normed, w[:, :768]) + bias_q).astype(BF16)


def project_kernel(x13_in, x2_in, vecs, w_in, q_ref, kv_ref, held, w, sems):
    copies = start_copies([x13_in.at[0], x2_in, w_in], [held.at[0], held.at[1], w], sems)
    for copy in copies:
        copy.wait()
    rows = held.shape[1]
    for i in range(2):
        at = pl.ds(i * rows, rows)
        project_rows(held[i], vecs, w, q_ref, kv_ref, at, at)


def project(x13, x2, vecs, w):
    n = 2 * x2.shape[0]
    return pl.pallas_call(
        project_kernel,
        in_specs=[ANY, ANY, VMEM, ANY],
        out_specs=[VMEM] * 2,
        out_shape=[shape_of((n, 768), BF16), shape_of((2, n, 768), BF16)],
        scratch_shapes=[
            pltpu.VMEM((2,) + x2.shape, BF16),
            pltpu.VMEM(w.shape, w.dtype),
            pltpu.SemaphoreType.DMA((3,)),
        ],
        compiler_params=limits(40),
        cost_estimate=lasting(4),
        name="project",
    )(x13, x2, vecs, w)


def project_short_kernel(
    where, x13, near, other, far, vecs, w_in, q_ref, head_ref, tail_ref, w, held, sems, *, spare
):
    (copy,) = start_copies([w_in], [w], sems)
    rows = near.shape[0]
    mine = where[2]
    for k, block in enumerate((x13[1], near[...], other[...], far[...])):
        held[k ^ mine] = block
    copy.wait()
    for i in range(2):
        project_rows(held[i], vecs, w, None, head_ref, pl.ds(i * rows, rows))
    project_rows(held[2][:spare], vecs, w, None, tail_ref, pl.ds(0, spare))
    centre, recip = centred(x13[1].astype(F32))
    normed = (centre * recip * vecs[0:1, :] + vecs[1:2, :]).astype(BF16)
    q_ref[...] = (dot_nn(normed, w[:, :768]) + vecs[2:3, :]).astype(BF16)


def project_short(where, x13, near, other, far, vecs, w, spare):
    rows = near.shape[0]
    return pl.pallas_call(
        functools.partial(project_short_kernel, spare=spare),
        in_specs=[SMEM] + [VMEM] * 5 + [ANY],
        out_specs=[VMEM] * 3,
        out_shape=[
            shape_of((rows, 768), BF16),
            shape_of((2, 2 * rows, 768), BF16),
            shape_of((2, spare, 768), BF16),
        ],
        scratch_shapes=[
            pltpu.VMEM(w.shape, w.dtype),
            pltpu.VMEM((4, rows, 768), BF16),
            pltpu.SemaphoreType.DMA((1,)),
        ],
        compiler_params=limits(40),
        cost_estimate=lasting(4),
        name="project_short",
    )(where, x13, near, other, far, vecs, w)


def start_copies(sources, targets, sems):
    copies = [
        pltpu.make_async_copy(source, target, sems.at[i])
        for i, (source, target) in enumerate(zip(sources, targets))
    ]
    for copy in copies:
        copy.start()
    return copies


def three_parts(values, lane):
    high = values.astype(BF16)
    rest = values - high.astype(F32)
    middle = rest.astype(BF16)
    least = (rest - middle.astype(F32)).astype(BF16)
    zero = jnp.zeros((), BF16)
    return jnp.where(
        lane == 0, high, jnp.where(lane == 1, middle, jnp.where(lane == 2, least, zero))
    )


def lane_index(rows=1):
    return lax.broadcasted_iota(jnp.int32, (rows, LANES), 1)


def attend_kernel(*refs, pieces, valid, step):
    q_ref = refs[0]
    kvs = refs[1 : 1 + pieces]
    o_ref, t_ref = refs[1 + pieces :]
    lane = lane_index()
    low = lane < 64
    half = lane % 64
    total = sum(kv.shape[1] for kv in kvs)
    keys, values = [], []
    for h in range(2):
        own = low if h == 0 else ~low
        key_parts, value_parts, at = [], [], 0
        for kv in kvs:
            n = kv.shape[1]
            beside = jnp.zeros((n, LANES), BF16)
            if at + n > valid:
                place = lax.broadcasted_iota(jnp.int32, (n, LANES), 0) + at
                beside = jnp.where(
                    (place >= valid) & (lane_index(n) % 64 == 0), MASK_LOW, 0.0
                ).astype(BF16)
            key_parts.append(jnp.where(own, kv[0], beside))
            value_parts.append(jnp.where(own, kv[1], jnp.ones((), BF16)))
            at += n
        keys.append(key_parts)
        values.append(value_parts)
    for s in range(q_ref.shape[0] // step):
        at = pl.ds(s * step, step)
        q = q_ref[at, :]
        sums, tops = [], []
        for h in range(2):
            own = low if h == 0 else ~low
            q_own = q
            if total > valid:
                q_own = jnp.where(own, q, jnp.where(half == 0, 1.0, 0.0).astype(BF16))
            scores = [dot_nt(q_own, k) for k in keys[h]]
            top = functools.reduce(
                jnp.maximum, [jnp.max(x, axis=1, keepdims=True) for x in scores]
            )
            scaled_top = top * EXP_SCALE
            weights = [jnp.exp2(x * EXP_SCALE - scaled_top).astype(BF16) for x in scores]
            sums.append(
                functools.reduce(jnp.add, [dot_nn(p, v) for p, v in zip(weights, values[h])])
            )
            tops.append(top)
        above = jnp.where(low, sums[0], sums[1])
        below = jnp.where(low, sums[1], sums[0])
        o_ref[at, :] = above / pltpu.roll(below, 64, 1)
        log_total = -(jnp.where(low, tops[1], tops[0]) + 8.0 * jnp.log(below))
        t_ref[at, :] = jnp.where(half == 3, jnp.ones((), BF16), three_parts(log_total, half))


def attend(q, kvs, valid, rows, step, first=0, count=6):
    n = q.shape[0]
    keys = sum(kv.shape[1] for kv in kvs)
    block = pl.BlockSpec((rows, LANES), lambda p, i: (i, p))
    return pl.pallas_call(
        functools.partial(attend_kernel, pieces=len(kvs), valid=valid, step=step),
        out_shape=[shape_of((n, LANES * count), F32), shape_of((n, LANES * count), BF16)],
        grid=(count, n // rows),
        in_specs=[pl.BlockSpec((rows, LANES), lambda p, i: (i, first + p))]
        + [pl.BlockSpec((2, kv.shape[1], LANES), lambda p, i: (0, 0, first + p)) for kv in kvs],
        out_specs=[block, block],
        compiler_params=limits(56),
        cost_estimate=lasting(n * keys * count // 280000),
        name="attend",
    )(q, *kvs)


def attend_back_kernel(*refs, pieces, valid, step, split):
    where = refs[0]
    q_ref, do_ref, o_ref, t_ref = refs[1:5]
    kvs = refs[5 : 5 + pieces]
    dq_ref = refs[5 + pieces]
    outs = refs[6 + pieces :]
    n = q_ref.shape[0]
    lane = lane_index()
    low = lane < 64
    half = lane % 64
    q, do, t = q_ref[...], do_ref[...], t_ref[...]
    product = do.astype(F32) * o_ref[...]
    delta = [
        jnp.sum(jnp.where(low, product, 0.0), axis=1, keepdims=True),
        jnp.sum(jnp.where(low, 0.0, product), axis=1, keepdims=True),
    ]
    d = three_parts(-jnp.where(low, delta[1], delta[0]), half)
    queries = [jnp.where(low, q, t), jnp.where(low, t, q)]
    backs = [jnp.where(low, do, d), jnp.where(low, d, do)]
    ones = jnp.where(half < 3, 1.0, 0.0).astype(BF16)
    sums = [jnp.zeros((LANES, n), F32), jnp.zeros((LANES, n), F32)]
    starts = [sum(kv.shape[1] for kv in kvs[:i]) for i in range(pieces)]
    small = None
    for i in reversed(range(pieces)):
        kv = kvs[i]
        for first in range(0, kv.shape[1], step):
            size = min(step, kv.shape[1] - first)
            at = pl.ds(first, size)
            key_sums, value_sums = [], []
            for h in range(2):
                own = low if h == 0 else ~low
                beside = ones
                if starts[i] + first + size > valid:
                    place = lax.broadcasted_iota(jnp.int32, (size, LANES), 0) + (starts[i] + first)
                    wide = lane_index(size) % 64
                    beside = jnp.where(
                        wide < 3, 1.0, jnp.where((place >= valid) & (wide == 3), MASK_LOW, 0.0)
                    ).astype(BF16)
                key = jnp.where(own, kv[0, at, :], beside)
                value = jnp.where(own, kv[1, at, :], ones)
                probs = jnp.exp2(dot_nt(key, queries[h]) * EXP_SCALE)
                back_scores = (probs * dot_nt(value, backs[h])).astype(BF16)
                value_sums.append(dot_nn(probs.astype(BF16), backs[h]))
                key_sums.append(dot_nn(back_scores, queries[h]))
                sums[h] = sums[h] + dot_tn(key, back_scores)
            both = (
                (jnp.where(low, key_sums[0], key_sums[1]) * 0.125).astype(BF16),
                jnp.where(low, value_sums[0], value_sums[1]).astype(BF16),
            )
            for k in range(2):
                if not split:
                    outs[i][k, at, :] = both[k]
                elif i == 0:
                    other = jnp.zeros_like(both[k])
                    if first == 0:
                        rest = jnp.zeros((size - small[k].shape[0], LANES), BF16)
                        other = jnp.concatenate([small[k], rest], axis=0)
                    stays = where[0] == 0
                    outs[0][k, at, :] = jnp.where(stays, both[k], other)
                    outs[1][k, at, :] = jnp.where(stays, other, both[k])
            small = both
    both = jnp.concatenate([sums[0][:64], sums[1][64:]], axis=0)
    dq_ref[...] = (both.T * 0.125).astype(BF16)


def attend_back(where, q, do, first_row, o, t, kvs, valid, step, first, count, split=False):
    n = q.shape[0]
    keys = sum(kv.shape[1] for kv in kvs)
    row = first_row // n
    block = pl.BlockSpec((n, LANES), lambda p: (0, first + p))
    back_block = pl.BlockSpec((n, LANES), lambda p: (row, first + p))
    wide = [pl.BlockSpec((2, kv.shape[1], LANES), lambda p: (0, 0, first + p)) for kv in kvs]
    out = pl.BlockSpec((n, LANES), lambda p: (0, p))
    outs = [kvs[0], kvs[0]] if split else kvs
    out_wide = [pl.BlockSpec((2, kv.shape[1], LANES), lambda p: (0, 0, p)) for kv in outs]
    return pl.pallas_call(
        functools.partial(
            attend_back_kernel, pieces=len(kvs), valid=valid, step=step, split=split
        ),
        out_shape=[shape_of((n, LANES * count), BF16)]
        + [shape_of((2, kv.shape[1], LANES * count), BF16) for kv in outs],
        grid=(count,),
        in_specs=[SMEM, block, back_block, block, block] + wide,
        out_specs=[out] + out_wide,
        compiler_params=limits(56),
        cost_estimate=lasting(n * keys * count // 180000),
        name="attend_back",
    )(where, q, do, o, t, *kvs)


def fill_part(where, send, keep, j, block):
    left, right = block[:, :384], block[:, 384:]
    first = where[0] == 0
    for ref, half in (
        (keep, jnp.where(first, left, right)),
        (send, jnp.where(first, right, left)),
    ):
        for p in range(16):
            ref[p ^ where[1], pl.ds(j * 48, 48), :] = half[p * 48 : (p + 1) * 48]


def attended_rows(att_full, att_short, i, rows):
    if i == 2:
        return att_short[...].astype(BF16)
    at = pl.ds(i * rows, rows)
    return att_full[at, :].astype(BF16)


def feed_kernel(
    where, att_full_in, att_short_in, x13_in, x2_in, c13, c2, w_out_in, vecs, w1, b1, w2,
    o13, o2, mid_out, normed_out, hidden_low, send, keep, gb1,
    att_full, att_short, x13, x2, w_out, mid, normed, out_sum, cot, active, sems,
    *, steps, tile,
):
    j = pl.program_id(0)
    xs, outs = (x13.at[0], x2, x13.at[1]), (o13.at[0], o2, o13.at[1])
    rows = x2.shape[0]
    bias_out, gain, shift, b2 = (vecs[i : i + 1, :] for i in range(4))

    def at(i):
        return pl.ds(i * rows, rows)

    def leaving():
        return [
            pltpu.make_async_copy(mid, mid_out, sems.at[0]),
            pltpu.make_async_copy(normed, normed_out, sems.at[1]),
        ]

    @pl.when(j == 0)
    def _():
        copies = start_copies(
            [w_out_in, att_full_in, x13_in, x2_in, att_short_in, c13.at[0], c2, c13.at[1]],
            [w_out, att_full, x13, x2, att_short] + [cot.at[at(i), :] for i in range(3)],
            sems,
        )
        for copy in copies[:4]:
            copy.wait()
        for i in range(3):
            if i == 2:
                copies[4].wait()
            att = attended_rows(att_full, att_short, i, rows)
            m = xs[i][...].astype(F32) + dot_nn(att, w_out[...]) + bias_out
            mid[at(i), :] = m
            centre, recip = centred(m)
            normed[at(i), :] = (centre * recip * gain + shift).astype(BF16)
            out_sum[at(i), :] = m + b2
        for copy in copies[5:]:
            copy.wait()
        for copy in leaving():
            copy.start()

    w1_tile, w2_tile = w1[...], w2[...]
    bias = b1[...]
    bias_sum = jnp.zeros((1, tile), F32)
    for i in range(3):
        h = dot_nn(normed[at(i), :], w1_tile) + bias
        back_active = dot_nt(cot[at(i), :], w2_tile)
        share = 0.5 + 0.5 * lax.erf(h * math.sqrt(0.5))
        act = (h * share).astype(BF16)
        slope = share + h * (math.sqrt(0.5 / math.pi) * jnp.exp(h * h * (-0.5)))
        back_hidden = back_active * slope
        bias_sum = bias_sum + jnp.sum(back_hidden, axis=0, keepdims=True)
        active[at(i), :] = act
        hidden_low[at(i), :] = back_hidden.astype(BF16)
        out_sum[at(i), :] += dot_nn(act, w2_tile)
    gb1[...] = bias_sum
    grad = dot_tn(active[...], cot[...]).astype(BF16)
    fill_part(where, send, keep, 0, grad)

    @pl.when(j == steps - 1)
    def _():
        for copy in leaving():
            copy.wait()
        for i in range(3):
            outs[i][...] = out_sum[at(i), :].astype(BF16)


def feed(where, att_full, att_short, xs, cots, w_out, vecs, w1, b1, w2):
    rows = xs[1].shape[0]
    n = rows * 3
    wide = w1.shape[1]
    tile = 768
    steps = wide // tile
    across = pl.BlockSpec((768, tile), lambda j: (0, j))
    down = pl.BlockSpec((tile, 768), lambda j: (j, 0))
    line = pl.BlockSpec((1, tile), lambda j: (0, j))
    return pl.pallas_call(
        functools.partial(feed_kernel, steps=steps, tile=tile),
        grid=(steps,),
        in_specs=[SMEM] + [ANY] * 7 + [VMEM, across, line, down],
        out_specs=[VMEM] * 2
        + [ANY] * 2
        + [pl.BlockSpec((n, tile), lambda j: (0, j))]
        + [pl.BlockSpec((16, 48, 384), lambda j: (0, j, 0))] * 2
        + [line],
        out_shape=[shape_of((2, rows, 768), BF16), shape_of((rows, 768), BF16)]
        + [
            shape_of((n, 768), F32),
            shape_of((n, 768), BF16),
            shape_of((n, wide), BF16),
            shape_of((16, 48 * steps, 384), BF16),
            shape_of((16, 48 * steps, 384), BF16),
            shape_of((1, wide), F32),
        ],
        scratch_shapes=[
            pltpu.VMEM(v.shape, v.dtype) for v in (att_full, att_short, *xs, w_out)
        ]
        + [
            pltpu.VMEM((n, 768), F32),
            pltpu.VMEM((n, 768), BF16),
            pltpu.VMEM((n, 768), F32),
            pltpu.VMEM((n, 768), BF16),
            pltpu.VMEM((n, tile), BF16),
            pltpu.SemaphoreType.DMA((8,)),
        ],
        compiler_params=limits(60),
        cost_estimate=lasting(36),
        name="feed",
    )(where, att_full, att_short, *xs, *cots, w_out, vecs, w1, b1, w2)


def feed_back_kernel(
    where, att_full_in, att_short_in, c13_in, c2_in, w_out, vecs, mid_in, normed,
    hidden_low, w1,
    back_att, back_mid, send, keep, sums,
    back_sum, flipped, low_mid, att, att_full, att_short, c13, c2, mid, sems,
    *, steps,
):
    j = pl.program_id(0)
    late = (att_full, att_short, c13, c2, mid)
    sources = (att_full_in, att_short_in, c13_in, c2_in, mid_in)
    cots = (c13.at[0], c2, c13.at[1])
    rows = c2.shape[0]
    gain = vecs[1:2, :]

    def at(i):
        return pl.ds(i * rows, rows)

    @pl.when(j == 0)
    def _():
        start_copies(sources, late, sems)
        flipped[...] = normed[...].T
        for i in range(3):
            back_sum[at(i), :] = jnp.zeros((rows, 768), F32)

    @pl.when(j < steps)
    def _():
        for i in range(3):
            back_sum[at(i), :] += dot_nt(hidden_low[at(i), :], w1[...])
        fill_part(where, send, keep, 0, dot_nn(flipped[...], hidden_low[...]).astype(BF16))

    @pl.when(j == steps)
    def _():
        for i in range(len(late)):
            pltpu.make_async_copy(sources[i], late[i], sems.at[i]).wait()
        zero = jnp.zeros((1, 768), F32)
        grad_out, grad_gain, grad_shift, grad_b2 = zero, zero, zero, zero
        for i in range(3):
            centre, recip = centred(mid[at(i), :])
            back = back_sum[at(i), :]
            unit, through = norm_back(centre, recip, back, gain)
            c = cots[i][...].astype(F32)
            m = c + through
            grad_gain = grad_gain + jnp.sum(back * unit, axis=0, keepdims=True)
            grad_shift = grad_shift + jnp.sum(back, axis=0, keepdims=True)
            grad_out = grad_out + jnp.sum(m, axis=0, keepdims=True)
            grad_b2 = grad_b2 + jnp.sum(c, axis=0, keepdims=True)
            back_mid[at(i), :] = m
            low = m.astype(BF16)
            low_mid[at(i), :] = low
            back_att[at(i), :] = dot_nt(low, w_out[...]).astype(BF16)
            att[at(i), :] = attended_rows(att_full, att_short, i, rows)
        fill_part(where, send, keep, 0, dot_tn(att[...], low_mid[...]).astype(BF16))
        sums[...] = jnp.concatenate(
            [grad_out, grad_gain, grad_shift, grad_b2, zero, zero, zero, zero], axis=0
        )


def feed_back(where, att_full, att_short, cots, w_out, vecs, mid, normed, hidden_low, w1):
    rows = cots[1].shape[0]
    n = rows * 3
    wide = w1.shape[1]
    tile = 768
    steps = wide // tile
    part = pl.BlockSpec((16, 48, 384), lambda j: (0, j, 0))
    return pl.pallas_call(
        functools.partial(feed_back_kernel, steps=steps),
        grid=(steps + 1,),
        in_specs=[SMEM]
        + [ANY] * 4
        + [VMEM, VMEM, ANY, VMEM]
        + [
            pl.BlockSpec((n, tile), lambda j: (0, jnp.minimum(j, steps - 1))),
            pl.BlockSpec((768, tile), lambda j: (0, jnp.minimum(j, steps - 1))),
        ],
        out_specs=[VMEM, VMEM, part, part, VMEM],
        out_shape=[
            shape_of((n, 768), BF16),
            shape_of((n, 768), F32),
            shape_of((16, 48 * (steps + 1), 384), BF16),
            shape_of((16, 48 * (steps + 1), 384), BF16),
            shape_of((8, 768), F32),
        ],
        scratch_shapes=[
            pltpu.VMEM((n, 768), F32),
            pltpu.VMEM((768, n), BF16),
            pltpu.VMEM((n, 768), BF16),
            pltpu.VMEM((n, 768), BF16),
        ]
        + [
            pltpu.VMEM(v.shape, v.dtype) for v in (att_full, att_short, *cots, mid)
        ]
        + [pltpu.SemaphoreType.DMA((5,))],
        compiler_params=limits(60),
        cost_estimate=lasting(26),
        name="feed_back",
    )(where, att_full, att_short, *cots, w_out, vecs, mid, normed, hidden_low, w1)


def project_back_kernel(
    where, x13_in, x2_in, vecs, dq_full_in, dq_short_in, own_full_in, got_full_in,
    keep_short_in, got_pair_in, got_near_in, send, keep, back_out,
    x13, x2, dq_full, dq_short, own_full, got_full, keep_short, got_pair, got_near, back, flipped,
    sems,
):
    rows = x2.shape[0]
    full = dq_full.shape[0]
    gain, shift = vecs[0:1, :], vecs[1:2, :]
    odd = where[1] % 2
    own_rows = pl.ds(pl.multiple_of(odd * rows, rows), rows)
    sources = [
        x13_in, x2_in, dq_full_in, dq_short_in, own_full_in, got_full_in,
        keep_short_in.at[:, own_rows, :], got_pair_in.at[:, own_rows, :], got_near_in,
    ]
    targets = [x13, x2, dq_full, dq_short, own_full, got_full, keep_short, got_pair, got_near]
    copies = start_copies(sources, targets, sems)
    for copy in copies[:2]:
        copy.wait()
    for i, x in enumerate((x13.at[0], x2, x13.at[1])):
        centre, recip = centred(x[...].astype(F32))
        flipped[:, pl.ds(i * rows, rows)] = (centre * recip * gain + shift).astype(BF16).T
    for copy in copies[2:4]:
        copy.wait()
    back[0, :full, :] = dq_full[...]
    back[0, full:, :] = dq_short[...]
    outs = [pltpu.make_async_copy(back.at[k], back_out.at[k], sems.at[k]) for k in range(3)]
    outs[0].start()
    fill_part(where, send, keep, 0, dot_nn(flipped[...], back[0]).astype(BF16))
    for copy in copies[4:]:
        copy.wait()
    for k in range(2):
        total = own_full[k].astype(F32) + got_full[k].astype(F32)
        back[k + 1, :full, :] = total.astype(BF16)
        total = keep_short[k].astype(F32) + got_pair[k].astype(F32) + got_near[k].astype(F32)
        back[k + 1, full:, :] = total.astype(BF16)
        outs[k + 1].start()
        fill_part(where, send, keep, k + 1, dot_nn(flipped[...], back[k + 1]).astype(BF16))
    for copy in outs:
        copy.wait()


def project_back(where, xs, vecs, *backs):
    rows = xs[1].shape[0]
    n = rows * 3
    short = (2, rows, 768)
    held = [(v.shape, v.dtype) for v in (*xs, *backs[:4])] + [(short, BF16)] * 3
    return pl.pallas_call(
        project_back_kernel,
        in_specs=[SMEM, ANY, ANY, VMEM] + [ANY] * 7,
        out_specs=[VMEM] * 2 + [ANY],
        out_shape=[shape_of((16, 144, 384), BF16)] * 2 + [shape_of((3, n, 768), BF16)],
        scratch_shapes=[pltpu.VMEM(*each) for each in held]
        + [pltpu.VMEM((3, n, 768), BF16), pltpu.VMEM((768, n), BF16)]
        + [pltpu.SemaphoreType.DMA((9,))],
        compiler_params=limits(60),
        cost_estimate=lasting(11),
        name="project_back",
    )(where, *xs, vecs, *backs)


def input_back_kernel(
    where, x13, x2, vecs, w_in, back_mid, back, sums, gb1, o13, o2, lines, total, w, sems
):
    i = pl.program_id(0)
    rows = x2.shape[0]
    gain = vecs[0:1, :]

    @pl.when(i == 0)
    def _():
        (copy,) = start_copies([w_in], [w], sems)
        total[...] = jnp.zeros(total.shape, F32)
        copy.wait()

    x = jnp.where(i == 1, x2[...], x13[0])
    centre, recip = centred(x.astype(F32))
    back_normed = dot_nt(back[0], w[:, :768])
    for k in (1, 2):
        back_normed = back_normed + dot_nt(back[k], w[:, 768 * k : 768 * (k + 1)])
    unit, through = norm_back(centre, recip, back_normed, gain)
    out = (back_mid[...] + through).astype(BF16)

    @pl.when(i == 1)
    def _():
        o2[...] = out

    @pl.when(i != 1)
    def _():
        o13[0] = out

    ones = jnp.ones((8, rows), BF16)
    total[...] += jnp.concatenate(
        [
            jnp.sum(back_normed * unit, axis=0, keepdims=True),
            jnp.sum(back_normed, axis=0, keepdims=True),
            dot_nn(ones, back[0])[0:1],
            dot_nn(ones, back[2])[0:1],
            jnp.zeros((4, 768), F32),
        ],
        axis=0,
    )

    @pl.when(i == 2)
    def _():
        each = [sums[k : k + 1, :] for k in range(4)] + [total[k : k + 1, :] for k in range(4)]
        each += [gb1[:, k * 768 : (k + 1) * 768] for k in range(gb1.shape[1] // 768)]
        for k in range(16):
            block = jnp.zeros((16, 384), F32)
            if k < len(each):
                block = jnp.concatenate(
                    [each[k][:, :384], each[k][:, 384:], block[:14]], axis=0
                )
            lines[k ^ where[1]] = block.astype(BF16)


def input_back(where, xs, vecs, w, back_mid, back, sums, gb1):
    rows = xs[1].shape[0]
    return pl.pallas_call(
        input_back_kernel,
        grid=(3,),
        in_specs=[
            SMEM,
            pl.BlockSpec((1, rows, 768), lambda i: (i // 2, 0, 0)),
            VMEM,
            VMEM,
            ANY,
            pl.BlockSpec((rows, 768), lambda i: (i, 0)),
            pl.BlockSpec((3, rows, 768), lambda i: (0, i, 0)),
            VMEM,
            VMEM,
        ],
        out_specs=[pl.BlockSpec((1, rows, 768), lambda i: (i // 2, 0, 0)), VMEM, VMEM],
        out_shape=[
            shape_of((2, rows, 768), BF16),
            shape_of((rows, 768), BF16),
            shape_of((16, 16, 384), BF16),
        ],
        scratch_shapes=[
            pltpu.VMEM((8, 768), F32),
            pltpu.VMEM(w.shape, w.dtype),
            pltpu.SemaphoreType.DMA((1,)),
        ],
        compiler_params=limits(40),
        cost_estimate=lasting(9),
        name="input_back",
    )(where, *xs, vecs, w, back_mid, back, sums, gb1)


def finish_kernel(where, mine, other, *refs, with_lines):
    if with_lines:
        mine_rows, other_rows, out, *vectors, rows = refs
    else:
        (out,) = refs
    first = where[0] == 0
    for q in range(16):
        a, b = mine[q // 4, q % 4].astype(F32), other[q // 4, q % 4].astype(F32)
        at = pl.ds(pl.multiple_of((q ^ where[1]) * 48, 48), 48)
        out[at, :384] = jnp.where(first, a, b)
        out[at, 384:] = jnp.where(first, b, a)
    if not with_lines:
        return

    @pl.when(pl.program_id(0) == 0)
    def _():
        for q in range(16):
            both = mine_rows[q // 4, q % 4].astype(F32) + other_rows[q // 4, q % 4].astype(F32)
            rows[pl.ds(q ^ where[1], 1), :] = jnp.concatenate([both[0:1], both[1:2]], axis=1)
        for k in range(len(vectors) - 1):
            vectors[k][...] = rows[k, :]
        size = rows.shape[1]
        for k in range(vectors[-1].shape[0] // size):
            vectors[-1][pl.ds(k * size, size)] = rows[len(vectors) - 1 + k, :]


def finish(where, mine, other, start, count, across, with_lines=False):
    block = pl.BlockSpec((4, 4, 48, 384), lambda j: (0, 0, start + j, 0))
    spare = pl.BlockSpec((4, 4, 16, 384), lambda j: (0, 0, 3 * count, 0))
    shape = (768, 768 * count) if across else (768 * count, 768)
    result = [shape_of(shape, F32)]
    specs = [pl.BlockSpec((768, 768), (lambda j: (0, j)) if across else (lambda j: (j, 0)))]
    scratch = []
    if with_lines:
        result += [shape_of((768,), F32)] * 8 + [shape_of((3072,), F32)]
        specs += [VMEM] * 9
        scratch = [pltpu.VMEM((16, 768), F32)]
    out = pl.pallas_call(
        functools.partial(finish_kernel, with_lines=with_lines),
        grid=(count,),
        in_specs=[SMEM, block, block] + [spare, spare] * with_lines,
        out_specs=specs,
        out_shape=result,
        scratch_shapes=scratch,
        compiler_params=limits(40),
        cost_estimate=lasting(4),
        name="finish",
    )(where, mine, other, *[mine, other] * with_lines)
    return out if with_lines else out[0]


FIRST_TO = {
    (0, 0): (0, 0), (0, 1): (0, 1), (0, 2): (1, 0), (0, 3): (1, 1),
    (1, 0): (0, 2), (1, 1): (0, 3), (1, 2): (1, 2), (1, 3): (1, 3),
}
SECOND_TO = {
    (0, 0): (0, 1), (0, 1): (0, 0), (0, 2): (1, 1), (0, 3): (1, 0),
    (1, 0): (0, 3), (1, 1): (0, 2), (1, 2): (1, 3), (1, 3): (1, 2),
}


def column_pairs(table):
    pairs = []
    for chip in range(4):
        for (core, z), (core_to, z_to) in table.items():
            pairs.append(((chip * 2 + core) * 4 + z, (chip * 2 + core_to) * 4 + z_to))
    return pairs


def exchange_short(block):
    pairs = ([], [], [])
    for chip in range(4):
        for core in range(2):
            for z in range(4):
                if core == 1 and z % 2 == 1:
                    continue
                me = (chip * 2 + core) * 4 + z
                to = (chip * 2 + 1 - core) * 4
                pairs[0].append((me, (chip * 2 + core) * 4 + (z ^ 1)))
                pairs[1].append((me, to + z))
                pairs[2].append((me, to + (z ^ 1)))
    return tuple(lax.ppermute(block, ("dp", "blk"), p) for p in pairs)


CHIPS = [[0, 2, 4, 6], [1, 3, 5, 7]]


def flip_pairs(size, mask):
    return [(i, i ^ mask) for i in range(size)]


def swap(array, axis, mask):
    return lax.ppermute(array, axis, flip_pairs(8 if axis == "dp" else 4, mask))


def add_low(*terms):
    return sum(term.astype(F32) for term in terms).astype(BF16)


class Place:
    def __init__(self):
        dp = lax.axis_index("dp")
        self.z = lax.axis_index("blk")
        self.core = dp % 2
        self.chip = dp // 2


def after(value, *others):
    return lax.optimization_barrier((value,) + others)[0]


def by_chip(keep, got):
    return [add_low(keep[4 * k : 4 * k + 4], got[4 * k : 4 * k + 4]) for k in range(4)]


def over_chips(sums):
    return [swap(sums[k], "dp", 2 * k) for k in (1, 2, 3)]


def over_line(quarter):
    return [swap(quarter[k], "blk", k) for k in (1, 2, 3)]


def gather_all(part):
    every = lax.all_gather(part, ("dp", "blk"), axis=0)
    return every.reshape((4, 2, 4) + every.shape[1:])


def local_paired(
    tokens,
    counts,
    ln1_gain,
    ln1_shift,
    w_qkv,
    bias_q,
    bias_v,
    w_out,
    bias_out,
    ln2_gain,
    ln2_shift,
    w_fc1,
    bias_fc1,
    w_fc2,
    bias_fc2,
    cotangent,
):
    place = Place()
    odd = place.z % 2
    short = jnp.argmin(counts).astype(jnp.int32)
    full_one = jnp.where(short == 0, 1, 0)
    full_two = jnp.where(short == 2, 1, 2)
    slots = (jnp.where(odd == 0, full_one, full_two), jnp.where(odd == 0, full_two, full_one), short)
    tables = (FIRST_TO, SECOND_TO, FIRST_TO)

    def arrange(pieces):
        (one, three), two = pieces
        return jnp.stack(
            [
                jnp.where(slots[0] == i, one, jnp.where(slots[1] == i, two, three))
                for i in range(3)
            ]
        )

    where = jnp.stack(
        [place.core, place.chip * 4 + place.z, 2 * place.core + odd]
    ).astype(jnp.int32)

    def leaving(array):
        pieces = [lax.dynamic_index_in_dim(array, slot, 0, keepdims=False) for slot in slots]
        return jnp.stack([pieces[0], pieces[2]]), pieces[1]

    def move(pieces):
        return tuple(
            lax.ppermute(piece, ("dp", "blk"), column_pairs(table))
            for piece, table in zip(pieces, (FIRST_TO, SECOND_TO))
        )

    def give(pieces):
        return tuple(
            None
            if piece is None
            else lax.ppermute(piece, ("dp", "blk"), [pair[::-1] for pair in column_pairs(table)])
            for piece, table in zip(pieces, (FIRST_TO, SECOND_TO))
        )

    wide = w_fc1.shape[1] // 768
    rows = tokens.shape[1]
    vectors = [ln1_gain, ln1_shift, bias_q, bias_v, bias_out, ln2_gain, ln2_shift, bias_fc2]
    vecs, b1 = prepare(jnp.stack(vectors), bias_fc1.reshape(1, -1))
    vecs_one, vecs_two = vecs[:4], vecs[4:]
    token_sends = leaving(tokens)
    x13, x2 = move(token_sends)
    xs = (x13, x2)
    cot_sends = leaving(after(cotangent, *token_sends))
    x3 = after(x13[1], x2, vecs, *cot_sends)
    short_blocks = exchange_short(x3)
    q_full, kv_full = project(x13, after(x2, x3), vecs_one, w_qkv)
    kv_other = swap(kv_full, "dp", 1)
    cots = move(after(cot_sends, x3))
    seq = 2 * kv_full.shape[1]
    kv_both = [kv_full, kv_other]
    att_full, t_full = attend(q_full, kv_both, seq, 768, 384)
    spare = -(-(SHORT - 2 * rows) // LANES) * LANES
    q_short, kv_head, kv_tail = project_short(
        where, x13, *after(short_blocks, att_full), vecs_one, w_qkv, spare
    )
    kv_short = [kv_head, kv_tail]
    att_short, t_short = attend(q_short, kv_short, SHORT, 384, 384)
    cots = after(cots, att_short)
    o13, o2, mid, normed_two, hidden_low, send_a, keep_a, gb1 = feed(
        where, att_full, att_short, xs, cots, w_out, vecs_two, w_fc1, b1, w_fc2
    )
    got_a = swap(send_a, "dp", 1)
    home_one = give((o13, o2))
    sums_a = by_chip(keep_a, got_a)
    chips_a = over_chips(sums_a)
    back_att, back_mid, send_b, keep_b, feed_sums = feed_back(
        where, att_full, att_short, cots, w_out, vecs_two, after(mid, *sums_a), normed_two,
        hidden_low, w_fc1,
    )
    home = (after(home_one[0], back_mid), home_one[1])
    quarter_a = add_low(after(sums_a[0], back_mid, home[0]), *chips_a)
    line_a = over_line(quarter_a)
    got_b = swap(after(send_b, quarter_a), "dp", 1)

    n_full = q_full.shape[0]
    dq_short, keep_short, send_pair = attend_back(
        where, after(q_short, quarter_a), back_att, n_full, att_short, t_short, kv_short, SHORT,
        448, 0, 6, True,
    )
    home = (home[0], after(home[1], dq_short))
    part_a = add_low(after(quarter_a[0], dq_short, home[1]), *line_a)
    all_a = gather_all(part_a)
    got_pair = swap(after(send_pair, part_a), "dp", 1)
    sums_b = by_chip(after(keep_b, dq_short, part_a), got_b)
    chips_b = over_chips(sums_b)
    away = (1 - odd) * rows
    send_short = add_low(
        lax.dynamic_slice_in_dim(keep_short, away, rows, 1),
        lax.dynamic_slice_in_dim(after(got_pair, *sums_b), away, rows, 1),
    )
    got_near = swap(send_short, "blk", 1)
    dq_full, own_full, sent_full = attend_back(
        where, after(q_full, send_short), back_att, 0, att_full, t_full, kv_both, seq, 768, 0, 6
    )
    got_near = after(got_near, dq_full)
    quarter_b = add_low(after(sums_b[0], dq_full, got_near), *chips_b)
    got_full = swap(after(sent_full, quarter_b), "dp", 1)
    line_b = over_line(quarter_b)
    send_c, keep_c, back = project_back(
        where, xs, vecs_one, dq_full, dq_short, own_full, got_full, keep_short, got_pair, got_near
    )
    part_b = add_low(after(quarter_b[0], keep_c), *line_b)
    got_c = swap(after(send_c, part_b), "dp", 1)
    near_b = over_line([part_b] * 4)
    i13, i2, line_sums = input_back(
        where, xs, vecs_one, w_qkv, back_mid, after(back, part_b), feed_sums, gb1
    )
    near_b = jnp.stack([after(part_b, i2)] + near_b)
    half_b = lax.all_gather(near_b, "dp", axis=0, axis_index_groups=CHIPS)
    sums_c = [
        jnp.concatenate([total, line_sums[4 * k : 4 * k + 4]], axis=1)
        for k, total in enumerate(by_chip(after(keep_c, i2, near_b), got_c))
    ]
    chips_c = over_chips(sums_c)
    (i13_home,) = give((after(i13, *sums_c), None))[:1]
    output = arrange(after(home, *sums_c))
    all_a = after(all_a, *sums_c)
    halves_a = [all_a[:, c] for c in range(2)]
    grad_w_fc2 = finish(jnp.zeros((3,), jnp.int32), *halves_a, 0, wide, False)
    i13_home = after(i13_home, grad_w_fc2, output)
    quarter_c = add_low(after(sums_c[0], i13_home), *chips_c)
    line_c = over_line(quarter_c)
    part_c = add_low(quarter_c[0], *line_c)
    near_c = jnp.stack([part_c] + over_line([part_c] * 4))
    far_c = over_chips([near_c] * 4)
    i2_home = give((None, after(i2, near_c)))[1]
    half_b = after(half_b, near_c)
    other_b = swap(half_b, "dp", 1)
    inside = where * jnp.array([1, 0, 0], jnp.int32) + jnp.array([0, 1, 0], jnp.int32) * place.z
    grad_w_fc1 = finish(inside, half_b, other_b, 0, wide, True)
    grad_w_out = finish(inside, half_b, other_b, wide, 1, True)
    i2_home = after(i2_home, grad_w_fc1, grad_w_out)
    whole_c = jnp.stack([after(near_c, i2_home)] + far_c)
    other_c = swap(whole_c, "dp", 1)
    input_grad = arrange(after((i13_home, i2_home), whole_c)).astype(F32)
    grad_w_qkv, *lines = finish(where, whole_c, other_c, 0, 3, True, True)
    return (
        output,
        input_grad,
        lines[4],
        lines[5],
        grad_w_qkv,
        lines[6],
        lines[7],
        grad_w_out,
        lines[0],
        lines[1],
        lines[2],
        grad_w_fc1,
        lines[8],
        grad_w_fc2,
        lines[3],
    )


def solution(mesh):
    paired = mesh.shape["dp"] == 8 and mesh.shape["blk"] == 4
    chosen = local_paired if paired else local
    return jax.shard_map(
        chosen,
        mesh=mesh,
        in_specs=(
            P("dp", "blk", None),
            P("dp"),
            P(),
            P(),
            P(),
            P(),
            P(),
            P(),
            P(),
            P(),
            P(),
            P(),
            P(),
            P(),
            P(),
            P("dp", "blk", None),
        ),
        out_specs=(
            P("dp", "blk", None),
            P("dp", "blk", None),
            P(),
            P(),
            P(),
            P(),
            P(),
            P(),
            P(),
            P(),
            P(),
            P(),
            P(),
            P(),
            P(),
        ),
        check_vma=False,
    )
```

```python
import functools
import math

import jax
import jax.numpy as jnp
from jax import lax
from jax.experimental import pallas as pl
from jax.experimental.pallas import tpu as pltpu
from jax.sharding import PartitionSpec as P

HEADS = 12
HD = 64
SHORT = 864


NORM_EPS = 1e-06
MASK_LOW = -1e30


def norm_rows(values, gain, shift):
    centre = values - jnp.mean(values, axis=-1, keepdims=True)
    spread = jnp.mean(centre * centre, axis=-1, keepdims=True)
    return centre * lax.rsqrt(spread + NORM_EPS) * gain + shift


def gelu_exact(values):
    return jax.nn.gelu(values, approximate=False)


def cube_valid(counts, offset, length):
    places = offset + jnp.arange(length, dtype=jnp.int32)
    return places[None, :] < counts[:, None]


def total_every(parts):
    split = (
        lax.psum_scatter(
            parts[0].astype(jnp.bfloat16), "blk", scatter_dimension=0, tiled=True
        ).astype(jnp.float32),
        lax.psum_scatter(
            parts[1].astype(jnp.bfloat16), "blk", scatter_dimension=0, tiled=True
        ).astype(jnp.float32),
        lax.psum_scatter(
            parts[2].astype(jnp.bfloat16), "blk", scatter_dimension=0, tiled=True
        ).astype(jnp.float32),
        lax.psum_scatter(
            parts[3].astype(jnp.bfloat16), "blk", scatter_dimension=0, tiled=True
        ).astype(jnp.float32),
        lax.psum_scatter(
            parts[4].astype(jnp.bfloat16), "blk", scatter_dimension=0, tiled=True
        ).astype(jnp.float32),
        lax.psum_scatter(
            parts[5].astype(jnp.bfloat16), "blk", scatter_dimension=0, tiled=True
        ).astype(jnp.float32),
        lax.psum_scatter(
            parts[6].astype(jnp.bfloat16), "blk", scatter_dimension=0, tiled=True
        ).astype(jnp.float32),
        lax.psum_scatter(
            parts[7].astype(jnp.bfloat16), "blk", scatter_dimension=0, tiled=True
        ).astype(jnp.float32),
        lax.psum_scatter(
            parts[8].astype(jnp.bfloat16), "blk", scatter_dimension=0, tiled=True
        ).astype(jnp.float32),
        lax.psum_scatter(
            parts[9].astype(jnp.bfloat16), "blk", scatter_dimension=0, tiled=True
        ).astype(jnp.float32),
        lax.psum_scatter(
            parts[10].astype(jnp.bfloat16), "blk", scatter_dimension=0, tiled=True
        ).astype(jnp.float32),
        lax.psum_scatter(
            parts[11].astype(jnp.bfloat16), "blk", scatter_dimension=0, tiled=True
        ).astype(jnp.float32),
        lax.psum_scatter(
            parts[12].astype(jnp.bfloat16), "blk", scatter_dimension=0, tiled=True
        ).astype(jnp.float32),
    )
    summed = (
        lax.psum(split[0].astype(jnp.bfloat16), "dp").astype(jnp.float32),
        lax.psum(split[1].astype(jnp.bfloat16), "dp").astype(jnp.float32),
        lax.psum(split[2].astype(jnp.bfloat16), "dp").astype(jnp.float32),
        lax.psum(split[3].astype(jnp.bfloat16), "dp").astype(jnp.float32),
        lax.psum(split[4].astype(jnp.bfloat16), "dp").astype(jnp.float32),
        lax.psum(split[5].astype(jnp.bfloat16), "dp").astype(jnp.float32),
        lax.psum(split[6].astype(jnp.bfloat16), "dp").astype(jnp.float32),
        lax.psum(split[7].astype(jnp.bfloat16), "dp").astype(jnp.float32),
        lax.psum(split[8].astype(jnp.bfloat16), "dp").astype(jnp.float32),
        lax.psum(split[9].astype(jnp.bfloat16), "dp").astype(jnp.float32),
        lax.psum(split[10].astype(jnp.bfloat16), "dp").astype(jnp.float32),
        lax.psum(split[11].astype(jnp.bfloat16), "dp").astype(jnp.float32),
        lax.psum(split[12].astype(jnp.bfloat16), "dp").astype(jnp.float32),
    )
    return (
        lax.all_gather(summed[0].astype(jnp.bfloat16), "blk", axis=0, tiled=True).astype(
            jnp.float32
        ),
        lax.all_gather(summed[1].astype(jnp.bfloat16), "blk", axis=0, tiled=True).astype(
            jnp.float32
        ),
        lax.all_gather(summed[2].astype(jnp.bfloat16), "blk", axis=0, tiled=True).astype(
            jnp.float32
        ),
        lax.all_gather(summed[3].astype(jnp.bfloat16), "blk", axis=0, tiled=True).astype(
            jnp.float32
        ),
        lax.all_gather(summed[4].astype(jnp.bfloat16), "blk", axis=0, tiled=True).astype(
            jnp.float32
        ),
        lax.all_gather(summed[5].astype(jnp.bfloat16), "blk", axis=0, tiled=True).astype(
            jnp.float32
        ),
        lax.all_gather(summed[6].astype(jnp.bfloat16), "blk", axis=0, tiled=True).astype(
            jnp.float32
        ),
        lax.all_gather(summed[7].astype(jnp.bfloat16), "blk", axis=0, tiled=True).astype(
            jnp.float32
        ),
        lax.all_gather(summed[8].astype(jnp.bfloat16), "blk", axis=0, tiled=True).astype(
            jnp.float32
        ),
        lax.all_gather(summed[9].astype(jnp.bfloat16), "blk", axis=0, tiled=True).astype(
            jnp.float32
        ),
        lax.all_gather(summed[10].astype(jnp.bfloat16), "blk", axis=0, tiled=True).astype(
            jnp.float32
        ),
        lax.all_gather(summed[11].astype(jnp.bfloat16), "blk", axis=0, tiled=True).astype(
            jnp.float32
        ),
        lax.all_gather(summed[12].astype(jnp.bfloat16), "blk", axis=0, tiled=True).astype(
            jnp.float32
        ),
    )


def local(
    tokens,
    counts,
    ln1_gain,
    ln1_shift,
    w_qkv,
    bias_q,
    bias_v,
    w_out,
    bias_out,
    ln2_gain,
    ln2_shift,
    w_fc1,
    bias_fc1,
    w_fc2,
    bias_fc2,
    cotangent,
):
    cube_count, row_count, width = tokens.shape
    head_count = HEADS
    depth = HD
    score_scale = HD ** (-0.5)
    inputs = tokens.astype(jnp.float32)
    gain_one = ln1_gain.astype(jnp.float32)
    shift_one = ln1_shift.astype(jnp.float32)
    gain_two = ln2_gain.astype(jnp.float32)
    shift_two = ln2_shift.astype(jnp.float32)
    normed = norm_rows(inputs, gain_one, shift_one).astype(jnp.bfloat16)
    project = jnp.dot(normed, w_qkv, preferred_element_type=jnp.float32)
    queries = (project[..., :width] + bias_q.astype(jnp.float32)).astype(jnp.bfloat16)
    key_local = project[..., width : 2 * width].astype(jnp.bfloat16)
    value_local = (project[..., 2 * width :] + bias_v.astype(jnp.float32)).astype(jnp.bfloat16)
    key_all, value_all = (
        lax.all_gather(key_local, "blk", axis=1, tiled=True),
        lax.all_gather(value_local, "blk", axis=1, tiled=True),
    )
    seq_rows = key_all.shape[1]
    block_rows = math.gcd(seq_rows, 512)
    block_count = seq_rows // block_rows
    block_steps = jnp.arange(block_count, dtype=jnp.int32)
    query_heads = queries.reshape(cube_count, row_count, head_count, depth)

    def key_slices(offset):
        key_part = lax.dynamic_slice_in_dim(key_all, offset, block_rows, 1).reshape(
            cube_count, block_rows, head_count, depth
        )
        value_part = lax.dynamic_slice_in_dim(value_all, offset, block_rows, 1).reshape(
            cube_count, block_rows, head_count, depth
        )
        usable = cube_valid(counts, offset, block_rows)[:, None, None, :]
        return (key_part, value_part, usable)

    def forward_block(carry, step_index):
        row_top, row_total, accum = carry
        key_part, value_part, usable = key_slices(step_index * block_rows)
        scores = (
            jnp.einsum("cqhd,ckhd->chqk", query_heads, key_part, preferred_element_type=jnp.float32)
            * score_scale
        )
        masked = jnp.where(usable, scores, MASK_LOW)
        new_top = jnp.maximum(row_top, jnp.max(masked, axis=-1))
        factor = jnp.exp(row_top - new_top)
        weights = jnp.where(usable, jnp.exp(masked - new_top[..., None]), 0.0)
        row_total = row_total * factor + jnp.sum(weights, axis=-1)
        accum = accum * jnp.transpose(factor, (0, 2, 1))[..., None] + jnp.einsum(
            "chqk,ckhd->cqhd",
            weights.astype(jnp.bfloat16),
            value_part,
            preferred_element_type=jnp.float32,
        )
        return ((new_top, row_total, accum), None)

    start_carry = (
        jnp.full((cube_count, head_count, row_count), MASK_LOW, jnp.float32),
        jnp.zeros((cube_count, head_count, row_count), jnp.float32),
        jnp.zeros((cube_count, row_count, head_count, depth), jnp.float32),
    )
    (row_top, row_total, accum), _ = lax.scan(forward_block, start_carry, block_steps)
    attended_f = (accum / jnp.transpose(row_total, (0, 2, 1))[..., None]).reshape(
        cube_count, row_count, width
    )
    log_total = row_top + jnp.log(row_total)
    attended = attended_f.astype(jnp.bfloat16)
    middle = (
        inputs
        + jnp.dot(attended, w_out, preferred_element_type=jnp.float32)
        + bias_out.astype(jnp.float32)
    )
    normed_two = norm_rows(middle, gain_two, shift_two).astype(jnp.bfloat16)
    hidden = jnp.dot(normed_two, w_fc1, preferred_element_type=jnp.float32) + bias_fc1.astype(
        jnp.float32
    )
    active = gelu_exact(hidden).astype(jnp.bfloat16)
    output = (
        middle
        + jnp.dot(active, w_fc2, preferred_element_type=jnp.float32)
        + bias_fc2.astype(jnp.float32)
    ).astype(jnp.bfloat16)
    grad_bias_fc2 = jnp.sum(cotangent.astype(jnp.float32), axis=(0, 1))
    grad_w_fc2 = jnp.einsum("ctf,ctd->fd", active, cotangent, preferred_element_type=jnp.float32)
    back_active = jnp.einsum("ctd,fd->ctf", cotangent, w_fc2, preferred_element_type=jnp.float32)
    _, gelu_pull = jax.vjp(gelu_exact, hidden)
    back_hidden = gelu_pull(back_active)[0]
    grad_bias_fc1 = jnp.sum(back_hidden, axis=(0, 1))
    hidden_low = back_hidden.astype(jnp.bfloat16)
    grad_w_fc1 = jnp.einsum(
        "ctd,ctf->df", normed_two, hidden_low, preferred_element_type=jnp.float32
    )
    back_normed_two = jnp.einsum(
        "ctf,df->ctd", hidden_low, w_fc1, preferred_element_type=jnp.float32
    )
    _, norm_pull_two = jax.vjp(norm_rows, middle, gain_two, shift_two)
    back_middle_norm, grad_ln2_gain, grad_ln2_shift = norm_pull_two(back_normed_two)
    back_middle = cotangent.astype(jnp.float32) + back_middle_norm
    mlp_grads = (
        grad_ln2_gain,
        grad_ln2_shift,
        grad_w_fc1,
        grad_bias_fc1,
        grad_w_fc2,
        grad_bias_fc2,
    )
    grad_bias_out = jnp.sum(back_middle, axis=(0, 1))
    middle_low = back_middle.astype(jnp.bfloat16)
    grad_w_out = jnp.einsum("ctd,cte->de", attended, middle_low, preferred_element_type=jnp.float32)
    back_attended = jnp.einsum(
        "cte,de->ctd", middle_low, w_out, preferred_element_type=jnp.float32
    ).astype(jnp.bfloat16)
    back_heads = back_attended.reshape(cube_count, row_count, head_count, depth)
    delta = jnp.transpose(
        jnp.sum(
            (back_attended.astype(jnp.float32) * attended_f).reshape(
                cube_count, row_count, head_count, depth
            ),
            axis=-1,
        ),
        (0, 2, 1),
    )

    def block_grads(key_part, value_part, usable):
        scores = (
            jnp.einsum("cqhd,ckhd->chqk", query_heads, key_part, preferred_element_type=jnp.float32)
            * score_scale
        )
        probs = jnp.where(usable, jnp.exp(scores - log_total[..., None]), 0.0)
        back_probs = jnp.einsum(
            "cqhd,ckhd->chqk", back_heads, value_part, preferred_element_type=jnp.float32
        )
        back_scores = (probs * (back_probs - delta[..., None])).astype(jnp.bfloat16)
        return (probs, back_scores)

    query_zero = jnp.zeros((cube_count, row_count, head_count, depth), jnp.float32)

    def back_block(carry, step_index):
        back_query, key_grads, value_grads = carry
        offset = step_index * block_rows
        key_part, value_part, usable = key_slices(offset)
        probs, back_scores = block_grads(key_part, value_part, usable)
        back_query = (
            back_query
            + jnp.einsum(
                "chqk,ckhd->cqhd", back_scores, key_part, preferred_element_type=jnp.float32
            )
            * score_scale
        )
        key_block = (
            jnp.einsum(
                "chqk,cqhd->ckhd", back_scores, query_heads, preferred_element_type=jnp.float32
            )
            * score_scale
        )
        value_block = jnp.einsum(
            "chqk,cqhd->ckhd",
            probs.astype(jnp.bfloat16),
            back_heads,
            preferred_element_type=jnp.float32,
        )
        key_grads = lax.dynamic_update_slice_in_dim(
            key_grads, key_block.reshape(cube_count, block_rows, width), offset, 1
        )
        value_grads = lax.dynamic_update_slice_in_dim(
            value_grads, value_block.reshape(cube_count, block_rows, width), offset, 1
        )
        return ((back_query, key_grads, value_grads), None)

    full_zero = jnp.zeros((cube_count, seq_rows, width), jnp.float32)
    (back_query, key_grads, value_grads), _ = lax.scan(
        back_block, (query_zero, full_zero, full_zero), block_steps
    )
    key_back, value_back = (
        lax.psum_scatter(
            key_grads.astype(jnp.bfloat16), "blk", scatter_dimension=1, tiled=True
        ).astype(jnp.float32),
        lax.psum_scatter(
            value_grads.astype(jnp.bfloat16), "blk", scatter_dimension=1, tiled=True
        ).astype(jnp.float32),
    )
    query_low = back_query.reshape(cube_count, row_count, width).astype(jnp.bfloat16)
    key_low = key_back.astype(jnp.bfloat16)
    value_low = value_back.astype(jnp.bfloat16)
    grad_bias_q = jnp.sum(query_low.astype(jnp.float32), axis=(0, 1))
    grad_bias_v = jnp.sum(value_low.astype(jnp.float32), axis=(0, 1))
    back_project = jnp.concatenate([query_low, key_low, value_low], axis=-1)
    grad_w_qkv = jnp.einsum("ctd,cte->de", normed, back_project, preferred_element_type=jnp.float32)
    back_normed = jnp.einsum("cte,de->ctd", back_project, w_qkv, preferred_element_type=jnp.float32)
    _, norm_pull_one = jax.vjp(norm_rows, inputs, gain_one, shift_one)
    back_inputs, grad_ln1_gain, grad_ln1_shift = norm_pull_one(back_normed)
    input_grad = back_middle + back_inputs
    attn_grads = (
        grad_ln1_gain,
        grad_ln1_shift,
        grad_w_qkv,
        grad_bias_q,
        grad_bias_v,
        grad_w_out,
        grad_bias_out,
    )
    every_grad = total_every(attn_grads + mlp_grads)
    attn_grads = every_grad[:7]
    mlp_grads = every_grad[7:]
    return (
        output,
        input_grad,
        attn_grads[0],
        attn_grads[1],
        attn_grads[2],
        attn_grads[3],
        attn_grads[4],
        attn_grads[5],
        attn_grads[6],
        mlp_grads[0],
        mlp_grads[1],
        mlp_grads[2],
        mlp_grads[3],
        mlp_grads[4],
        mlp_grads[5],
    )


F32 = jnp.float32
BF16 = jnp.bfloat16
EXP_SCALE = math.log2(math.e) / 8
LANES = 128
CUT = 256
VMEM = pl.BlockSpec(memory_space=pltpu.VMEM)
SMEM = pl.BlockSpec(memory_space=pltpu.SMEM)
ANY = pl.BlockSpec(memory_space=pl.ANY)


def lasting(micros):
    return pl.CostEstimate(flops=micros * 10**9, bytes_accessed=2**20, transcendentals=0)


def shape_of(shape, dtype):
    return jax.ShapeDtypeStruct(shape, dtype)


def limits(mib):
    return pltpu.CompilerParams(vmem_limit_bytes=mib * 2**20)


def dot_nt(a, b):
    return lax.dot_general(a, b, (((1,), (1,)), ((), ())), preferred_element_type=F32)


def dot_nn(a, b):
    return lax.dot_general(a, b, (((1,), (0,)), ((), ())), preferred_element_type=F32)


def dot_tn(a, b):
    return lax.dot_general(a, b, (((0,), (0,)), ((), ())), preferred_element_type=F32)


def centred(values):
    centre = values - jnp.mean(values, axis=1, keepdims=True)
    spread = jnp.mean(centre * centre, axis=1, keepdims=True)
    return centre, lax.rsqrt(spread + NORM_EPS)


def norm_back(centre, recip, back, gain):
    unit = centre * recip
    grad = back * gain
    inner = jnp.mean(grad * unit, axis=1, keepdims=True)
    return unit, recip * (grad - jnp.mean(grad, axis=1, keepdims=True) - unit * inner)


def prepare_kernel(a, b, w, out_a, out_b, out_w):
    out_a[...] = a[...].astype(F32)
    out_b[...] = b[...].astype(F32)
    out_w[...] = w[...]


def prepare(a, b, w):
    return pl.pallas_call(
        prepare_kernel,
        in_specs=[VMEM] * 3,
        out_specs=[VMEM] * 3,
        out_shape=[shape_of(a.shape, F32), shape_of(b.shape, F32), shape_of(w.shape, w.dtype)],
        compiler_params=limits(16),
        cost_estimate=lasting(2),
        name="prepare",
    )(a, b, w)


def project_rows(x, vecs, w, q_ref, kv_ref, at, q_at=None):
    gain, shift, bias_q, bias_v = (vecs[i : i + 1, :] for i in range(4))
    centre, recip = centred(x.astype(F32))
    normed = (centre * recip * gain + shift).astype(BF16)
    kv_ref[0, at, :] = dot_nn(normed, w[:, 768:1536]).astype(BF16)
    kv_ref[1, at, :] = (dot_nn(normed, w[:, 1536:]) + bias_v).astype(BF16)
    if q_at is not None:
        q_ref[q_at, :] = (dot_nn(normed, w[:, :768]) + bias_q).astype(BF16)


def project_kernel(x13_in, x2_in, vecs, w_in, q_ref, kv_ref, held, w, sems):
    copies = start_copies([x13_in.at[0], x2_in, w_in], [held.at[0], held.at[1], w], sems)
    for copy in copies:
        copy.wait()
    rows = held.shape[1]
    for i in range(2):
        at = pl.ds(i * rows, rows)
        project_rows(held[i], vecs, w, q_ref, kv_ref, at, at)


def project(x13, x2, vecs, w):
    n = 2 * x2.shape[0]
    return pl.pallas_call(
        project_kernel,
        in_specs=[ANY, ANY, VMEM, ANY],
        out_specs=[VMEM] * 2,
        out_shape=[shape_of((n, 768), BF16), shape_of((2, n, 768), BF16)],
        scratch_shapes=[
            pltpu.VMEM((2,) + x2.shape, BF16),
            pltpu.VMEM(w.shape, w.dtype),
            pltpu.SemaphoreType.DMA((3,)),
        ],
        compiler_params=limits(24),
        cost_estimate=lasting(4),
        name="project",
    )(x13, x2, vecs, w)


def project_short_kernel(
    where, x13, near, other, far, vecs, w_in, q_ref, head_ref, tail_ref, w, held, sems, *, spare
):
    (copy,) = start_copies([w_in], [w], sems)
    rows = near.shape[0]
    mine = where[2]
    for k, block in enumerate((x13[1], near[...], other[...], far[...])):
        held[k ^ mine] = block
    copy.wait()
    for i in range(2):
        project_rows(held[i], vecs, w, None, head_ref, pl.ds(i * rows, rows))
    project_rows(held[2][:spare], vecs, w, None, tail_ref, pl.ds(0, spare))
    centre, recip = centred(x13[1].astype(F32))
    normed = (centre * recip * vecs[0:1, :] + vecs[1:2, :]).astype(BF16)
    q_ref[...] = (dot_nn(normed, w[:, :768]) + vecs[2:3, :]).astype(BF16)


def project_short(where, x13, near, other, far, vecs, w, spare):
    rows = near.shape[0]
    return pl.pallas_call(
        functools.partial(project_short_kernel, spare=spare),
        in_specs=[SMEM] + [VMEM] * 5 + [ANY],
        out_specs=[VMEM] * 3,
        out_shape=[
            shape_of((rows, 768), BF16),
            shape_of((2, 2 * rows, 768), BF16),
            shape_of((2, spare, 768), BF16),
        ],
        scratch_shapes=[
            pltpu.VMEM(w.shape, w.dtype),
            pltpu.VMEM((4, rows, 768), BF16),
            pltpu.SemaphoreType.DMA((1,)),
        ],
        compiler_params=limits(24),
        cost_estimate=lasting(4),
        name="project_short",
    )(where, x13, near, other, far, vecs, w)


def start_copies(sources, targets, sems):
    copies = [
        pltpu.make_async_copy(source, target, sems.at[i])
        for i, (source, target) in enumerate(zip(sources, targets))
    ]
    for copy in copies:
        copy.start()
    return copies


def three_parts(values, lane):
    high = values.astype(BF16)
    rest = values - high.astype(F32)
    middle = rest.astype(BF16)
    least = (rest - middle.astype(F32)).astype(BF16)
    zero = jnp.zeros((), BF16)
    return jnp.where(
        lane == 0, high, jnp.where(lane == 1, middle, jnp.where(lane == 2, least, zero))
    )


def lane_index(rows=1):
    return lax.broadcasted_iota(jnp.int32, (rows, LANES), 1)


def attend_kernel(*refs, pieces, valid, step):
    q_ref = refs[0]
    kvs = refs[1 : 1 + pieces]
    o_ref, t_ref = refs[1 + pieces :]
    lane = lane_index()
    low = lane < 64
    half = lane % 64
    total = sum(kv.shape[1] for kv in kvs)
    keys, values = [], []
    for h in range(2):
        own = low if h == 0 else ~low
        key_parts, value_parts, at = [], [], 0
        for kv in kvs:
            n = kv.shape[1]
            beside = jnp.zeros((n, LANES), BF16)
            if at + n > valid:
                place = lax.broadcasted_iota(jnp.int32, (n, LANES), 0) + at
                beside = jnp.where(
                    (place >= valid) & (lane_index(n) % 64 == 0), MASK_LOW, 0.0
                ).astype(BF16)
            key_parts.append(jnp.where(own, kv[0], beside))
            value_parts.append(jnp.where(own, kv[1], jnp.ones((), BF16)))
            at += n
        keys.append(key_parts)
        values.append(value_parts)
    cuts = [
        (i, first, min(CUT, kv.shape[1] - first))
        for i, kv in enumerate(kvs)
        for first in range(0, kv.shape[1], CUT)
    ]
    for s in range(q_ref.shape[0] // step):
        at = pl.ds(s * step, step)
        q = q_ref[at, :]
        sums, tops = [], []
        for h in range(2):
            own = low if h == 0 else ~low
            q_own = q
            if total > valid:
                q_own = jnp.where(own, q, jnp.where(half == 0, 1.0, 0.0).astype(BF16))
            top, kept = None, None
            for i, first, size in cuts:
                scores = dot_nt(q_own, keys[h][i][first : first + size]) * EXP_SCALE
                new_top = jnp.max(scores, axis=1, keepdims=True)
                if top is not None:
                    new_top = jnp.maximum(top, new_top)
                weights = jnp.exp2(scores - new_top).astype(BF16)
                part = dot_nn(weights, values[h][i][first : first + size])
                kept = part if top is None else kept * jnp.exp2(top - new_top) + part
                top = new_top
            sums.append(kept)
            tops.append(top)
        above = jnp.where(low, sums[0], sums[1])
        below = jnp.where(low, sums[1], sums[0])
        o_ref[at, :] = above / pltpu.roll(below, 64, 1)
        top = jnp.where(low, tops[1], tops[0]) * (1.0 / EXP_SCALE)
        t_ref[at, :] = jnp.where(
            half == 3, jnp.ones((), BF16), three_parts(-(top + 8.0 * jnp.log(below)), half)
        )


def attend(q, kvs, valid, rows, step, first=0, count=6):
    n = q.shape[0]
    keys = sum(kv.shape[1] for kv in kvs)
    block = pl.BlockSpec((rows, LANES), lambda p, i: (i, p))
    return pl.pallas_call(
        functools.partial(attend_kernel, pieces=len(kvs), valid=valid, step=step),
        out_shape=[shape_of((n, LANES * count), F32), shape_of((n, LANES * count), BF16)],
        grid=(count, n // rows),
        in_specs=[pl.BlockSpec((rows, LANES), lambda p, i: (i, first + p))]
        + [pl.BlockSpec((2, kv.shape[1], LANES), lambda p, i: (0, 0, first + p)) for kv in kvs],
        out_specs=[block, block],
        compiler_params=limits(24),
        cost_estimate=lasting(n * keys * count // 280000),
        name="attend",
    )(q, *kvs)


def attend_back_kernel(*refs, pieces, valid, step, split):
    where = refs[0]
    q_ref, do_ref, o_ref, t_ref = refs[1:5]
    kvs = refs[5 : 5 + pieces]
    dq_ref = refs[5 + pieces]
    outs = refs[6 + pieces :]
    n = q_ref.shape[0]
    lane = lane_index()
    low = lane < 64
    half = lane % 64
    q, do, t = q_ref[...], do_ref[...], t_ref[...]
    product = do.astype(F32) * o_ref[...]
    delta = [
        jnp.sum(jnp.where(low, product, 0.0), axis=1, keepdims=True),
        jnp.sum(jnp.where(low, 0.0, product), axis=1, keepdims=True),
    ]
    d = three_parts(-jnp.where(low, delta[1], delta[0]), half)
    queries = [jnp.where(low, q, t), jnp.where(low, t, q)]
    backs = [jnp.where(low, do, d), jnp.where(low, d, do)]
    ones = jnp.where(half < 3, 1.0, 0.0).astype(BF16)
    sums = [jnp.zeros((LANES, n), F32), jnp.zeros((LANES, n), F32)]
    starts = [sum(kv.shape[1] for kv in kvs[:i]) for i in range(pieces)]
    small = None
    for i in reversed(range(pieces)):
        kv = kvs[i]
        for first in range(0, kv.shape[1], step):
            size = min(step, kv.shape[1] - first)
            at = pl.ds(first, size)
            key_sums, value_sums = [], []
            for h in range(2):
                own = low if h == 0 else ~low
                beside = ones
                if starts[i] + first + size > valid:
                    place = lax.broadcasted_iota(jnp.int32, (size, LANES), 0) + (starts[i] + first)
                    wide = lane_index(size) % 64
                    beside = jnp.where(
                        wide < 3, 1.0, jnp.where((place >= valid) & (wide == 3), MASK_LOW, 0.0)
                    ).astype(BF16)
                key = jnp.where(own, kv[0, at, :], beside)
                value = jnp.where(own, kv[1, at, :], ones)
                probs = jnp.exp2(dot_nt(key, queries[h]) * EXP_SCALE)
                back_scores = (probs * dot_nt(value, backs[h])).astype(BF16)
                value_sums.append(dot_nn(probs.astype(BF16), backs[h]))
                key_sums.append(dot_nn(back_scores, queries[h]))
                sums[h] = sums[h] + dot_tn(key, back_scores)
            both = (
                (jnp.where(low, key_sums[0], key_sums[1]) * 0.125).astype(BF16),
                jnp.where(low, value_sums[0], value_sums[1]).astype(BF16),
            )
            for k in range(2):
                if not split:
                    outs[i][k, at, :] = both[k]
                elif i == 0:
                    other = jnp.zeros_like(both[k])
                    if first == 0:
                        rest = jnp.zeros((size - small[k].shape[0], LANES), BF16)
                        other = jnp.concatenate([small[k], rest], axis=0)
                    stays = where[0] == 0
                    outs[0][k, at, :] = jnp.where(stays, both[k], other)
                    outs[1][k, at, :] = jnp.where(stays, other, both[k])
            small = both
    both = jnp.concatenate([sums[0][:64], sums[1][64:]], axis=0)
    dq_ref[...] = (both.T * 0.125).astype(BF16)


def attend_back(where, q, do, first_row, o, t, kvs, valid, step, first, count, split=False):
    n = q.shape[0]
    keys = sum(kv.shape[1] for kv in kvs)
    row = first_row // n
    block = pl.BlockSpec((n, LANES), lambda p: (0, first + p))
    back_block = pl.BlockSpec((n, LANES), lambda p: (row, first + p))
    wide = [pl.BlockSpec((2, kv.shape[1], LANES), lambda p: (0, 0, first + p)) for kv in kvs]
    out = pl.BlockSpec((n, LANES), lambda p: (0, p))
    outs = [kvs[0], kvs[0]] if split else kvs
    out_wide = [pl.BlockSpec((2, kv.shape[1], LANES), lambda p: (0, 0, p)) for kv in outs]
    return pl.pallas_call(
        functools.partial(
            attend_back_kernel, pieces=len(kvs), valid=valid, step=step, split=split
        ),
        out_shape=[shape_of((n, LANES * count), BF16)]
        + [shape_of((2, kv.shape[1], LANES * count), BF16) for kv in outs],
        grid=(count,),
        in_specs=[SMEM, block, back_block, block, block] + wide,
        out_specs=[out] + out_wide,
        compiler_params=limits(28),
        cost_estimate=lasting(n * keys * count // 180000),
        name="attend_back",
    )(where, q, do, o, t, *kvs)


def fill_part(where, send, keep, j, block):
    left, right = block[:, :384], block[:, 384:]
    first = where[0] == 0
    for ref, half in (
        (keep, jnp.where(first, left, right)),
        (send, jnp.where(first, right, left)),
    ):
        for p in range(16):
            ref[p ^ where[1], pl.ds(j * 48, 48), :] = half[p * 48 : (p + 1) * 48]


def attended_rows(att_full, att_short, i, rows):
    if i == 2:
        return att_short[...].astype(BF16)
    at = pl.ds(i * rows, rows)
    return att_full[at, :].astype(BF16)


def feed_kernel(
    where, att_full_in, att_short_in, x13_in, x2_in, c13, c2, w_out_in, vecs, w1, b1, w2,
    o13, o2, mid_out, normed_out, hidden_low, send, keep, gb1,
    att_full, att_short, x13, x2, w_out, mid, normed, out_sum, cot, active, sems,
    *, steps, tile,
):
    j = pl.program_id(0)
    xs, outs = (x13.at[0], x2, x13.at[1]), (o13.at[0], o2, o13.at[1])
    rows = x2.shape[0]
    bias_out, gain, shift, b2 = (vecs[i : i + 1, :] for i in range(4))

    def at(i):
        return pl.ds(i * rows, rows)

    def leaving():
        return [
            pltpu.make_async_copy(mid, mid_out, sems.at[0]),
            pltpu.make_async_copy(normed, normed_out, sems.at[1]),
        ]

    @pl.when(j == 0)
    def _():
        copies = start_copies(
            [w_out_in, att_full_in, x13_in, x2_in, att_short_in, c13.at[0], c2, c13.at[1]],
            [w_out, att_full, x13, x2, att_short] + [cot.at[at(i), :] for i in range(3)],
            sems,
        )
        for copy in copies[:4]:
            copy.wait()
        for i in range(3):
            if i == 2:
                copies[4].wait()
            att = attended_rows(att_full, att_short, i, rows)
            m = xs[i][...].astype(F32) + dot_nn(att, w_out[...]) + bias_out
            mid[at(i), :] = m
            centre, recip = centred(m)
            normed[at(i), :] = (centre * recip * gain + shift).astype(BF16)
            out_sum[at(i), :] = m + b2
        for copy in copies[5:]:
            copy.wait()
        for copy in leaving():
            copy.start()

    w1_tile, w2_tile = w1[...], w2[...]
    bias = b1[...]
    bias_sum = jnp.zeros((1, tile), F32)
    for i in range(3):
        h = dot_nn(normed[at(i), :], w1_tile) + bias
        back_active = dot_nt(cot[at(i), :], w2_tile)
        share = 0.5 + 0.5 * lax.erf(h * math.sqrt(0.5))
        act = (h * share).astype(BF16)
        slope = share + h * (math.sqrt(0.5 / math.pi) * jnp.exp(h * h * (-0.5)))
        back_hidden = back_active * slope
        bias_sum = bias_sum + jnp.sum(back_hidden, axis=0, keepdims=True)
        active[at(i), :] = act
        hidden_low[at(i), :] = back_hidden.astype(BF16)
        out_sum[at(i), :] += dot_nn(act, w2_tile)
    gb1[...] = bias_sum
    grad = dot_tn(active[...], cot[...]).astype(BF16)
    fill_part(where, send, keep, 0, grad)

    @pl.when(j == steps - 1)
    def _():
        for copy in leaving():
            copy.wait()
        for i in range(3):
            outs[i][...] = out_sum[at(i), :].astype(BF16)


def feed(where, att_full, att_short, xs, cots, w_out, vecs, w1, b1, w2):
    rows = xs[1].shape[0]
    n = rows * 3
    wide = w1.shape[1]
    tile = 768
    steps = wide // tile
    across = pl.BlockSpec((768, tile), lambda j: (0, j))
    down = pl.BlockSpec((tile, 768), lambda j: (j, 0))
    line = pl.BlockSpec((1, tile), lambda j: (0, j))
    return pl.pallas_call(
        functools.partial(feed_kernel, steps=steps, tile=tile),
        grid=(steps,),
        in_specs=[SMEM] + [ANY] * 7 + [VMEM, across, line, down],
        out_specs=[VMEM] * 2
        + [ANY] * 2
        + [pl.BlockSpec((n, tile), lambda j: (0, j))]
        + [pl.BlockSpec((16, 48, 384), lambda j: (0, j, 0))] * 2
        + [line],
        out_shape=[shape_of((2, rows, 768), BF16), shape_of((rows, 768), BF16)]
        + [
            shape_of((n, 768), F32),
            shape_of((n, 768), BF16),
            shape_of((n, wide), BF16),
            shape_of((16, 48 * steps, 384), BF16),
            shape_of((16, 48 * steps, 384), BF16),
            shape_of((1, wide), F32),
        ],
        scratch_shapes=[
            pltpu.VMEM(v.shape, v.dtype) for v in (att_full, att_short, *xs, w_out)
        ]
        + [
            pltpu.VMEM((n, 768), F32),
            pltpu.VMEM((n, 768), BF16),
            pltpu.VMEM((n, 768), F32),
            pltpu.VMEM((n, 768), BF16),
            pltpu.VMEM((n, tile), BF16),
            pltpu.SemaphoreType.DMA((8,)),
        ],
        compiler_params=limits(48),
        cost_estimate=lasting(36),
        name="feed",
    )(where, att_full, att_short, *xs, *cots, w_out, vecs, w1, b1, w2)


def feed_back_kernel(
    where, att_full_in, att_short_in, c13_in, c2_in, w_out, vecs, mid_in, normed,
    hidden_low, w1,
    back_att, back_mid, send, keep, sums,
    back_sum, flipped, low_mid, att, att_full, att_short, c13, c2, mid, sems,
    *, steps,
):
    j = pl.program_id(0)
    late = (att_full, att_short, c13, c2, mid)
    sources = (att_full_in, att_short_in, c13_in, c2_in, mid_in)
    cots = (c13.at[0], c2, c13.at[1])
    rows = c2.shape[0]
    gain = vecs[1:2, :]

    def at(i):
        return pl.ds(i * rows, rows)

    @pl.when(j == 0)
    def _():
        start_copies(sources, late, sems)
        flipped[...] = normed[...].T
        for i in range(3):
            back_sum[at(i), :] = jnp.zeros((rows, 768), F32)

    @pl.when(j < steps)
    def _():
        for i in range(3):
            back_sum[at(i), :] += dot_nt(hidden_low[at(i), :], w1[...])
        fill_part(where, send, keep, 0, dot_nn(flipped[...], hidden_low[...]).astype(BF16))

    @pl.when(j == steps)
    def _():
        for i in range(len(late)):
            pltpu.make_async_copy(sources[i], late[i], sems.at[i]).wait()
        zero = jnp.zeros((1, 768), F32)
        grad_out, grad_gain, grad_shift, grad_b2 = zero, zero, zero, zero
        for i in range(3):
            centre, recip = centred(mid[at(i), :])
            back = back_sum[at(i), :]
            unit, through = norm_back(centre, recip, back, gain)
            c = cots[i][...].astype(F32)
            m = c + through
            grad_gain = grad_gain + jnp.sum(back * unit, axis=0, keepdims=True)
            grad_shift = grad_shift + jnp.sum(back, axis=0, keepdims=True)
            grad_out = grad_out + jnp.sum(m, axis=0, keepdims=True)
            grad_b2 = grad_b2 + jnp.sum(c, axis=0, keepdims=True)
            back_mid[at(i), :] = m
            low = m.astype(BF16)
            low_mid[at(i), :] = low
            back_att[at(i), :] = dot_nt(low, w_out[...]).astype(BF16)
            att[at(i), :] = attended_rows(att_full, att_short, i, rows)
        fill_part(where, send, keep, 0, dot_tn(att[...], low_mid[...]).astype(BF16))
        sums[...] = jnp.concatenate(
            [grad_out, grad_gain, grad_shift, grad_b2, zero, zero, zero, zero], axis=0
        )


def feed_back(where, att_full, att_short, cots, w_out, vecs, mid, normed, hidden_low, w1):
    rows = cots[1].shape[0]
    n = rows * 3
    wide = w1.shape[1]
    tile = 768
    steps = wide // tile
    part = pl.BlockSpec((16, 48, 384), lambda j: (0, j, 0))
    return pl.pallas_call(
        functools.partial(feed_back_kernel, steps=steps),
        grid=(steps + 1,),
        in_specs=[SMEM]
        + [ANY] * 4
        + [VMEM, VMEM, ANY, VMEM]
        + [
            pl.BlockSpec((n, tile), lambda j: (0, jnp.minimum(j, steps - 1))),
            pl.BlockSpec((768, tile), lambda j: (0, jnp.minimum(j, steps - 1))),
        ],
        out_specs=[VMEM, VMEM, part, part, VMEM],
        out_shape=[
            shape_of((n, 768), BF16),
            shape_of((n, 768), F32),
            shape_of((16, 48 * (steps + 1), 384), BF16),
            shape_of((16, 48 * (steps + 1), 384), BF16),
            shape_of((8, 768), F32),
        ],
        scratch_shapes=[
            pltpu.VMEM((n, 768), F32),
            pltpu.VMEM((768, n), BF16),
            pltpu.VMEM((n, 768), BF16),
            pltpu.VMEM((n, 768), BF16),
        ]
        + [
            pltpu.VMEM(v.shape, v.dtype) for v in (att_full, att_short, *cots, mid)
        ]
        + [pltpu.SemaphoreType.DMA((5,))],
        compiler_params=limits(44),
        cost_estimate=lasting(26),
        name="feed_back",
    )(where, att_full, att_short, *cots, w_out, vecs, mid, normed, hidden_low, w1)


def project_back_kernel(
    where, x13_in, x2_in, vecs, dq_full_in, dq_short_in, own_full_in, got_full_in,
    keep_short_in, got_pair_in, got_near_in, send, keep, back_out,
    x13, x2, dq_full, dq_short, own_full, got_full, keep_short, got_pair, got_near, back, flipped,
    sems,
):
    rows = x2.shape[0]
    full = dq_full.shape[0]
    gain, shift = vecs[0:1, :], vecs[1:2, :]
    odd = where[1] % 2
    own_rows = pl.ds(pl.multiple_of(odd * rows, rows), rows)
    sources = [
        x13_in, x2_in, dq_full_in, dq_short_in, own_full_in, got_full_in,
        keep_short_in.at[:, own_rows, :], got_pair_in.at[:, own_rows, :], got_near_in,
    ]
    targets = [x13, x2, dq_full, dq_short, own_full, got_full, keep_short, got_pair, got_near]
    copies = start_copies(sources, targets, sems)
    for copy in copies[:2]:
        copy.wait()
    for i, x in enumerate((x13.at[0], x2, x13.at[1])):
        centre, recip = centred(x[...].astype(F32))
        flipped[:, pl.ds(i * rows, rows)] = (centre * recip * gain + shift).astype(BF16).T
    for copy in copies[2:4]:
        copy.wait()
    back[0, :full, :] = dq_full[...]
    back[0, full:, :] = dq_short[...]
    outs = [pltpu.make_async_copy(back.at[k], back_out.at[k], sems.at[k]) for k in range(3)]
    outs[0].start()
    fill_part(where, send, keep, 0, dot_nn(flipped[...], back[0]).astype(BF16))
    for copy in copies[4:]:
        copy.wait()
    for k in range(2):
        total = own_full[k].astype(F32) + got_full[k].astype(F32)
        back[k + 1, :full, :] = total.astype(BF16)
        total = keep_short[k].astype(F32) + got_pair[k].astype(F32) + got_near[k].astype(F32)
        back[k + 1, full:, :] = total.astype(BF16)
        outs[k + 1].start()
        fill_part(where, send, keep, k + 1, dot_nn(flipped[...], back[k + 1]).astype(BF16))
    for copy in outs:
        copy.wait()


def project_back(where, xs, vecs, *backs):
    rows = xs[1].shape[0]
    n = rows * 3
    short = (2, rows, 768)
    held = [(v.shape, v.dtype) for v in (*xs, *backs[:4])] + [(short, BF16)] * 3
    return pl.pallas_call(
        project_back_kernel,
        in_specs=[SMEM, ANY, ANY, VMEM] + [ANY] * 7,
        out_specs=[VMEM] * 2 + [ANY],
        out_shape=[shape_of((16, 144, 384), BF16)] * 2 + [shape_of((3, n, 768), BF16)],
        scratch_shapes=[pltpu.VMEM(*each) for each in held]
        + [pltpu.VMEM((3, n, 768), BF16), pltpu.VMEM((768, n), BF16)]
        + [pltpu.SemaphoreType.DMA((9,))],
        compiler_params=limits(40),
        cost_estimate=lasting(11),
        name="project_back",
    )(where, *xs, vecs, *backs)


def input_back_kernel(
    where, x13, x2, vecs, w_in, back_mid, back, sums, gb1, o13, o2, lines, total, w, sems
):
    i = pl.program_id(0)
    rows = x2.shape[0]
    gain = vecs[0:1, :]

    @pl.when(i == 0)
    def _():
        (copy,) = start_copies([w_in], [w], sems)
        total[...] = jnp.zeros(total.shape, F32)
        copy.wait()

    x = jnp.where(i == 1, x2[...], x13[0])
    centre, recip = centred(x.astype(F32))
    back_normed = dot_nt(back[0], w[:, :768])
    for k in (1, 2):
        back_normed = back_normed + dot_nt(back[k], w[:, 768 * k : 768 * (k + 1)])
    unit, through = norm_back(centre, recip, back_normed, gain)
    out = (back_mid[...] + through).astype(BF16)

    @pl.when(i == 1)
    def _():
        o2[...] = out

    @pl.when(i != 1)
    def _():
        o13[0] = out

    ones = jnp.ones((8, rows), BF16)
    total[...] += jnp.concatenate(
        [
            jnp.sum(back_normed * unit, axis=0, keepdims=True),
            jnp.sum(back_normed, axis=0, keepdims=True),
            dot_nn(ones, back[0])[0:1],
            dot_nn(ones, back[2])[0:1],
            jnp.zeros((4, 768), F32),
        ],
        axis=0,
    )

    @pl.when(i == 2)
    def _():
        each = [sums[k : k + 1, :] for k in range(4)] + [total[k : k + 1, :] for k in range(4)]
        each += [gb1[:, k * 768 : (k + 1) * 768] for k in range(gb1.shape[1] // 768)]
        for k in range(16):
            block = jnp.zeros((16, 384), F32)
            if k < len(each):
                block = jnp.concatenate(
                    [each[k][:, :384], each[k][:, 384:], block[:14]], axis=0
                )
            lines[k ^ where[1]] = block.astype(BF16)


def input_back(where, xs, vecs, w, back_mid, back, sums, gb1):
    rows = xs[1].shape[0]
    return pl.pallas_call(
        input_back_kernel,
        grid=(3,),
        in_specs=[
            SMEM,
            pl.BlockSpec((1, rows, 768), lambda i: (i // 2, 0, 0)),
            VMEM,
            VMEM,
            ANY,
            pl.BlockSpec((rows, 768), lambda i: (i, 0)),
            pl.BlockSpec((3, rows, 768), lambda i: (0, i, 0)),
            VMEM,
            VMEM,
        ],
        out_specs=[pl.BlockSpec((1, rows, 768), lambda i: (i // 2, 0, 0)), VMEM, VMEM],
        out_shape=[
            shape_of((2, rows, 768), BF16),
            shape_of((rows, 768), BF16),
            shape_of((16, 16, 384), BF16),
        ],
        scratch_shapes=[
            pltpu.VMEM((8, 768), F32),
            pltpu.VMEM(w.shape, w.dtype),
            pltpu.SemaphoreType.DMA((1,)),
        ],
        compiler_params=limits(32),
        cost_estimate=lasting(9),
        name="input_back",
    )(where, *xs, vecs, w, back_mid, back, sums, gb1)


def finish_kernel(where, mine, other, *refs, with_lines):
    if with_lines:
        mine_rows, other_rows, out, *vectors, rows = refs
    else:
        (out,) = refs
    first = where[0] == 0
    for q in range(16):
        a, b = mine[q // 4, q % 4].astype(F32), other[q // 4, q % 4].astype(F32)
        at = pl.ds(pl.multiple_of((q ^ where[1]) * 48, 48), 48)
        out[at, :384] = jnp.where(first, a, b)
        out[at, 384:] = jnp.where(first, b, a)
    if not with_lines:
        return

    @pl.when(pl.program_id(0) == 0)
    def _():
        for q in range(16):
            both = mine_rows[q // 4, q % 4].astype(F32) + other_rows[q // 4, q % 4].astype(F32)
            rows[pl.ds(q ^ where[1], 1), :] = jnp.concatenate([both[0:1], both[1:2]], axis=1)
        for k in range(len(vectors) - 1):
            vectors[k][...] = rows[k, :]
        size = rows.shape[1]
        for k in range(vectors[-1].shape[0] // size):
            vectors[-1][pl.ds(k * size, size)] = rows[len(vectors) - 1 + k, :]


def finish(where, mine, other, start, count, across, with_lines=False):
    block = pl.BlockSpec((4, 4, 48, 384), lambda j: (0, 0, start + j, 0))
    spare = pl.BlockSpec((4, 4, 16, 384), lambda j: (0, 0, 3 * count, 0))
    shape = (768, 768 * count) if across else (768 * count, 768)
    result = [shape_of(shape, F32)]
    specs = [pl.BlockSpec((768, 768), (lambda j: (0, j)) if across else (lambda j: (j, 0)))]
    scratch = []
    if with_lines:
        result += [shape_of((768,), F32)] * 8 + [shape_of((3072,), F32)]
        specs += [VMEM] * 9
        scratch = [pltpu.VMEM((16, 768), F32)]
    out = pl.pallas_call(
        functools.partial(finish_kernel, with_lines=with_lines),
        grid=(count,),
        in_specs=[SMEM, block, block] + [spare, spare] * with_lines,
        out_specs=specs,
        out_shape=result,
        scratch_shapes=scratch,
        compiler_params=limits(20),
        cost_estimate=lasting(4),
        name="finish",
    )(where, mine, other, *[mine, other] * with_lines)
    return out if with_lines else out[0]


FIRST_TO = {
    (0, 0): (0, 0), (0, 1): (0, 1), (0, 2): (1, 0), (0, 3): (1, 1),
    (1, 0): (0, 2), (1, 1): (0, 3), (1, 2): (1, 2), (1, 3): (1, 3),
}
SECOND_TO = {
    (0, 0): (0, 1), (0, 1): (0, 0), (0, 2): (1, 1), (0, 3): (1, 0),
    (1, 0): (0, 3), (1, 1): (0, 2), (1, 2): (1, 3), (1, 3): (1, 2),
}


def column_pairs(table):
    pairs = []
    for chip in range(4):
        for (core, z), (core_to, z_to) in table.items():
            pairs.append(((chip * 2 + core) * 4 + z, (chip * 2 + core_to) * 4 + z_to))
    return pairs


def exchange_short(block):
    pairs = ([], [], [])
    for chip in range(4):
        for core in range(2):
            for z in range(4):
                if core == 1 and z % 2 == 1:
                    continue
                me = (chip * 2 + core) * 4 + z
                to = (chip * 2 + 1 - core) * 4
                pairs[0].append((me, (chip * 2 + core) * 4 + (z ^ 1)))
                pairs[1].append((me, to + z))
                pairs[2].append((me, to + (z ^ 1)))
    return tuple(lax.ppermute(block, ("dp", "blk"), p) for p in pairs)


CHIPS = [[0, 2, 4, 6], [1, 3, 5, 7]]


def flip_pairs(size, mask):
    return [(i, i ^ mask) for i in range(size)]


def swap(array, axis, mask):
    return lax.ppermute(array, axis, flip_pairs(8 if axis == "dp" else 4, mask))


def add_low(*terms):
    return sum(term.astype(F32) for term in terms).astype(BF16)


def find_slots(counts, odd):
    short = jnp.where(counts[1] < counts[0], 1, jnp.where(counts[2] < counts[0], 2, 0))
    one = jnp.where(short == 0, 1, 0)
    two = jnp.where(short == 2, 1, 2)
    return jnp.where(odd == 0, one, two), jnp.where(odd == 0, two, one), short


def leave_kernel(counts, odd, source, pair, single, sems):
    slots = find_slots(counts, odd[0])
    copies = start_copies(
        [source.at[slots[0]], source.at[slots[2]], source.at[slots[1]]],
        [pair.at[0], pair.at[1], single],
        sems,
    )
    for copy in copies:
        copy.wait()


def leave(counts, odd, array):
    rows = array.shape[1]
    return pl.pallas_call(
        leave_kernel,
        in_specs=[SMEM, SMEM, ANY],
        out_specs=[VMEM, VMEM],
        out_shape=[shape_of((2, rows, 768), BF16), shape_of((rows, 768), BF16)],
        scratch_shapes=[pltpu.SemaphoreType.DMA((3,))],
        cost_estimate=lasting(2),
        name="leave",
    )(counts, odd.reshape(1).astype(jnp.int32), array)


class Place:
    def __init__(self):
        dp = lax.axis_index("dp")
        self.z = lax.axis_index("blk")
        self.core = dp % 2
        self.chip = dp // 2


def after(value, *others):
    return lax.optimization_barrier((value,) + others)[0]


def by_chip(keep, got):
    return [add_low(keep[4 * k : 4 * k + 4], got[4 * k : 4 * k + 4]) for k in range(4)]


def over_chips(sums):
    return [swap(sums[k], "dp", 2 * k) for k in (1, 2, 3)]


def over_line(quarter):
    return [swap(quarter[k], "blk", k) for k in (1, 2, 3)]


def gather_all(part):
    every = lax.all_gather(part, ("dp", "blk"), axis=0)
    return every.reshape((4, 2, 4) + every.shape[1:])


def local_paired(
    tokens,
    counts,
    ln1_gain,
    ln1_shift,
    w_qkv,
    bias_q,
    bias_v,
    w_out,
    bias_out,
    ln2_gain,
    ln2_shift,
    w_fc1,
    bias_fc1,
    w_fc2,
    bias_fc2,
    cotangent,
):
    place = Place()
    odd = place.z % 2
    slots = find_slots(counts, odd)

    def arrange(pieces):
        (one, three), two = pieces
        return jnp.stack(
            [
                jnp.where(slots[0] == i, one, jnp.where(slots[1] == i, two, three))
                for i in range(3)
            ]
        )

    where = jnp.stack(
        [place.core, place.chip * 4 + place.z, 2 * place.core + odd]
    ).astype(jnp.int32)

    def move(pieces):
        return tuple(
            lax.ppermute(piece, ("dp", "blk"), column_pairs(table))
            for piece, table in zip(pieces, (FIRST_TO, SECOND_TO))
        )

    def give(pieces):
        return tuple(
            None
            if piece is None
            else lax.ppermute(piece, ("dp", "blk"), [pair[::-1] for pair in column_pairs(table)])
            for piece, table in zip(pieces, (FIRST_TO, SECOND_TO))
        )

    wide = w_fc1.shape[1] // 768
    rows = tokens.shape[1]
    vectors = [ln1_gain, ln1_shift, bias_q, bias_v, bias_out, ln2_gain, ln2_shift, bias_fc2]
    vecs, b1, w_near = prepare(jnp.stack(vectors), bias_fc1.reshape(1, -1), w_qkv)
    vecs_one, vecs_two = vecs[:4], vecs[4:]
    token_sends = leave(counts, odd, tokens)
    x13, x2 = move(token_sends)
    xs = (x13, x2)
    cot_sends = leave(counts, odd, after(cotangent, *token_sends))
    x3 = after(x13[1], x2, vecs, *cot_sends)
    short_blocks = exchange_short(x3)
    q_full, kv_full = project(x13, after(x2, x3), vecs_one, w_near)
    kv_other = swap(kv_full, "dp", 1)
    cots = move(after(cot_sends, x3))
    seq = 2 * kv_full.shape[1]
    kv_both = [kv_full, kv_other]
    att_full, t_full = attend(q_full, kv_both, seq, 768, 384)
    spare = -(-(SHORT - 2 * rows) // LANES) * LANES
    q_short, kv_head, kv_tail = project_short(
        where, x13, *after(short_blocks, att_full), vecs_one, w_near, spare
    )
    kv_short = [kv_head, kv_tail]
    att_short, t_short = attend(q_short, kv_short, SHORT, 384, 384)
    cots = after(cots, att_short)
    o13, o2, mid, normed_two, hidden_low, send_a, keep_a, gb1 = feed(
        where, att_full, att_short, xs, cots, w_out, vecs_two, w_fc1, b1, w_fc2
    )
    got_a = swap(send_a, "dp", 1)
    home_one = give((o13, o2))
    sums_a = by_chip(keep_a, got_a)
    chips_a = over_chips(sums_a)
    back_att, back_mid, send_b, keep_b, feed_sums = feed_back(
        where, att_full, att_short, cots, w_out, vecs_two, after(mid, *sums_a), normed_two,
        hidden_low, w_fc1,
    )
    home = (after(home_one[0], back_mid), home_one[1])
    quarter_a = add_low(after(sums_a[0], back_mid, home[0]), *chips_a)
    line_a = over_line(quarter_a)
    got_b = swap(after(send_b, quarter_a), "dp", 1)

    n_full = q_full.shape[0]
    dq_short, keep_short, send_pair = attend_back(
        where, after(q_short, quarter_a), back_att, n_full, att_short, t_short, kv_short, SHORT,
        768, 0, 6, True,
    )
    home = (home[0], after(home[1], dq_short))
    part_a = add_low(after(quarter_a[0], dq_short, home[1]), *line_a)
    all_a = gather_all(part_a)
    got_pair = swap(after(send_pair, part_a), "dp", 1)
    sums_b = by_chip(after(keep_b, dq_short, part_a), got_b)
    chips_b = over_chips(sums_b)
    away = (1 - odd) * rows
    send_short = add_low(
        lax.dynamic_slice_in_dim(keep_short, away, rows, 1),
        lax.dynamic_slice_in_dim(after(got_pair, *sums_b), away, rows, 1),
    )
    got_near = swap(send_short, "blk", 1)
    dq_full, own_full, sent_full = attend_back(
        where, after(q_full, send_short), back_att, 0, att_full, t_full, kv_both, seq, 768, 0, 6
    )
    got_near = after(got_near, dq_full)
    quarter_b = add_low(after(sums_b[0], dq_full, got_near), *chips_b)
    got_full = swap(after(sent_full, quarter_b), "dp", 1)
    line_b = over_line(quarter_b)
    send_c, keep_c, back = project_back(
        where, xs, vecs_one, dq_full, dq_short, own_full, got_full, keep_short, got_pair, got_near
    )
    part_b = add_low(after(quarter_b[0], keep_c), *line_b)
    got_c = swap(after(send_c, part_b), "dp", 1)
    near_b = over_line([part_b] * 4)
    i13, i2, line_sums = input_back(
        where, xs, vecs_one, w_qkv, back_mid, after(back, part_b), feed_sums, gb1
    )
    near_b = jnp.stack([after(part_b, i2)] + near_b)
    half_b = lax.all_gather(near_b, "dp", axis=0, axis_index_groups=CHIPS)
    sums_c = [
        jnp.concatenate([total, line_sums[4 * k : 4 * k + 4]], axis=1)
        for k, total in enumerate(by_chip(after(keep_c, i2, near_b), got_c))
    ]
    chips_c = over_chips(sums_c)
    (i13_home,) = give((i13, None))[:1]
    output = arrange(after(home, *sums_c))
    all_a = after(all_a, *sums_c)
    halves_a = [all_a[:, c] for c in range(2)]
    grad_w_fc2 = finish(jnp.zeros((3,), jnp.int32), *halves_a, 0, wide, False)
    i13_home = after(i13_home, grad_w_fc2, output)
    quarter_c = add_low(after(sums_c[0], i13_home), *chips_c)
    line_c = over_line(quarter_c)
    part_c = add_low(quarter_c[0], *line_c)
    near_c = jnp.stack([part_c] + over_line([part_c] * 4))
    far_c = over_chips([near_c] * 4)
    i2_home = give((None, after(i2, near_c)))[1]
    half_b = after(half_b, near_c)
    other_b = swap(half_b, "dp", 1)
    inside = where * jnp.array([1, 0, 0], jnp.int32) + jnp.array([0, 1, 0], jnp.int32) * place.z
    grad_w_fc1 = finish(inside, half_b, other_b, 0, wide, True)
    grad_w_out = finish(inside, half_b, other_b, wide, 1, True)
    i2_home = after(i2_home, grad_w_fc1, grad_w_out)
    whole_c = jnp.stack([after(near_c, i2_home)] + far_c)
    other_c = swap(whole_c, "dp", 1)
    input_grad = arrange(after((i13_home, i2_home), whole_c)).astype(F32)
    grad_w_qkv, *lines = finish(where, whole_c, other_c, 0, 3, True, True)
    return (
        output,
        input_grad,
        lines[4],
        lines[5],
        grad_w_qkv,
        lines[6],
        lines[7],
        grad_w_out,
        lines[0],
        lines[1],
        lines[2],
        grad_w_fc1,
        lines[8],
        grad_w_fc2,
        lines[3],
    )


def solution(mesh):
    paired = mesh.shape["dp"] == 8 and mesh.shape["blk"] == 4
    chosen = local_paired if paired else local
    return jax.shard_map(
        chosen,
        mesh=mesh,
        in_specs=(
            P("dp", "blk", None),
            P("dp"),
            P(),
            P(),
            P(),
            P(),
            P(),
            P(),
            P(),
            P(),
            P(),
            P(),
            P(),
            P(),
            P(),
            P("dp", "blk", None),
        ),
        out_specs=(
            P("dp", "blk", None),
            P("dp", "blk", None),
            P(),
            P(),
            P(),
            P(),
            P(),
            P(),
            P(),
            P(),
            P(),
            P(),
            P(),
            P(),
            P(),
        ),
        check_vma=False,
    )
```

```python
import functools
import math

import jax
import jax.numpy as jnp
from jax import lax
from jax.experimental import pallas as pl
from jax.experimental.pallas import tpu as pltpu
from jax.sharding import PartitionSpec as P

HEADS = 12
HD = 64
SHORT = 864


NORM_EPS = 1e-06
MASK_LOW = -1e30


def norm_rows(values, gain, shift):
    centre = values - jnp.mean(values, axis=-1, keepdims=True)
    spread = jnp.mean(centre * centre, axis=-1, keepdims=True)
    return centre * lax.rsqrt(spread + NORM_EPS) * gain + shift


def gelu_exact(values):
    return jax.nn.gelu(values, approximate=False)


def cube_valid(counts, offset, length):
    places = offset + jnp.arange(length, dtype=jnp.int32)
    return places[None, :] < counts[:, None]


def total_every(parts):
    split = (
        lax.psum_scatter(
            parts[0].astype(jnp.bfloat16), "blk", scatter_dimension=0, tiled=True
        ).astype(jnp.float32),
        lax.psum_scatter(
            parts[1].astype(jnp.bfloat16), "blk", scatter_dimension=0, tiled=True
        ).astype(jnp.float32),
        lax.psum_scatter(
            parts[2].astype(jnp.bfloat16), "blk", scatter_dimension=0, tiled=True
        ).astype(jnp.float32),
        lax.psum_scatter(
            parts[3].astype(jnp.bfloat16), "blk", scatter_dimension=0, tiled=True
        ).astype(jnp.float32),
        lax.psum_scatter(
            parts[4].astype(jnp.bfloat16), "blk", scatter_dimension=0, tiled=True
        ).astype(jnp.float32),
        lax.psum_scatter(
            parts[5].astype(jnp.bfloat16), "blk", scatter_dimension=0, tiled=True
        ).astype(jnp.float32),
        lax.psum_scatter(
            parts[6].astype(jnp.bfloat16), "blk", scatter_dimension=0, tiled=True
        ).astype(jnp.float32),
        lax.psum_scatter(
            parts[7].astype(jnp.bfloat16), "blk", scatter_dimension=0, tiled=True
        ).astype(jnp.float32),
        lax.psum_scatter(
            parts[8].astype(jnp.bfloat16), "blk", scatter_dimension=0, tiled=True
        ).astype(jnp.float32),
        lax.psum_scatter(
            parts[9].astype(jnp.bfloat16), "blk", scatter_dimension=0, tiled=True
        ).astype(jnp.float32),
        lax.psum_scatter(
            parts[10].astype(jnp.bfloat16), "blk", scatter_dimension=0, tiled=True
        ).astype(jnp.float32),
        lax.psum_scatter(
            parts[11].astype(jnp.bfloat16), "blk", scatter_dimension=0, tiled=True
        ).astype(jnp.float32),
        lax.psum_scatter(
            parts[12].astype(jnp.bfloat16), "blk", scatter_dimension=0, tiled=True
        ).astype(jnp.float32),
    )
    summed = (
        lax.psum(split[0].astype(jnp.bfloat16), "dp").astype(jnp.float32),
        lax.psum(split[1].astype(jnp.bfloat16), "dp").astype(jnp.float32),
        lax.psum(split[2].astype(jnp.bfloat16), "dp").astype(jnp.float32),
        lax.psum(split[3].astype(jnp.bfloat16), "dp").astype(jnp.float32),
        lax.psum(split[4].astype(jnp.bfloat16), "dp").astype(jnp.float32),
        lax.psum(split[5].astype(jnp.bfloat16), "dp").astype(jnp.float32),
        lax.psum(split[6].astype(jnp.bfloat16), "dp").astype(jnp.float32),
        lax.psum(split[7].astype(jnp.bfloat16), "dp").astype(jnp.float32),
        lax.psum(split[8].astype(jnp.bfloat16), "dp").astype(jnp.float32),
        lax.psum(split[9].astype(jnp.bfloat16), "dp").astype(jnp.float32),
        lax.psum(split[10].astype(jnp.bfloat16), "dp").astype(jnp.float32),
        lax.psum(split[11].astype(jnp.bfloat16), "dp").astype(jnp.float32),
        lax.psum(split[12].astype(jnp.bfloat16), "dp").astype(jnp.float32),
    )
    return (
        lax.all_gather(summed[0].astype(jnp.bfloat16), "blk", axis=0, tiled=True).astype(
            jnp.float32
        ),
        lax.all_gather(summed[1].astype(jnp.bfloat16), "blk", axis=0, tiled=True).astype(
            jnp.float32
        ),
        lax.all_gather(summed[2].astype(jnp.bfloat16), "blk", axis=0, tiled=True).astype(
            jnp.float32
        ),
        lax.all_gather(summed[3].astype(jnp.bfloat16), "blk", axis=0, tiled=True).astype(
            jnp.float32
        ),
        lax.all_gather(summed[4].astype(jnp.bfloat16), "blk", axis=0, tiled=True).astype(
            jnp.float32
        ),
        lax.all_gather(summed[5].astype(jnp.bfloat16), "blk", axis=0, tiled=True).astype(
            jnp.float32
        ),
        lax.all_gather(summed[6].astype(jnp.bfloat16), "blk", axis=0, tiled=True).astype(
            jnp.float32
        ),
        lax.all_gather(summed[7].astype(jnp.bfloat16), "blk", axis=0, tiled=True).astype(
            jnp.float32
        ),
        lax.all_gather(summed[8].astype(jnp.bfloat16), "blk", axis=0, tiled=True).astype(
            jnp.float32
        ),
        lax.all_gather(summed[9].astype(jnp.bfloat16), "blk", axis=0, tiled=True).astype(
            jnp.float32
        ),
        lax.all_gather(summed[10].astype(jnp.bfloat16), "blk", axis=0, tiled=True).astype(
            jnp.float32
        ),
        lax.all_gather(summed[11].astype(jnp.bfloat16), "blk", axis=0, tiled=True).astype(
            jnp.float32
        ),
        lax.all_gather(summed[12].astype(jnp.bfloat16), "blk", axis=0, tiled=True).astype(
            jnp.float32
        ),
    )


def local(
    tokens,
    counts,
    ln1_gain,
    ln1_shift,
    w_qkv,
    bias_q,
    bias_v,
    w_out,
    bias_out,
    ln2_gain,
    ln2_shift,
    w_fc1,
    bias_fc1,
    w_fc2,
    bias_fc2,
    cotangent,
):
    cube_count, row_count, width = tokens.shape
    head_count = HEADS
    depth = HD
    score_scale = HD ** (-0.5)
    inputs = tokens.astype(jnp.float32)
    gain_one = ln1_gain.astype(jnp.float32)
    shift_one = ln1_shift.astype(jnp.float32)
    gain_two = ln2_gain.astype(jnp.float32)
    shift_two = ln2_shift.astype(jnp.float32)
    normed = norm_rows(inputs, gain_one, shift_one).astype(jnp.bfloat16)
    project = jnp.dot(normed, w_qkv, preferred_element_type=jnp.float32)
    queries = (project[..., :width] + bias_q.astype(jnp.float32)).astype(jnp.bfloat16)
    key_local = project[..., width : 2 * width].astype(jnp.bfloat16)
    value_local = (project[..., 2 * width :] + bias_v.astype(jnp.float32)).astype(jnp.bfloat16)
    key_all, value_all = (
        lax.all_gather(key_local, "blk", axis=1, tiled=True),
        lax.all_gather(value_local, "blk", axis=1, tiled=True),
    )
    seq_rows = key_all.shape[1]
    block_rows = math.gcd(seq_rows, 512)
    block_count = seq_rows // block_rows
    block_steps = jnp.arange(block_count, dtype=jnp.int32)
    query_heads = queries.reshape(cube_count, row_count, head_count, depth)

    def key_slices(offset):
        key_part = lax.dynamic_slice_in_dim(key_all, offset, block_rows, 1).reshape(
            cube_count, block_rows, head_count, depth
        )
        value_part = lax.dynamic_slice_in_dim(value_all, offset, block_rows, 1).reshape(
            cube_count, block_rows, head_count, depth
        )
        usable = cube_valid(counts, offset, block_rows)[:, None, None, :]
        return (key_part, value_part, usable)

    def forward_block(carry, step_index):
        row_top, row_total, accum = carry
        key_part, value_part, usable = key_slices(step_index * block_rows)
        scores = (
            jnp.einsum("cqhd,ckhd->chqk", query_heads, key_part, preferred_element_type=jnp.float32)
            * score_scale
        )
        masked = jnp.where(usable, scores, MASK_LOW)
        new_top = jnp.maximum(row_top, jnp.max(masked, axis=-1))
        factor = jnp.exp(row_top - new_top)
        weights = jnp.where(usable, jnp.exp(masked - new_top[..., None]), 0.0)
        row_total = row_total * factor + jnp.sum(weights, axis=-1)
        accum = accum * jnp.transpose(factor, (0, 2, 1))[..., None] + jnp.einsum(
            "chqk,ckhd->cqhd",
            weights.astype(jnp.bfloat16),
            value_part,
            preferred_element_type=jnp.float32,
        )
        return ((new_top, row_total, accum), None)

    start_carry = (
        jnp.full((cube_count, head_count, row_count), MASK_LOW, jnp.float32),
        jnp.zeros((cube_count, head_count, row_count), jnp.float32),
        jnp.zeros((cube_count, row_count, head_count, depth), jnp.float32),
    )
    (row_top, row_total, accum), _ = lax.scan(forward_block, start_carry, block_steps)
    attended_f = (accum / jnp.transpose(row_total, (0, 2, 1))[..., None]).reshape(
        cube_count, row_count, width
    )
    log_total = row_top + jnp.log(row_total)
    attended = attended_f.astype(jnp.bfloat16)
    middle = (
        inputs
        + jnp.dot(attended, w_out, preferred_element_type=jnp.float32)
        + bias_out.astype(jnp.float32)
    )
    normed_two = norm_rows(middle, gain_two, shift_two).astype(jnp.bfloat16)
    hidden = jnp.dot(normed_two, w_fc1, preferred_element_type=jnp.float32) + bias_fc1.astype(
        jnp.float32
    )
    active = gelu_exact(hidden).astype(jnp.bfloat16)
    output = (
        middle
        + jnp.dot(active, w_fc2, preferred_element_type=jnp.float32)
        + bias_fc2.astype(jnp.float32)
    ).astype(jnp.bfloat16)
    grad_bias_fc2 = jnp.sum(cotangent.astype(jnp.float32), axis=(0, 1))
    grad_w_fc2 = jnp.einsum("ctf,ctd->fd", active, cotangent, preferred_element_type=jnp.float32)
    back_active = jnp.einsum("ctd,fd->ctf", cotangent, w_fc2, preferred_element_type=jnp.float32)
    _, gelu_pull = jax.vjp(gelu_exact, hidden)
    back_hidden = gelu_pull(back_active)[0]
    grad_bias_fc1 = jnp.sum(back_hidden, axis=(0, 1))
    hidden_low = back_hidden.astype(jnp.bfloat16)
    grad_w_fc1 = jnp.einsum(
        "ctd,ctf->df", normed_two, hidden_low, preferred_element_type=jnp.float32
    )
    back_normed_two = jnp.einsum(
        "ctf,df->ctd", hidden_low, w_fc1, preferred_element_type=jnp.float32
    )
    _, norm_pull_two = jax.vjp(norm_rows, middle, gain_two, shift_two)
    back_middle_norm, grad_ln2_gain, grad_ln2_shift = norm_pull_two(back_normed_two)
    back_middle = cotangent.astype(jnp.float32) + back_middle_norm
    mlp_grads = (
        grad_ln2_gain,
        grad_ln2_shift,
        grad_w_fc1,
        grad_bias_fc1,
        grad_w_fc2,
        grad_bias_fc2,
    )
    grad_bias_out = jnp.sum(back_middle, axis=(0, 1))
    middle_low = back_middle.astype(jnp.bfloat16)
    grad_w_out = jnp.einsum("ctd,cte->de", attended, middle_low, preferred_element_type=jnp.float32)
    back_attended = jnp.einsum(
        "cte,de->ctd", middle_low, w_out, preferred_element_type=jnp.float32
    ).astype(jnp.bfloat16)
    back_heads = back_attended.reshape(cube_count, row_count, head_count, depth)
    delta = jnp.transpose(
        jnp.sum(
            (back_attended.astype(jnp.float32) * attended_f).reshape(
                cube_count, row_count, head_count, depth
            ),
            axis=-1,
        ),
        (0, 2, 1),
    )

    def block_grads(key_part, value_part, usable):
        scores = (
            jnp.einsum("cqhd,ckhd->chqk", query_heads, key_part, preferred_element_type=jnp.float32)
            * score_scale
        )
        probs = jnp.where(usable, jnp.exp(scores - log_total[..., None]), 0.0)
        back_probs = jnp.einsum(
            "cqhd,ckhd->chqk", back_heads, value_part, preferred_element_type=jnp.float32
        )
        back_scores = (probs * (back_probs - delta[..., None])).astype(jnp.bfloat16)
        return (probs, back_scores)

    query_zero = jnp.zeros((cube_count, row_count, head_count, depth), jnp.float32)

    def back_block(carry, step_index):
        back_query, key_grads, value_grads = carry
        offset = step_index * block_rows
        key_part, value_part, usable = key_slices(offset)
        probs, back_scores = block_grads(key_part, value_part, usable)
        back_query = (
            back_query
            + jnp.einsum(
                "chqk,ckhd->cqhd", back_scores, key_part, preferred_element_type=jnp.float32
            )
            * score_scale
        )
        key_block = (
            jnp.einsum(
                "chqk,cqhd->ckhd", back_scores, query_heads, preferred_element_type=jnp.float32
            )
            * score_scale
        )
        value_block = jnp.einsum(
            "chqk,cqhd->ckhd",
            probs.astype(jnp.bfloat16),
            back_heads,
            preferred_element_type=jnp.float32,
        )
        key_grads = lax.dynamic_update_slice_in_dim(
            key_grads, key_block.reshape(cube_count, block_rows, width), offset, 1
        )
        value_grads = lax.dynamic_update_slice_in_dim(
            value_grads, value_block.reshape(cube_count, block_rows, width), offset, 1
        )
        return ((back_query, key_grads, value_grads), None)

    full_zero = jnp.zeros((cube_count, seq_rows, width), jnp.float32)
    (back_query, key_grads, value_grads), _ = lax.scan(
        back_block, (query_zero, full_zero, full_zero), block_steps
    )
    key_back, value_back = (
        lax.psum_scatter(
            key_grads.astype(jnp.bfloat16), "blk", scatter_dimension=1, tiled=True
        ).astype(jnp.float32),
        lax.psum_scatter(
            value_grads.astype(jnp.bfloat16), "blk", scatter_dimension=1, tiled=True
        ).astype(jnp.float32),
    )
    query_low = back_query.reshape(cube_count, row_count, width).astype(jnp.bfloat16)
    key_low = key_back.astype(jnp.bfloat16)
    value_low = value_back.astype(jnp.bfloat16)
    grad_bias_q = jnp.sum(query_low.astype(jnp.float32), axis=(0, 1))
    grad_bias_v = jnp.sum(value_low.astype(jnp.float32), axis=(0, 1))
    back_project = jnp.concatenate([query_low, key_low, value_low], axis=-1)
    grad_w_qkv = jnp.einsum("ctd,cte->de", normed, back_project, preferred_element_type=jnp.float32)
    back_normed = jnp.einsum("cte,de->ctd", back_project, w_qkv, preferred_element_type=jnp.float32)
    _, norm_pull_one = jax.vjp(norm_rows, inputs, gain_one, shift_one)
    back_inputs, grad_ln1_gain, grad_ln1_shift = norm_pull_one(back_normed)
    input_grad = back_middle + back_inputs
    attn_grads = (
        grad_ln1_gain,
        grad_ln1_shift,
        grad_w_qkv,
        grad_bias_q,
        grad_bias_v,
        grad_w_out,
        grad_bias_out,
    )
    every_grad = total_every(attn_grads + mlp_grads)
    attn_grads = every_grad[:7]
    mlp_grads = every_grad[7:]
    return (
        output,
        input_grad,
        attn_grads[0],
        attn_grads[1],
        attn_grads[2],
        attn_grads[3],
        attn_grads[4],
        attn_grads[5],
        attn_grads[6],
        mlp_grads[0],
        mlp_grads[1],
        mlp_grads[2],
        mlp_grads[3],
        mlp_grads[4],
        mlp_grads[5],
    )


F32 = jnp.float32
BF16 = jnp.bfloat16
EXP_SCALE = math.log2(math.e) / 8
LANES = 128
CUT = 256
VMEM = pl.BlockSpec(memory_space=pltpu.VMEM)
SMEM = pl.BlockSpec(memory_space=pltpu.SMEM)
ANY = pl.BlockSpec(memory_space=pl.ANY)


def lasting(micros):
    return pl.CostEstimate(flops=micros * 10**9, bytes_accessed=2**20, transcendentals=0)


def shape_of(shape, dtype):
    return jax.ShapeDtypeStruct(shape, dtype)


def limits(mib):
    return pltpu.CompilerParams(vmem_limit_bytes=mib * 2**20)


def dot_nt(a, b):
    return lax.dot_general(a, b, (((1,), (1,)), ((), ())), preferred_element_type=F32)


def dot_nn(a, b):
    return lax.dot_general(a, b, (((1,), (0,)), ((), ())), preferred_element_type=F32)


def dot_tn(a, b):
    return lax.dot_general(a, b, (((0,), (0,)), ((), ())), preferred_element_type=F32)


def centred(values):
    centre = values - jnp.mean(values, axis=1, keepdims=True)
    spread = jnp.mean(centre * centre, axis=1, keepdims=True)
    return centre, lax.rsqrt(spread + NORM_EPS)


def norm_back(centre, recip, back, gain):
    unit = centre * recip
    grad = back * gain
    inner = jnp.mean(grad * unit, axis=1, keepdims=True)
    return unit, recip * (grad - jnp.mean(grad, axis=1, keepdims=True) - unit * inner)


def prepare_kernel(a, b, w, out_a, out_b, out_w):
    out_a[...] = a[...].astype(F32)
    out_b[...] = b[...].astype(F32)
    out_w[...] = w[...]


def prepare(a, b, w):
    return pl.pallas_call(
        prepare_kernel,
        in_specs=[VMEM] * 3,
        out_specs=[VMEM] * 3,
        out_shape=[shape_of(a.shape, F32), shape_of(b.shape, F32), shape_of(w.shape, w.dtype)],
        compiler_params=limits(16),
        cost_estimate=lasting(2),
        name="prepare",
    )(a, b, w)


def project_rows(x, vecs, w, q_ref, kv_ref, at, q_at=None):
    gain, shift, bias_q, bias_v = (vecs[i : i + 1, :] for i in range(4))
    centre, recip = centred(x.astype(F32))
    normed = (centre * recip * gain + shift).astype(BF16)
    kv_ref[0, at, :] = dot_nn(normed, w[:, 768:1536]).astype(BF16)
    kv_ref[1, at, :] = (dot_nn(normed, w[:, 1536:]) + bias_v).astype(BF16)
    if q_at is not None:
        q_ref[q_at, :] = (dot_nn(normed, w[:, :768]) + bias_q).astype(BF16)


def project_kernel(x13_in, x2_in, vecs, w_in, q_ref, kv_ref, held, w, sems):
    copies = start_copies([x13_in.at[0], x2_in, w_in], [held.at[0], held.at[1], w], sems)
    for copy in copies:
        copy.wait()
    rows = held.shape[1]
    for i in range(2):
        at = pl.ds(i * rows, rows)
        project_rows(held[i], vecs, w, q_ref, kv_ref, at, at)


def project(x13, x2, vecs, w):
    n = 2 * x2.shape[0]
    return pl.pallas_call(
        project_kernel,
        in_specs=[ANY, ANY, VMEM, ANY],
        out_specs=[VMEM] * 2,
        out_shape=[shape_of((n, 768), BF16), shape_of((2, n, 768), BF16)],
        scratch_shapes=[
            pltpu.VMEM((2,) + x2.shape, BF16),
            pltpu.VMEM(w.shape, w.dtype),
            pltpu.SemaphoreType.DMA((3,)),
        ],
        compiler_params=limits(24),
        cost_estimate=lasting(4),
        name="project",
    )(x13, x2, vecs, w)


def project_short_kernel(
    where, x13, near, other, far, vecs, w_in, q_ref, head_ref, tail_ref, w, held, sems, *, spare
):
    (copy,) = start_copies([w_in], [w], sems)
    rows = near.shape[0]
    mine = where[2]
    for k, block in enumerate((x13[1], near[...], other[...], far[...])):
        held[k ^ mine] = block
    copy.wait()
    for i in range(2):
        project_rows(held[i], vecs, w, None, head_ref, pl.ds(i * rows, rows))
    project_rows(held[2][:spare], vecs, w, None, tail_ref, pl.ds(0, spare))
    centre, recip = centred(x13[1].astype(F32))
    normed = (centre * recip * vecs[0:1, :] + vecs[1:2, :]).astype(BF16)
    q_ref[...] = (dot_nn(normed, w[:, :768]) + vecs[2:3, :]).astype(BF16)


def project_short(where, x13, near, other, far, vecs, w, spare):
    rows = near.shape[0]
    return pl.pallas_call(
        functools.partial(project_short_kernel, spare=spare),
        in_specs=[SMEM] + [VMEM] * 5 + [ANY],
        out_specs=[VMEM] * 3,
        out_shape=[
            shape_of((rows, 768), BF16),
            shape_of((2, 2 * rows, 768), BF16),
            shape_of((2, spare, 768), BF16),
        ],
        scratch_shapes=[
            pltpu.VMEM(w.shape, w.dtype),
            pltpu.VMEM((4, rows, 768), BF16),
            pltpu.SemaphoreType.DMA((1,)),
        ],
        compiler_params=limits(24),
        cost_estimate=lasting(4),
        name="project_short",
    )(where, x13, near, other, far, vecs, w)


def start_copies(sources, targets, sems):
    copies = [
        pltpu.make_async_copy(source, target, sems.at[i])
        for i, (source, target) in enumerate(zip(sources, targets))
    ]
    for copy in copies:
        copy.start()
    return copies


def three_parts(values, lane):
    high = values.astype(BF16)
    rest = values - high.astype(F32)
    middle = rest.astype(BF16)
    least = (rest - middle.astype(F32)).astype(BF16)
    zero = jnp.zeros((), BF16)
    return jnp.where(
        lane == 0, high, jnp.where(lane == 1, middle, jnp.where(lane == 2, least, zero))
    )


def lane_index(rows=1):
    return lax.broadcasted_iota(jnp.int32, (rows, LANES), 1)


def attend_kernel(*refs, pieces, valid, step):
    q_ref = refs[0]
    kvs = refs[1 : 1 + pieces]
    o_ref, t_ref = refs[1 + pieces :]
    lane = lane_index()
    low = lane < 64
    half = lane % 64
    total = sum(kv.shape[1] for kv in kvs)
    keys, values = [], []
    for h in range(2):
        own = low if h == 0 else ~low
        key_parts, value_parts, at = [], [], 0
        for kv in kvs:
            n = kv.shape[1]
            beside = jnp.zeros((n, LANES), BF16)
            if at + n > valid:
                place = lax.broadcasted_iota(jnp.int32, (n, LANES), 0) + at
                beside = jnp.where(
                    (place >= valid) & (lane_index(n) % 64 == 0), MASK_LOW, 0.0
                ).astype(BF16)
            key_parts.append(jnp.where(own, kv[0], beside))
            value_parts.append(jnp.where(own, kv[1], jnp.ones((), BF16)))
            at += n
        keys.append(key_parts)
        values.append(value_parts)
    cuts = [
        (i, first, min(CUT, kv.shape[1] - first))
        for i, kv in enumerate(kvs)
        for first in range(0, kv.shape[1], CUT)
    ]
    for s in range(q_ref.shape[0] // step):
        at = pl.ds(s * step, step)
        q = q_ref[at, :]
        sums, tops = [], []
        for h in range(2):
            own = low if h == 0 else ~low
            q_own = q
            if total > valid:
                q_own = jnp.where(own, q, jnp.where(half == 0, 1.0, 0.0).astype(BF16))
            top, kept = None, None
            for i, first, size in cuts:
                scores = dot_nt(q_own, keys[h][i][first : first + size]) * EXP_SCALE
                new_top = jnp.max(scores, axis=1, keepdims=True)
                if top is not None:
                    new_top = jnp.maximum(top, new_top)
                weights = jnp.exp2(scores - new_top).astype(BF16)
                part = dot_nn(weights, values[h][i][first : first + size])
                kept = part if top is None else kept * jnp.exp2(top - new_top) + part
                top = new_top
            sums.append(kept)
            tops.append(top)
        above = jnp.where(low, sums[0], sums[1])
        below = jnp.where(low, sums[1], sums[0])
        o_ref[at, :] = above / pltpu.roll(below, 64, 1)
        top = jnp.where(low, tops[1], tops[0]) * (1.0 / EXP_SCALE)
        t_ref[at, :] = jnp.where(
            half == 3, jnp.ones((), BF16), three_parts(-(top + 8.0 * jnp.log(below)), half)
        )


def attend(q, kvs, valid, rows, step, first=0, count=6):
    n = q.shape[0]
    keys = sum(kv.shape[1] for kv in kvs)
    block = pl.BlockSpec((rows, LANES), lambda p, i: (i, p))
    return pl.pallas_call(
        functools.partial(attend_kernel, pieces=len(kvs), valid=valid, step=step),
        out_shape=[shape_of((n, LANES * count), F32), shape_of((n, LANES * count), BF16)],
        grid=(count, n // rows),
        in_specs=[pl.BlockSpec((rows, LANES), lambda p, i: (i, first + p))]
        + [pl.BlockSpec((2, kv.shape[1], LANES), lambda p, i: (0, 0, first + p)) for kv in kvs],
        out_specs=[block, block],
        compiler_params=limits(24),
        cost_estimate=lasting(n * keys * count // 280000),
        name="attend",
    )(q, *kvs)


def attend_back_kernel(*refs, pieces, valid, step, split):
    where = refs[0]
    q_ref, do_ref, o_ref, t_ref = refs[1:5]
    kvs = refs[5 : 5 + pieces]
    dq_ref = refs[5 + pieces]
    outs = refs[6 + pieces :]
    n = q_ref.shape[0]
    lane = lane_index()
    low = lane < 64
    half = lane % 64
    q, do, t = q_ref[...], do_ref[...], t_ref[...]
    product = do.astype(F32) * o_ref[...]
    delta = [
        jnp.sum(jnp.where(low, product, 0.0), axis=1, keepdims=True),
        jnp.sum(jnp.where(low, 0.0, product), axis=1, keepdims=True),
    ]
    d = three_parts(-jnp.where(low, delta[1], delta[0]), half)
    queries = [jnp.where(low, q, t), jnp.where(low, t, q)]
    backs = [jnp.where(low, do, d), jnp.where(low, d, do)]
    ones = jnp.where(half < 3, 1.0, 0.0).astype(BF16)
    sums = [jnp.zeros((LANES, n), F32), jnp.zeros((LANES, n), F32)]
    starts = [sum(kv.shape[1] for kv in kvs[:i]) for i in range(pieces)]
    small = None
    for i in reversed(range(pieces)):
        kv = kvs[i]
        for first in range(0, kv.shape[1], step):
            size = min(step, kv.shape[1] - first)
            at = pl.ds(first, size)
            key_sums, value_sums = [], []
            for h in range(2):
                own = low if h == 0 else ~low
                beside = ones
                if starts[i] + first + size > valid:
                    place = lax.broadcasted_iota(jnp.int32, (size, LANES), 0) + (starts[i] + first)
                    wide = lane_index(size) % 64
                    beside = jnp.where(
                        wide < 3, 1.0, jnp.where((place >= valid) & (wide == 3), MASK_LOW, 0.0)
                    ).astype(BF16)
                key = jnp.where(own, kv[0, at, :], beside)
                value = jnp.where(own, kv[1, at, :], ones)
                probs = jnp.exp2(dot_nt(key, queries[h]) * EXP_SCALE)
                back_scores = (probs * dot_nt(value, backs[h])).astype(BF16)
                value_sums.append(dot_nn(probs.astype(BF16), backs[h]))
                key_sums.append(dot_nn(back_scores, queries[h]))
                sums[h] = sums[h] + dot_tn(key, back_scores)
            both = (
                (jnp.where(low, key_sums[0], key_sums[1]) * 0.125).astype(BF16),
                jnp.where(low, value_sums[0], value_sums[1]).astype(BF16),
            )
            for k in range(2):
                if not split:
                    outs[i][k, at, :] = both[k]
                elif i == 0:
                    other = jnp.zeros_like(both[k])
                    if first == 0:
                        rest = jnp.zeros((size - small[k].shape[0], LANES), BF16)
                        other = jnp.concatenate([small[k], rest], axis=0)
                    stays = where[0] == 0
                    outs[0][k, at, :] = jnp.where(stays, both[k], other)
                    outs[1][k, at, :] = jnp.where(stays, other, both[k])
            small = both
    both = jnp.concatenate([sums[0][:64], sums[1][64:]], axis=0)
    dq_ref[...] = (both.T * 0.125).astype(BF16)


def attend_back(where, q, do, first_row, o, t, kvs, valid, step, first, count, split=False):
    n = q.shape[0]
    keys = sum(kv.shape[1] for kv in kvs)
    row = first_row // n
    block = pl.BlockSpec((n, LANES), lambda p: (0, first + p))
    back_block = pl.BlockSpec((n, LANES), lambda p: (row, first + p))
    wide = [pl.BlockSpec((2, kv.shape[1], LANES), lambda p: (0, 0, first + p)) for kv in kvs]
    out = pl.BlockSpec((n, LANES), lambda p: (0, p))
    outs = [kvs[0], kvs[0]] if split else kvs
    out_wide = [pl.BlockSpec((2, kv.shape[1], LANES), lambda p: (0, 0, p)) for kv in outs]
    return pl.pallas_call(
        functools.partial(
            attend_back_kernel, pieces=len(kvs), valid=valid, step=step, split=split
        ),
        out_shape=[shape_of((n, LANES * count), BF16)]
        + [shape_of((2, kv.shape[1], LANES * count), BF16) for kv in outs],
        grid=(count,),
        in_specs=[SMEM, block, back_block, block, block] + wide,
        out_specs=[out] + out_wide,
        compiler_params=limits(56),
        cost_estimate=lasting(n * keys * count // 180000),
        name="attend_back",
    )(where, q, do, o, t, *kvs)


def fill_part(where, send, keep, j, block):
    left, right = block[:, :384], block[:, 384:]
    first = where[0] == 0
    for ref, half in (
        (keep, jnp.where(first, left, right)),
        (send, jnp.where(first, right, left)),
    ):
        for p in range(16):
            ref[p ^ where[1], pl.ds(j * 48, 48), :] = half[p * 48 : (p + 1) * 48]


def attended_rows(att_full, att_short, i, rows):
    if i == 2:
        return att_short[...].astype(BF16)
    at = pl.ds(i * rows, rows)
    return att_full[at, :].astype(BF16)


def feed_kernel(
    where, att_full_in, att_short_in, x13_in, x2_in, c13, c2, w_out_in, vecs, w1, b1, w2,
    o13, o2, mid_out, normed_out, hidden_low, send, keep, gb1,
    att_full, att_short, x13, x2, w_out, mid, normed, out_sum, cot, active, sems,
    *, steps, tile,
):
    j = pl.program_id(0)
    xs, outs = (x13.at[0], x2, x13.at[1]), (o13.at[0], o2, o13.at[1])
    rows = x2.shape[0]
    bias_out, gain, shift, b2 = (vecs[i : i + 1, :] for i in range(4))

    def at(i):
        return pl.ds(i * rows, rows)

    def leaving():
        return [
            pltpu.make_async_copy(mid, mid_out, sems.at[0]),
            pltpu.make_async_copy(normed, normed_out, sems.at[1]),
        ]

    @pl.when(j == 0)
    def _():
        copies = start_copies(
            [w_out_in, att_full_in, x13_in, x2_in, att_short_in, c13.at[0], c2, c13.at[1]],
            [w_out, att_full, x13, x2, att_short] + [cot.at[at(i), :] for i in range(3)],
            sems,
        )
        for copy in copies[:4]:
            copy.wait()
        for i in range(3):
            if i == 2:
                copies[4].wait()
            att = attended_rows(att_full, att_short, i, rows)
            m = xs[i][...].astype(F32) + dot_nn(att, w_out[...]) + bias_out
            mid[at(i), :] = m
            centre, recip = centred(m)
            normed[at(i), :] = (centre * recip * gain + shift).astype(BF16)
            out_sum[at(i), :] = m + b2
        for copy in copies[5:]:
            copy.wait()
        for copy in leaving():
            copy.start()

    w1_tile, w2_tile = w1[...], w2[...]
    bias = b1[...]
    bias_sum = jnp.zeros((1, tile), F32)
    for i in range(3):
        h = dot_nn(normed[at(i), :], w1_tile) + bias
        back_active = dot_nt(cot[at(i), :], w2_tile)
        share = 0.5 + 0.5 * lax.erf(h * math.sqrt(0.5))
        act = (h * share).astype(BF16)
        slope = share + h * (math.sqrt(0.5 / math.pi) * jnp.exp(h * h * (-0.5)))
        back_hidden = back_active * slope
        bias_sum = bias_sum + jnp.sum(back_hidden, axis=0, keepdims=True)
        active[at(i), :] = act
        hidden_low[at(i), :] = back_hidden.astype(BF16)
        out_sum[at(i), :] += dot_nn(act, w2_tile)
    gb1[...] = bias_sum
    grad = dot_tn(active[...], cot[...]).astype(BF16)
    fill_part(where, send, keep, 0, grad)

    @pl.when(j == steps - 1)
    def _():
        for copy in leaving():
            copy.wait()
        for i in range(3):
            outs[i][...] = out_sum[at(i), :].astype(BF16)


def feed(where, att_full, att_short, xs, cots, w_out, vecs, w1, b1, w2):
    rows = xs[1].shape[0]
    n = rows * 3
    wide = w1.shape[1]
    tile = 768
    steps = wide // tile
    across = pl.BlockSpec((768, tile), lambda j: (0, j))
    down = pl.BlockSpec((tile, 768), lambda j: (j, 0))
    line = pl.BlockSpec((1, tile), lambda j: (0, j))
    return pl.pallas_call(
        functools.partial(feed_kernel, steps=steps, tile=tile),
        grid=(steps,),
        in_specs=[SMEM] + [ANY] * 7 + [VMEM, across, line, down],
        out_specs=[VMEM] * 2
        + [ANY] * 2
        + [pl.BlockSpec((n, tile), lambda j: (0, j))]
        + [pl.BlockSpec((16, 48, 384), lambda j: (0, j, 0))] * 2
        + [line],
        out_shape=[shape_of((2, rows, 768), BF16), shape_of((rows, 768), BF16)]
        + [
            shape_of((n, 768), F32),
            shape_of((n, 768), BF16),
            shape_of((n, wide), BF16),
            shape_of((16, 48 * steps, 384), BF16),
            shape_of((16, 48 * steps, 384), BF16),
            shape_of((1, wide), F32),
        ],
        scratch_shapes=[
            pltpu.VMEM(v.shape, v.dtype) for v in (att_full, att_short, *xs, w_out)
        ]
        + [
            pltpu.VMEM((n, 768), F32),
            pltpu.VMEM((n, 768), BF16),
            pltpu.VMEM((n, 768), F32),
            pltpu.VMEM((n, 768), BF16),
            pltpu.VMEM((n, tile), BF16),
            pltpu.SemaphoreType.DMA((8,)),
        ],
        compiler_params=limits(40),
        cost_estimate=lasting(36),
        name="feed",
    )(where, att_full, att_short, *xs, *cots, w_out, vecs, w1, b1, w2)


def feed_back_kernel(
    where, att_full_in, att_short_in, c13_in, c2_in, w_out, vecs, mid_in, normed,
    hidden_low, w1,
    back_att, back_mid, send, keep, sums,
    back_sum, flipped, low_mid, att, att_full, att_short, c13, c2, mid, sems,
    *, steps,
):
    j = pl.program_id(0)
    late = (att_full, att_short, c13, c2, mid)
    sources = (att_full_in, att_short_in, c13_in, c2_in, mid_in)
    cots = (c13.at[0], c2, c13.at[1])
    rows = c2.shape[0]
    gain = vecs[1:2, :]

    def at(i):
        return pl.ds(i * rows, rows)

    @pl.when(j == 0)
    def _():
        start_copies(sources, late, sems)
        flipped[...] = normed[...].T
        for i in range(3):
            back_sum[at(i), :] = jnp.zeros((rows, 768), F32)

    @pl.when(j < steps)
    def _():
        for i in range(3):
            back_sum[at(i), :] += dot_nt(hidden_low[at(i), :], w1[...])
        fill_part(where, send, keep, 0, dot_nn(flipped[...], hidden_low[...]).astype(BF16))

    @pl.when(j == steps)
    def _():
        for i in range(len(late)):
            pltpu.make_async_copy(sources[i], late[i], sems.at[i]).wait()
        zero = jnp.zeros((1, 768), F32)
        grad_out, grad_gain, grad_shift, grad_b2 = zero, zero, zero, zero
        for i in range(3):
            centre, recip = centred(mid[at(i), :])
            back = back_sum[at(i), :]
            unit, through = norm_back(centre, recip, back, gain)
            c = cots[i][...].astype(F32)
            m = c + through
            grad_gain = grad_gain + jnp.sum(back * unit, axis=0, keepdims=True)
            grad_shift = grad_shift + jnp.sum(back, axis=0, keepdims=True)
            grad_out = grad_out + jnp.sum(m, axis=0, keepdims=True)
            grad_b2 = grad_b2 + jnp.sum(c, axis=0, keepdims=True)
            back_mid[at(i), :] = m
            low = m.astype(BF16)
            low_mid[at(i), :] = low
            back_att[at(i), :] = dot_nt(low, w_out[...]).astype(BF16)
            att[at(i), :] = attended_rows(att_full, att_short, i, rows)
        fill_part(where, send, keep, 0, dot_tn(att[...], low_mid[...]).astype(BF16))
        sums[...] = jnp.concatenate(
            [grad_out, grad_gain, grad_shift, grad_b2, zero, zero, zero, zero], axis=0
        )


def feed_back(where, att_full, att_short, cots, w_out, vecs, mid, normed, hidden_low, w1):
    rows = cots[1].shape[0]
    n = rows * 3
    wide = w1.shape[1]
    tile = 768
    steps = wide // tile
    part = pl.BlockSpec((16, 48, 384), lambda j: (0, j, 0))
    return pl.pallas_call(
        functools.partial(feed_back_kernel, steps=steps),
        grid=(steps + 1,),
        in_specs=[SMEM]
        + [ANY] * 4
        + [VMEM, VMEM, ANY, VMEM]
        + [
            pl.BlockSpec((n, tile), lambda j: (0, jnp.minimum(j, steps - 1))),
            pl.BlockSpec((768, tile), lambda j: (0, jnp.minimum(j, steps - 1))),
        ],
        out_specs=[VMEM, VMEM, part, part, VMEM],
        out_shape=[
            shape_of((n, 768), BF16),
            shape_of((n, 768), F32),
            shape_of((16, 48 * (steps + 1), 384), BF16),
            shape_of((16, 48 * (steps + 1), 384), BF16),
            shape_of((8, 768), F32),
        ],
        scratch_shapes=[
            pltpu.VMEM((n, 768), F32),
            pltpu.VMEM((768, n), BF16),
            pltpu.VMEM((n, 768), BF16),
            pltpu.VMEM((n, 768), BF16),
        ]
        + [
            pltpu.VMEM(v.shape, v.dtype) for v in (att_full, att_short, *cots, mid)
        ]
        + [pltpu.SemaphoreType.DMA((5,))],
        compiler_params=limits(38),
        cost_estimate=lasting(26),
        name="feed_back",
    )(where, att_full, att_short, *cots, w_out, vecs, mid, normed, hidden_low, w1)


def project_back_kernel(
    where, x13_in, x2_in, vecs, dq_full_in, dq_short_in, own_full_in, got_full_in,
    keep_short_in, got_pair_in, got_near_in, send, keep, back_out,
    x13, x2, dq_full, dq_short, own_full, got_full, keep_short, got_pair, got_near, back, flipped,
    sems,
):
    rows = x2.shape[0]
    full = dq_full.shape[0]
    gain, shift = vecs[0:1, :], vecs[1:2, :]
    odd = where[1] % 2
    own_rows = pl.ds(pl.multiple_of(odd * rows, rows), rows)
    sources = [
        x13_in, x2_in, dq_full_in, dq_short_in, own_full_in, got_full_in,
        keep_short_in.at[:, own_rows, :], got_pair_in.at[:, own_rows, :], got_near_in,
    ]
    targets = [x13, x2, dq_full, dq_short, own_full, got_full, keep_short, got_pair, got_near]
    copies = start_copies(sources, targets, sems)
    for copy in copies[:2]:
        copy.wait()
    for i, x in enumerate((x13.at[0], x2, x13.at[1])):
        centre, recip = centred(x[...].astype(F32))
        flipped[:, pl.ds(i * rows, rows)] = (centre * recip * gain + shift).astype(BF16).T
    for copy in copies[2:4]:
        copy.wait()
    back[0, :full, :] = dq_full[...]
    back[0, full:, :] = dq_short[...]
    outs = [pltpu.make_async_copy(back.at[k], back_out.at[k], sems.at[k]) for k in range(3)]
    outs[0].start()
    fill_part(where, send, keep, 0, dot_nn(flipped[...], back[0]).astype(BF16))
    for copy in copies[4:]:
        copy.wait()
    for k in range(2):
        total = own_full[k].astype(F32) + got_full[k].astype(F32)
        back[k + 1, :full, :] = total.astype(BF16)
        total = keep_short[k].astype(F32) + got_pair[k].astype(F32) + got_near[k].astype(F32)
        back[k + 1, full:, :] = total.astype(BF16)
        outs[k + 1].start()
        fill_part(where, send, keep, k + 1, dot_nn(flipped[...], back[k + 1]).astype(BF16))
    for copy in outs:
        copy.wait()


def project_back(where, xs, vecs, *backs):
    rows = xs[1].shape[0]
    n = rows * 3
    short = (2, rows, 768)
    held = [(v.shape, v.dtype) for v in (*xs, *backs[:4])] + [(short, BF16)] * 3
    return pl.pallas_call(
        project_back_kernel,
        in_specs=[SMEM, ANY, ANY, VMEM] + [ANY] * 7,
        out_specs=[VMEM] * 2 + [ANY],
        out_shape=[shape_of((16, 144, 384), BF16)] * 2 + [shape_of((3, n, 768), BF16)],
        scratch_shapes=[pltpu.VMEM(*each) for each in held]
        + [pltpu.VMEM((3, n, 768), BF16), pltpu.VMEM((768, n), BF16)]
        + [pltpu.SemaphoreType.DMA((9,))],
        compiler_params=limits(40),
        cost_estimate=lasting(11),
        name="project_back",
    )(where, *xs, vecs, *backs)


def input_back_kernel(
    where, x13, x2, vecs, w_in, back_mid, back, sums, gb1, o13, o2, lines, total, w, sems
):
    i = pl.program_id(0)
    rows = x2.shape[0]
    gain = vecs[0:1, :]

    @pl.when(i == 0)
    def _():
        (copy,) = start_copies([w_in], [w], sems)
        total[...] = jnp.zeros(total.shape, F32)
        copy.wait()

    x = jnp.where(i == 1, x2[...], x13[0])
    centre, recip = centred(x.astype(F32))
    back_normed = dot_nt(back[0], w[:, :768])
    for k in (1, 2):
        back_normed = back_normed + dot_nt(back[k], w[:, 768 * k : 768 * (k + 1)])
    unit, through = norm_back(centre, recip, back_normed, gain)
    out = (back_mid[...] + through).astype(BF16)

    @pl.when(i == 1)
    def _():
        o2[...] = out

    @pl.when(i != 1)
    def _():
        o13[0] = out

    ones = jnp.ones((8, rows), BF16)
    total[...] += jnp.concatenate(
        [
            jnp.sum(back_normed * unit, axis=0, keepdims=True),
            jnp.sum(back_normed, axis=0, keepdims=True),
            dot_nn(ones, back[0])[0:1],
            dot_nn(ones, back[2])[0:1],
            jnp.zeros((4, 768), F32),
        ],
        axis=0,
    )

    @pl.when(i == 2)
    def _():
        each = [sums[k : k + 1, :] for k in range(4)] + [total[k : k + 1, :] for k in range(4)]
        each += [gb1[:, k * 768 : (k + 1) * 768] for k in range(gb1.shape[1] // 768)]
        for k in range(16):
            block = jnp.zeros((16, 384), F32)
            if k < len(each):
                block = jnp.concatenate(
                    [each[k][:, :384], each[k][:, 384:], block[:14]], axis=0
                )
            lines[k ^ where[1]] = block.astype(BF16)


def input_back(where, xs, vecs, w, back_mid, back, sums, gb1):
    rows = xs[1].shape[0]
    return pl.pallas_call(
        input_back_kernel,
        grid=(3,),
        in_specs=[
            SMEM,
            pl.BlockSpec((1, rows, 768), lambda i: (i // 2, 0, 0)),
            VMEM,
            VMEM,
            ANY,
            pl.BlockSpec((rows, 768), lambda i: (i, 0)),
            pl.BlockSpec((3, rows, 768), lambda i: (0, i, 0)),
            VMEM,
            VMEM,
        ],
        out_specs=[pl.BlockSpec((1, rows, 768), lambda i: (i // 2, 0, 0)), VMEM, VMEM],
        out_shape=[
            shape_of((2, rows, 768), BF16),
            shape_of((rows, 768), BF16),
            shape_of((16, 16, 384), BF16),
        ],
        scratch_shapes=[
            pltpu.VMEM((8, 768), F32),
            pltpu.VMEM(w.shape, w.dtype),
            pltpu.SemaphoreType.DMA((1,)),
        ],
        compiler_params=limits(32),
        cost_estimate=lasting(9),
        name="input_back",
    )(where, *xs, vecs, w, back_mid, back, sums, gb1)


def finish_kernel(where, mine, other, *refs, with_lines):
    if with_lines:
        mine_rows, other_rows, out, *vectors, rows = refs
    else:
        (out,) = refs
    first = where[0] == 0
    for q in range(16):
        a, b = mine[q // 4, q % 4].astype(F32), other[q // 4, q % 4].astype(F32)
        at = pl.ds(pl.multiple_of((q ^ where[1]) * 48, 48), 48)
        out[at, :384] = jnp.where(first, a, b)
        out[at, 384:] = jnp.where(first, b, a)
    if not with_lines:
        return

    @pl.when(pl.program_id(0) == 0)
    def _():
        for q in range(16):
            both = mine_rows[q // 4, q % 4].astype(F32) + other_rows[q // 4, q % 4].astype(F32)
            rows[pl.ds(q ^ where[1], 1), :] = jnp.concatenate([both[0:1], both[1:2]], axis=1)
        for k in range(len(vectors) - 1):
            vectors[k][...] = rows[k, :]
        size = rows.shape[1]
        for k in range(vectors[-1].shape[0] // size):
            vectors[-1][pl.ds(k * size, size)] = rows[len(vectors) - 1 + k, :]


def finish(where, mine, other, start, count, across, with_lines=False):
    block = pl.BlockSpec((4, 4, 48, 384), lambda j: (0, 0, start + j, 0))
    spare = pl.BlockSpec((4, 4, 16, 384), lambda j: (0, 0, 3 * count, 0))
    shape = (768, 768 * count) if across else (768 * count, 768)
    result = [shape_of(shape, F32)]
    specs = [pl.BlockSpec((768, 768), (lambda j: (0, j)) if across else (lambda j: (j, 0)))]
    scratch = []
    if with_lines:
        result += [shape_of((768,), F32)] * 8 + [shape_of((3072,), F32)]
        specs += [VMEM] * 9
        scratch = [pltpu.VMEM((16, 768), F32)]
    out = pl.pallas_call(
        functools.partial(finish_kernel, with_lines=with_lines),
        grid=(count,),
        in_specs=[SMEM, block, block] + [spare, spare] * with_lines,
        out_specs=specs,
        out_shape=result,
        scratch_shapes=scratch,
        compiler_params=limits(20),
        cost_estimate=lasting(4),
        name="finish",
    )(where, mine, other, *[mine, other] * with_lines)
    return out if with_lines else out[0]


FIRST_TO = {
    (0, 0): (0, 0), (0, 1): (0, 1), (0, 2): (1, 0), (0, 3): (1, 1),
    (1, 0): (0, 2), (1, 1): (0, 3), (1, 2): (1, 2), (1, 3): (1, 3),
}
SECOND_TO = {
    (0, 0): (0, 1), (0, 1): (0, 0), (0, 2): (1, 1), (0, 3): (1, 0),
    (1, 0): (0, 3), (1, 1): (0, 2), (1, 2): (1, 3), (1, 3): (1, 2),
}


def column_pairs(table):
    pairs = []
    for chip in range(4):
        for (core, z), (core_to, z_to) in table.items():
            pairs.append(((chip * 2 + core) * 4 + z, (chip * 2 + core_to) * 4 + z_to))
    return pairs


def exchange_short(block):
    pairs = ([], [], [])
    for chip in range(4):
        for core in range(2):
            for z in range(4):
                if core == 1 and z % 2 == 1:
                    continue
                me = (chip * 2 + core) * 4 + z
                to = (chip * 2 + 1 - core) * 4
                pairs[0].append((me, (chip * 2 + core) * 4 + (z ^ 1)))
                pairs[1].append((me, to + z))
                pairs[2].append((me, to + (z ^ 1)))
    return tuple(lax.ppermute(block, ("dp", "blk"), p) for p in pairs)


CHIPS = [[0, 2, 4, 6], [1, 3, 5, 7]]


def flip_pairs(size, mask):
    return [(i, i ^ mask) for i in range(size)]


def swap(array, axis, mask):
    return lax.ppermute(array, axis, flip_pairs(8 if axis == "dp" else 4, mask))


def add_low(*terms):
    return sum(term.astype(F32) for term in terms).astype(BF16)


def find_slots(counts, odd):
    short = jnp.where(counts[1] < counts[0], 1, jnp.where(counts[2] < counts[0], 2, 0))
    one = jnp.where(short == 0, 1, 0)
    two = jnp.where(short == 2, 1, 2)
    return jnp.where(odd == 0, one, two), jnp.where(odd == 0, two, one), short


def leave_kernel(counts, odd, source, pair, single, sems):
    slots = find_slots(counts, odd[0])
    copies = start_copies(
        [source.at[slots[0]], source.at[slots[2]], source.at[slots[1]]],
        [pair.at[0], pair.at[1], single],
        sems,
    )
    for copy in copies:
        copy.wait()


def leave(counts, odd, array):
    rows = array.shape[1]
    return pl.pallas_call(
        leave_kernel,
        in_specs=[SMEM, SMEM, ANY],
        out_specs=[VMEM, VMEM],
        out_shape=[shape_of((2, rows, 768), BF16), shape_of((rows, 768), BF16)],
        scratch_shapes=[pltpu.SemaphoreType.DMA((3,))],
        cost_estimate=lasting(2),
        name="leave",
    )(counts, odd.reshape(1).astype(jnp.int32), array)


class Place:
    def __init__(self):
        dp = lax.axis_index("dp")
        self.z = lax.axis_index("blk")
        self.core = dp % 2
        self.chip = dp // 2


def after(value, *others):
    return lax.optimization_barrier((value,) + others)[0]


def by_chip(keep, got):
    return [add_low(keep[4 * k : 4 * k + 4], got[4 * k : 4 * k + 4]) for k in range(4)]


def over_chips(sums):
    return [swap(sums[k], "dp", 2 * k) for k in (1, 2, 3)]


def over_line(quarter):
    return [swap(quarter[k], "blk", k) for k in (1, 2, 3)]


def gather_all(part):
    every = lax.all_gather(part, ("dp", "blk"), axis=0)
    return every.reshape((4, 2, 4) + every.shape[1:])


def local_paired(
    tokens,
    counts,
    ln1_gain,
    ln1_shift,
    w_qkv,
    bias_q,
    bias_v,
    w_out,
    bias_out,
    ln2_gain,
    ln2_shift,
    w_fc1,
    bias_fc1,
    w_fc2,
    bias_fc2,
    cotangent,
):
    place = Place()
    odd = place.z % 2
    slots = find_slots(counts, odd)

    def arrange(pieces):
        (one, three), two = pieces
        return jnp.stack(
            [
                jnp.where(slots[0] == i, one, jnp.where(slots[1] == i, two, three))
                for i in range(3)
            ]
        )

    where = jnp.stack(
        [place.core, place.chip * 4 + place.z, 2 * place.core + odd]
    ).astype(jnp.int32)

    def move(pieces):
        return tuple(
            lax.ppermute(piece, ("dp", "blk"), column_pairs(table))
            for piece, table in zip(pieces, (FIRST_TO, SECOND_TO))
        )

    def give(pieces):
        return tuple(
            None
            if piece is None
            else lax.ppermute(piece, ("dp", "blk"), [pair[::-1] for pair in column_pairs(table)])
            for piece, table in zip(pieces, (FIRST_TO, SECOND_TO))
        )

    wide = w_fc1.shape[1] // 768
    rows = tokens.shape[1]
    vectors = [ln1_gain, ln1_shift, bias_q, bias_v, bias_out, ln2_gain, ln2_shift, bias_fc2]
    vecs, b1, w_near = prepare(jnp.stack(vectors), bias_fc1.reshape(1, -1), w_qkv)
    vecs_one, vecs_two = vecs[:4], vecs[4:]
    token_sends = leave(counts, odd, tokens)
    x13, x2 = move(token_sends)
    xs = (x13, x2)
    cot_sends = leave(counts, odd, after(cotangent, *token_sends))
    x3 = after(x13[1], x2, vecs, *cot_sends)
    short_blocks = exchange_short(x3)
    q_full, kv_full = project(x13, after(x2, x3), vecs_one, w_near)
    kv_other = swap(kv_full, "dp", 1)
    cots = move(after(cot_sends, x3))
    seq = 2 * kv_full.shape[1]
    kv_both = [kv_full, kv_other]
    att_full, t_full = attend(q_full, kv_both, seq, 768, 384)
    spare = -(-(SHORT - 2 * rows) // LANES) * LANES
    q_short, kv_head, kv_tail = project_short(
        where, x13, *after(short_blocks, att_full), vecs_one, w_near, spare
    )
    kv_short = [kv_head, kv_tail]
    att_short, t_short = attend(q_short, kv_short, SHORT, 384, 384)
    cots = after(cots, att_short)
    o13, o2, mid, normed_two, hidden_low, send_a, keep_a, gb1 = feed(
        where, att_full, att_short, xs, cots, w_out, vecs_two, w_fc1, b1, w_fc2
    )
    got_a = swap(send_a, "dp", 1)
    home_one = give((o13, o2))
    sums_a = by_chip(keep_a, got_a)
    chips_a = over_chips(sums_a)
    back_att, back_mid, send_b, keep_b, feed_sums = feed_back(
        where, att_full, att_short, cots, w_out, vecs_two, after(mid, *sums_a), normed_two,
        hidden_low, w_fc1,
    )
    home = (after(home_one[0], back_mid), home_one[1])
    quarter_a = add_low(after(sums_a[0], back_mid, home[0]), *chips_a)
    line_a = over_line(quarter_a)
    got_b = swap(after(send_b, quarter_a), "dp", 1)

    n_full = q_full.shape[0]
    dq_short, keep_short, send_pair = attend_back(
        where, after(q_short, quarter_a), back_att, n_full, att_short, t_short, kv_short, SHORT,
        768, 0, 6, True,
    )
    home = (home[0], after(home[1], dq_short))
    part_a = add_low(after(quarter_a[0], dq_short, home[1]), *line_a)
    all_a = gather_all(part_a)
    got_pair = swap(after(send_pair, part_a), "dp", 1)
    sums_b = by_chip(after(keep_b, dq_short, part_a), got_b)
    chips_b = over_chips(sums_b)
    away = (1 - odd) * rows
    send_short = add_low(
        lax.dynamic_slice_in_dim(keep_short, away, rows, 1),
        lax.dynamic_slice_in_dim(after(got_pair, *sums_b), away, rows, 1),
    )
    got_near = swap(send_short, "blk", 1)
    dq_full, own_full, sent_full = attend_back(
        where, after(q_full, send_short), back_att, 0, att_full, t_full, kv_both, seq, 768, 0, 6
    )
    got_near = after(got_near, dq_full)
    quarter_b = add_low(after(sums_b[0], dq_full, got_near), *chips_b)
    got_full = swap(after(sent_full, quarter_b), "dp", 1)
    line_b = over_line(quarter_b)
    send_c, keep_c, back = project_back(
        where, xs, vecs_one, dq_full, dq_short, own_full, got_full, keep_short, got_pair, got_near
    )
    part_b = add_low(after(quarter_b[0], keep_c), *line_b)
    got_c = swap(after(send_c, part_b), "dp", 1)
    near_b = over_line([part_b] * 4)
    i13, i2, line_sums = input_back(
        where, xs, vecs_one, w_qkv, back_mid, after(back, part_b), feed_sums, gb1
    )
    near_b = jnp.stack([after(part_b, i2)] + near_b)
    half_b = lax.all_gather(near_b, "dp", axis=0, axis_index_groups=CHIPS)
    sums_c = [
        jnp.concatenate([total, line_sums[4 * k : 4 * k + 4]], axis=1)
        for k, total in enumerate(by_chip(after(keep_c, i2, near_b), got_c))
    ]
    chips_c = over_chips(sums_c)
    (i13_home,) = give((i13, None))[:1]
    output = arrange(after(home, *sums_c))
    all_a = after(all_a, *sums_c)
    halves_a = [all_a[:, c] for c in range(2)]
    grad_w_fc2 = finish(jnp.zeros((3,), jnp.int32), *halves_a, 0, wide, False)
    i13_home = after(i13_home, grad_w_fc2, output)
    quarter_c = add_low(after(sums_c[0], i13_home), *chips_c)
    line_c = over_line(quarter_c)
    part_c = add_low(quarter_c[0], *line_c)
    near_c = jnp.stack([part_c] + over_line([part_c] * 4))
    far_c = over_chips([near_c] * 4)
    i2_home = give((None, after(i2, near_c)))[1]
    half_b = after(half_b, near_c)
    other_b = swap(half_b, "dp", 1)
    inside = where * jnp.array([1, 0, 0], jnp.int32) + jnp.array([0, 1, 0], jnp.int32) * place.z
    grad_w_fc1 = finish(inside, half_b, other_b, 0, wide, True)
    grad_w_out = finish(inside, half_b, other_b, wide, 1, True)
    i2_home = after(i2_home, grad_w_fc1, grad_w_out)
    whole_c = jnp.stack([after(near_c, i2_home)] + far_c)
    other_c = swap(whole_c, "dp", 1)
    input_grad = arrange(after((i13_home, i2_home), whole_c)).astype(F32)
    grad_w_qkv, *lines = finish(where, whole_c, other_c, 0, 3, True, True)
    return (
        output,
        input_grad,
        lines[4],
        lines[5],
        grad_w_qkv,
        lines[6],
        lines[7],
        grad_w_out,
        lines[0],
        lines[1],
        lines[2],
        grad_w_fc1,
        lines[8],
        grad_w_fc2,
        lines[3],
    )


def solution(mesh):
    paired = mesh.shape["dp"] == 8 and mesh.shape["blk"] == 4
    chosen = local_paired if paired else local
    return jax.shard_map(
        chosen,
        mesh=mesh,
        in_specs=(
            P("dp", "blk", None),
            P("dp"),
            P(),
            P(),
            P(),
            P(),
            P(),
            P(),
            P(),
            P(),
            P(),
            P(),
            P(),
            P(),
            P(),
            P("dp", "blk", None),
        ),
        out_specs=(
            P("dp", "blk", None),
            P("dp", "blk", None),
            P(),
            P(),
            P(),
            P(),
            P(),
            P(),
            P(),
            P(),
            P(),
            P(),
            P(),
            P(),
            P(),
        ),
        check_vma=False,
    )
```

```python
import functools
import math

import jax
import jax.numpy as jnp
from jax import lax
from jax.experimental import pallas as pl
from jax.experimental.pallas import tpu as pltpu
from jax.sharding import PartitionSpec as P

HEADS = 12
HD = 64
SHORT = 864


NORM_EPS = 1e-06
MASK_LOW = -1e30


def norm_rows(values, gain, shift):
    centre = values - jnp.mean(values, axis=-1, keepdims=True)
    spread = jnp.mean(centre * centre, axis=-1, keepdims=True)
    return centre * lax.rsqrt(spread + NORM_EPS) * gain + shift


def gelu_exact(values):
    return jax.nn.gelu(values, approximate=False)


def cube_valid(counts, offset, length):
    places = offset + jnp.arange(length, dtype=jnp.int32)
    return places[None, :] < counts[:, None]


def total_every(parts):
    split = (
        lax.psum_scatter(
            parts[0].astype(jnp.bfloat16), "blk", scatter_dimension=0, tiled=True
        ).astype(jnp.float32),
        lax.psum_scatter(
            parts[1].astype(jnp.bfloat16), "blk", scatter_dimension=0, tiled=True
        ).astype(jnp.float32),
        lax.psum_scatter(
            parts[2].astype(jnp.bfloat16), "blk", scatter_dimension=0, tiled=True
        ).astype(jnp.float32),
        lax.psum_scatter(
            parts[3].astype(jnp.bfloat16), "blk", scatter_dimension=0, tiled=True
        ).astype(jnp.float32),
        lax.psum_scatter(
            parts[4].astype(jnp.bfloat16), "blk", scatter_dimension=0, tiled=True
        ).astype(jnp.float32),
        lax.psum_scatter(
            parts[5].astype(jnp.bfloat16), "blk", scatter_dimension=0, tiled=True
        ).astype(jnp.float32),
        lax.psum_scatter(
            parts[6].astype(jnp.bfloat16), "blk", scatter_dimension=0, tiled=True
        ).astype(jnp.float32),
        lax.psum_scatter(
            parts[7].astype(jnp.bfloat16), "blk", scatter_dimension=0, tiled=True
        ).astype(jnp.float32),
        lax.psum_scatter(
            parts[8].astype(jnp.bfloat16), "blk", scatter_dimension=0, tiled=True
        ).astype(jnp.float32),
        lax.psum_scatter(
            parts[9].astype(jnp.bfloat16), "blk", scatter_dimension=0, tiled=True
        ).astype(jnp.float32),
        lax.psum_scatter(
            parts[10].astype(jnp.bfloat16), "blk", scatter_dimension=0, tiled=True
        ).astype(jnp.float32),
        lax.psum_scatter(
            parts[11].astype(jnp.bfloat16), "blk", scatter_dimension=0, tiled=True
        ).astype(jnp.float32),
        lax.psum_scatter(
            parts[12].astype(jnp.bfloat16), "blk", scatter_dimension=0, tiled=True
        ).astype(jnp.float32),
    )
    summed = (
        lax.psum(split[0].astype(jnp.bfloat16), "dp").astype(jnp.float32),
        lax.psum(split[1].astype(jnp.bfloat16), "dp").astype(jnp.float32),
        lax.psum(split[2].astype(jnp.bfloat16), "dp").astype(jnp.float32),
        lax.psum(split[3].astype(jnp.bfloat16), "dp").astype(jnp.float32),
        lax.psum(split[4].astype(jnp.bfloat16), "dp").astype(jnp.float32),
        lax.psum(split[5].astype(jnp.bfloat16), "dp").astype(jnp.float32),
        lax.psum(split[6].astype(jnp.bfloat16), "dp").astype(jnp.float32),
        lax.psum(split[7].astype(jnp.bfloat16), "dp").astype(jnp.float32),
        lax.psum(split[8].astype(jnp.bfloat16), "dp").astype(jnp.float32),
        lax.psum(split[9].astype(jnp.bfloat16), "dp").astype(jnp.float32),
        lax.psum(split[10].astype(jnp.bfloat16), "dp").astype(jnp.float32),
        lax.psum(split[11].astype(jnp.bfloat16), "dp").astype(jnp.float32),
        lax.psum(split[12].astype(jnp.bfloat16), "dp").astype(jnp.float32),
    )
    return (
        lax.all_gather(summed[0].astype(jnp.bfloat16), "blk", axis=0, tiled=True).astype(
            jnp.float32
        ),
        lax.all_gather(summed[1].astype(jnp.bfloat16), "blk", axis=0, tiled=True).astype(
            jnp.float32
        ),
        lax.all_gather(summed[2].astype(jnp.bfloat16), "blk", axis=0, tiled=True).astype(
            jnp.float32
        ),
        lax.all_gather(summed[3].astype(jnp.bfloat16), "blk", axis=0, tiled=True).astype(
            jnp.float32
        ),
        lax.all_gather(summed[4].astype(jnp.bfloat16), "blk", axis=0, tiled=True).astype(
            jnp.float32
        ),
        lax.all_gather(summed[5].astype(jnp.bfloat16), "blk", axis=0, tiled=True).astype(
            jnp.float32
        ),
        lax.all_gather(summed[6].astype(jnp.bfloat16), "blk", axis=0, tiled=True).astype(
            jnp.float32
        ),
        lax.all_gather(summed[7].astype(jnp.bfloat16), "blk", axis=0, tiled=True).astype(
            jnp.float32
        ),
        lax.all_gather(summed[8].astype(jnp.bfloat16), "blk", axis=0, tiled=True).astype(
            jnp.float32
        ),
        lax.all_gather(summed[9].astype(jnp.bfloat16), "blk", axis=0, tiled=True).astype(
            jnp.float32
        ),
        lax.all_gather(summed[10].astype(jnp.bfloat16), "blk", axis=0, tiled=True).astype(
            jnp.float32
        ),
        lax.all_gather(summed[11].astype(jnp.bfloat16), "blk", axis=0, tiled=True).astype(
            jnp.float32
        ),
        lax.all_gather(summed[12].astype(jnp.bfloat16), "blk", axis=0, tiled=True).astype(
            jnp.float32
        ),
    )


def local(
    tokens,
    counts,
    ln1_gain,
    ln1_shift,
    w_qkv,
    bias_q,
    bias_v,
    w_out,
    bias_out,
    ln2_gain,
    ln2_shift,
    w_fc1,
    bias_fc1,
    w_fc2,
    bias_fc2,
    cotangent,
):
    cube_count, row_count, width = tokens.shape
    head_count = HEADS
    depth = HD
    score_scale = HD ** (-0.5)
    inputs = tokens.astype(jnp.float32)
    gain_one = ln1_gain.astype(jnp.float32)
    shift_one = ln1_shift.astype(jnp.float32)
    gain_two = ln2_gain.astype(jnp.float32)
    shift_two = ln2_shift.astype(jnp.float32)
    normed = norm_rows(inputs, gain_one, shift_one).astype(jnp.bfloat16)
    project = jnp.dot(normed, w_qkv, preferred_element_type=jnp.float32)
    queries = (project[..., :width] + bias_q.astype(jnp.float32)).astype(jnp.bfloat16)
    key_local = project[..., width : 2 * width].astype(jnp.bfloat16)
    value_local = (project[..., 2 * width :] + bias_v.astype(jnp.float32)).astype(jnp.bfloat16)
    key_all, value_all = (
        lax.all_gather(key_local, "blk", axis=1, tiled=True),
        lax.all_gather(value_local, "blk", axis=1, tiled=True),
    )
    seq_rows = key_all.shape[1]
    block_rows = math.gcd(seq_rows, 512)
    block_count = seq_rows // block_rows
    block_steps = jnp.arange(block_count, dtype=jnp.int32)
    query_heads = queries.reshape(cube_count, row_count, head_count, depth)

    def key_slices(offset):
        key_part = lax.dynamic_slice_in_dim(key_all, offset, block_rows, 1).reshape(
            cube_count, block_rows, head_count, depth
        )
        value_part = lax.dynamic_slice_in_dim(value_all, offset, block_rows, 1).reshape(
            cube_count, block_rows, head_count, depth
        )
        usable = cube_valid(counts, offset, block_rows)[:, None, None, :]
        return (key_part, value_part, usable)

    def forward_block(carry, step_index):
        row_top, row_total, accum = carry
        key_part, value_part, usable = key_slices(step_index * block_rows)
        scores = (
            jnp.einsum("cqhd,ckhd->chqk", query_heads, key_part, preferred_element_type=jnp.float32)
            * score_scale
        )
        masked = jnp.where(usable, scores, MASK_LOW)
        new_top = jnp.maximum(row_top, jnp.max(masked, axis=-1))
        factor = jnp.exp(row_top - new_top)
        weights = jnp.where(usable, jnp.exp(masked - new_top[..., None]), 0.0)
        row_total = row_total * factor + jnp.sum(weights, axis=-1)
        accum = accum * jnp.transpose(factor, (0, 2, 1))[..., None] + jnp.einsum(
            "chqk,ckhd->cqhd",
            weights.astype(jnp.bfloat16),
            value_part,
            preferred_element_type=jnp.float32,
        )
        return ((new_top, row_total, accum), None)

    start_carry = (
        jnp.full((cube_count, head_count, row_count), MASK_LOW, jnp.float32),
        jnp.zeros((cube_count, head_count, row_count), jnp.float32),
        jnp.zeros((cube_count, row_count, head_count, depth), jnp.float32),
    )
    (row_top, row_total, accum), _ = lax.scan(forward_block, start_carry, block_steps)
    attended_f = (accum / jnp.transpose(row_total, (0, 2, 1))[..., None]).reshape(
        cube_count, row_count, width
    )
    log_total = row_top + jnp.log(row_total)
    attended = attended_f.astype(jnp.bfloat16)
    middle = (
        inputs
        + jnp.dot(attended, w_out, preferred_element_type=jnp.float32)
        + bias_out.astype(jnp.float32)
    )
    normed_two = norm_rows(middle, gain_two, shift_two).astype(jnp.bfloat16)
    hidden = jnp.dot(normed_two, w_fc1, preferred_element_type=jnp.float32) + bias_fc1.astype(
        jnp.float32
    )
    active = gelu_exact(hidden).astype(jnp.bfloat16)
    output = (
        middle
        + jnp.dot(active, w_fc2, preferred_element_type=jnp.float32)
        + bias_fc2.astype(jnp.float32)
    ).astype(jnp.bfloat16)
    grad_bias_fc2 = jnp.sum(cotangent.astype(jnp.float32), axis=(0, 1))
    grad_w_fc2 = jnp.einsum("ctf,ctd->fd", active, cotangent, preferred_element_type=jnp.float32)
    back_active = jnp.einsum("ctd,fd->ctf", cotangent, w_fc2, preferred_element_type=jnp.float32)
    _, gelu_pull = jax.vjp(gelu_exact, hidden)
    back_hidden = gelu_pull(back_active)[0]
    grad_bias_fc1 = jnp.sum(back_hidden, axis=(0, 1))
    hidden_low = back_hidden.astype(jnp.bfloat16)
    grad_w_fc1 = jnp.einsum(
        "ctd,ctf->df", normed_two, hidden_low, preferred_element_type=jnp.float32
    )
    back_normed_two = jnp.einsum(
        "ctf,df->ctd", hidden_low, w_fc1, preferred_element_type=jnp.float32
    )
    _, norm_pull_two = jax.vjp(norm_rows, middle, gain_two, shift_two)
    back_middle_norm, grad_ln2_gain, grad_ln2_shift = norm_pull_two(back_normed_two)
    back_middle = cotangent.astype(jnp.float32) + back_middle_norm
    mlp_grads = (
        grad_ln2_gain,
        grad_ln2_shift,
        grad_w_fc1,
        grad_bias_fc1,
        grad_w_fc2,
        grad_bias_fc2,
    )
    grad_bias_out = jnp.sum(back_middle, axis=(0, 1))
    middle_low = back_middle.astype(jnp.bfloat16)
    grad_w_out = jnp.einsum("ctd,cte->de", attended, middle_low, preferred_element_type=jnp.float32)
    back_attended = jnp.einsum(
        "cte,de->ctd", middle_low, w_out, preferred_element_type=jnp.float32
    ).astype(jnp.bfloat16)
    back_heads = back_attended.reshape(cube_count, row_count, head_count, depth)
    delta = jnp.transpose(
        jnp.sum(
            (back_attended.astype(jnp.float32) * attended_f).reshape(
                cube_count, row_count, head_count, depth
            ),
            axis=-1,
        ),
        (0, 2, 1),
    )

    def block_grads(key_part, value_part, usable):
        scores = (
            jnp.einsum("cqhd,ckhd->chqk", query_heads, key_part, preferred_element_type=jnp.float32)
            * score_scale
        )
        probs = jnp.where(usable, jnp.exp(scores - log_total[..., None]), 0.0)
        back_probs = jnp.einsum(
            "cqhd,ckhd->chqk", back_heads, value_part, preferred_element_type=jnp.float32
        )
        back_scores = (probs * (back_probs - delta[..., None])).astype(jnp.bfloat16)
        return (probs, back_scores)

    query_zero = jnp.zeros((cube_count, row_count, head_count, depth), jnp.float32)

    def back_block(carry, step_index):
        back_query, key_grads, value_grads = carry
        offset = step_index * block_rows
        key_part, value_part, usable = key_slices(offset)
        probs, back_scores = block_grads(key_part, value_part, usable)
        back_query = (
            back_query
            + jnp.einsum(
                "chqk,ckhd->cqhd", back_scores, key_part, preferred_element_type=jnp.float32
            )
            * score_scale
        )
        key_block = (
            jnp.einsum(
                "chqk,cqhd->ckhd", back_scores, query_heads, preferred_element_type=jnp.float32
            )
            * score_scale
        )
        value_block = jnp.einsum(
            "chqk,cqhd->ckhd",
            probs.astype(jnp.bfloat16),
            back_heads,
            preferred_element_type=jnp.float32,
        )
        key_grads = lax.dynamic_update_slice_in_dim(
            key_grads, key_block.reshape(cube_count, block_rows, width), offset, 1
        )
        value_grads = lax.dynamic_update_slice_in_dim(
            value_grads, value_block.reshape(cube_count, block_rows, width), offset, 1
        )
        return ((back_query, key_grads, value_grads), None)

    full_zero = jnp.zeros((cube_count, seq_rows, width), jnp.float32)
    (back_query, key_grads, value_grads), _ = lax.scan(
        back_block, (query_zero, full_zero, full_zero), block_steps
    )
    key_back, value_back = (
        lax.psum_scatter(
            key_grads.astype(jnp.bfloat16), "blk", scatter_dimension=1, tiled=True
        ).astype(jnp.float32),
        lax.psum_scatter(
            value_grads.astype(jnp.bfloat16), "blk", scatter_dimension=1, tiled=True
        ).astype(jnp.float32),
    )
    query_low = back_query.reshape(cube_count, row_count, width).astype(jnp.bfloat16)
    key_low = key_back.astype(jnp.bfloat16)
    value_low = value_back.astype(jnp.bfloat16)
    grad_bias_q = jnp.sum(query_low.astype(jnp.float32), axis=(0, 1))
    grad_bias_v = jnp.sum(value_low.astype(jnp.float32), axis=(0, 1))
    back_project = jnp.concatenate([query_low, key_low, value_low], axis=-1)
    grad_w_qkv = jnp.einsum("ctd,cte->de", normed, back_project, preferred_element_type=jnp.float32)
    back_normed = jnp.einsum("cte,de->ctd", back_project, w_qkv, preferred_element_type=jnp.float32)
    _, norm_pull_one = jax.vjp(norm_rows, inputs, gain_one, shift_one)
    back_inputs, grad_ln1_gain, grad_ln1_shift = norm_pull_one(back_normed)
    input_grad = back_middle + back_inputs
    attn_grads = (
        grad_ln1_gain,
        grad_ln1_shift,
        grad_w_qkv,
        grad_bias_q,
        grad_bias_v,
        grad_w_out,
        grad_bias_out,
    )
    every_grad = total_every(attn_grads + mlp_grads)
    attn_grads = every_grad[:7]
    mlp_grads = every_grad[7:]
    return (
        output,
        input_grad,
        attn_grads[0],
        attn_grads[1],
        attn_grads[2],
        attn_grads[3],
        attn_grads[4],
        attn_grads[5],
        attn_grads[6],
        mlp_grads[0],
        mlp_grads[1],
        mlp_grads[2],
        mlp_grads[3],
        mlp_grads[4],
        mlp_grads[5],
    )


F32 = jnp.float32
BF16 = jnp.bfloat16
EXP_SCALE = math.log2(math.e) / 8
LANES = 128
CUT = 256
VMEM = pl.BlockSpec(memory_space=pltpu.VMEM)
SMEM = pl.BlockSpec(memory_space=pltpu.SMEM)
ANY = pl.BlockSpec(memory_space=pl.ANY)


def lasting(micros):
    return pl.CostEstimate(flops=micros * 10**9, bytes_accessed=2**20, transcendentals=0)


def shape_of(shape, dtype):
    return jax.ShapeDtypeStruct(shape, dtype)


def limits(mib):
    return pltpu.CompilerParams(vmem_limit_bytes=mib * 2**20)


def dot_nt(a, b):
    return lax.dot_general(a, b, (((1,), (1,)), ((), ())), preferred_element_type=F32)


def dot_nn(a, b):
    return lax.dot_general(a, b, (((1,), (0,)), ((), ())), preferred_element_type=F32)


def dot_tn(a, b):
    return lax.dot_general(a, b, (((0,), (0,)), ((), ())), preferred_element_type=F32)


def centred(values):
    centre = values - jnp.mean(values, axis=1, keepdims=True)
    spread = jnp.mean(centre * centre, axis=1, keepdims=True)
    return centre, lax.rsqrt(spread + NORM_EPS)


def norm_back(centre, recip, back, gain):
    unit = centre * recip
    grad = back * gain
    inner = jnp.mean(grad * unit, axis=1, keepdims=True)
    return unit, recip * (grad - jnp.mean(grad, axis=1, keepdims=True) - unit * inner)


def prepare_kernel(a, b, w, out_a, out_b, out_w):
    out_a[...] = a[...].astype(F32)
    out_b[...] = b[...].astype(F32)
    out_w[...] = w[...]


def prepare(a, b, w):
    return pl.pallas_call(
        prepare_kernel,
        in_specs=[VMEM] * 3,
        out_specs=[VMEM] * 3,
        out_shape=[shape_of(a.shape, F32), shape_of(b.shape, F32), shape_of(w.shape, w.dtype)],
        compiler_params=limits(16),
        cost_estimate=lasting(2),
        name="prepare",
    )(a, b, w)


def project_rows(x, vecs, w, q_ref, kv_ref, at, q_at=None):
    gain, shift, bias_q, bias_v = (vecs[i : i + 1, :] for i in range(4))
    centre, recip = centred(x.astype(F32))
    normed = (centre * recip * gain + shift).astype(BF16)
    kv_ref[0, at, :] = dot_nn(normed, w[:, 768:1536]).astype(BF16)
    kv_ref[1, at, :] = (dot_nn(normed, w[:, 1536:]) + bias_v).astype(BF16)
    if q_at is not None:
        q_ref[q_at, :] = (dot_nn(normed, w[:, :768]) + bias_q).astype(BF16)


def project_kernel(x13_in, x2_in, vecs, w_in, q_ref, kv_ref, held, w, sems):
    copies = start_copies([x13_in.at[0], x2_in, w_in], [held.at[0], held.at[1], w], sems)
    for copy in copies:
        copy.wait()
    rows = held.shape[1]
    for i in range(2):
        at = pl.ds(i * rows, rows)
        project_rows(held[i], vecs, w, q_ref, kv_ref, at, at)


def project(x13, x2, vecs, w):
    n = 2 * x2.shape[0]
    return pl.pallas_call(
        project_kernel,
        in_specs=[ANY, ANY, VMEM, ANY],
        out_specs=[VMEM] * 2,
        out_shape=[shape_of((n, 768), BF16), shape_of((2, n, 768), BF16)],
        scratch_shapes=[
            pltpu.VMEM((2,) + x2.shape, BF16),
            pltpu.VMEM(w.shape, w.dtype),
            pltpu.SemaphoreType.DMA((3,)),
        ],
        compiler_params=limits(24),
        cost_estimate=lasting(4),
        name="project",
    )(x13, x2, vecs, w)


def project_short_kernel(
    where, x13, near, other, far, vecs, w_in, q_ref, head_ref, tail_ref, w, held, sems, *, spare
):
    (copy,) = start_copies([w_in], [w], sems)
    rows = near.shape[0]
    mine = where[2]
    for k, block in enumerate((x13[1], near[...], other[...], far[...])):
        held[k ^ mine] = block
    copy.wait()
    for i in range(2):
        project_rows(held[i], vecs, w, None, head_ref, pl.ds(i * rows, rows))
    project_rows(held[2][:spare], vecs, w, None, tail_ref, pl.ds(0, spare))
    centre, recip = centred(x13[1].astype(F32))
    normed = (centre * recip * vecs[0:1, :] + vecs[1:2, :]).astype(BF16)
    q_ref[...] = (dot_nn(normed, w[:, :768]) + vecs[2:3, :]).astype(BF16)


def project_short(where, x13, near, other, far, vecs, w, spare):
    rows = near.shape[0]
    return pl.pallas_call(
        functools.partial(project_short_kernel, spare=spare),
        in_specs=[SMEM] + [VMEM] * 5 + [ANY],
        out_specs=[VMEM] * 3,
        out_shape=[
            shape_of((rows, 768), BF16),
            shape_of((2, 2 * rows, 768), BF16),
            shape_of((2, spare, 768), BF16),
        ],
        scratch_shapes=[
            pltpu.VMEM(w.shape, w.dtype),
            pltpu.VMEM((4, rows, 768), BF16),
            pltpu.SemaphoreType.DMA((1,)),
        ],
        compiler_params=limits(24),
        cost_estimate=lasting(4),
        name="project_short",
    )(where, x13, near, other, far, vecs, w)


def start_copies(sources, targets, sems):
    copies = [
        pltpu.make_async_copy(source, target, sems.at[i])
        for i, (source, target) in enumerate(zip(sources, targets))
    ]
    for copy in copies:
        copy.start()
    return copies


def three_parts(values, lane):
    high = values.astype(BF16)
    rest = values - high.astype(F32)
    middle = rest.astype(BF16)
    least = (rest - middle.astype(F32)).astype(BF16)
    zero = jnp.zeros((), BF16)
    return jnp.where(
        lane == 0, high, jnp.where(lane == 1, middle, jnp.where(lane == 2, least, zero))
    )


def lane_index(rows=1):
    return lax.broadcasted_iota(jnp.int32, (rows, LANES), 1)


def attend_kernel(*refs, pieces, valid, step):
    q_ref = refs[0]
    kvs = refs[1 : 1 + pieces]
    o_ref, t_ref = refs[1 + pieces :]
    lane = lane_index()
    low = lane < 64
    half = lane % 64
    total = sum(kv.shape[1] for kv in kvs)
    keys, values = [], []
    for h in range(2):
        own = low if h == 0 else ~low
        key_parts, value_parts, at = [], [], 0
        for kv in kvs:
            n = kv.shape[1]
            beside = jnp.zeros((n, LANES), BF16)
            if at + n > valid:
                place = lax.broadcasted_iota(jnp.int32, (n, LANES), 0) + at
                beside = jnp.where(
                    (place >= valid) & (lane_index(n) % 64 == 0), MASK_LOW, 0.0
                ).astype(BF16)
            key_parts.append(jnp.where(own, kv[0], beside))
            value_parts.append(jnp.where(own, kv[1], jnp.ones((), BF16)))
            at += n
        keys.append(key_parts)
        values.append(value_parts)
    cuts = [
        (i, first, min(CUT, kv.shape[1] - first))
        for i, kv in enumerate(kvs)
        for first in range(0, kv.shape[1], CUT)
    ]
    for s in range(q_ref.shape[0] // step):
        at = pl.ds(s * step, step)
        q = q_ref[at, :]
        sums, tops = [], []
        for h in range(2):
            own = low if h == 0 else ~low
            q_own = q
            if total > valid:
                q_own = jnp.where(own, q, jnp.where(half == 0, 1.0, 0.0).astype(BF16))
            top, kept = None, None
            for i, first, size in cuts:
                scores = dot_nt(q_own, keys[h][i][first : first + size]) * EXP_SCALE
                new_top = jnp.max(scores, axis=1, keepdims=True)
                if top is not None:
                    new_top = jnp.maximum(top, new_top)
                weights = jnp.exp2(scores - new_top).astype(BF16)
                part = dot_nn(weights, values[h][i][first : first + size])
                kept = part if top is None else kept * jnp.exp2(top - new_top) + part
                top = new_top
            sums.append(kept)
            tops.append(top)
        above = jnp.where(low, sums[0], sums[1])
        below = jnp.where(low, sums[1], sums[0])
        o_ref[at, :] = above / pltpu.roll(below, 64, 1)
        top = jnp.where(low, tops[1], tops[0]) * (1.0 / EXP_SCALE)
        t_ref[at, :] = jnp.where(
            half == 3, jnp.ones((), BF16), three_parts(-(top + 8.0 * jnp.log(below)), half)
        )


def attend(q, kvs, valid, rows, step, first=0, count=6):
    n = q.shape[0]
    keys = sum(kv.shape[1] for kv in kvs)
    block = pl.BlockSpec((rows, LANES), lambda p, i: (i, p))
    return pl.pallas_call(
        functools.partial(attend_kernel, pieces=len(kvs), valid=valid, step=step),
        out_shape=[shape_of((n, LANES * count), F32), shape_of((n, LANES * count), BF16)],
        grid=(count, n // rows),
        in_specs=[pl.BlockSpec((rows, LANES), lambda p, i: (i, first + p))]
        + [pl.BlockSpec((2, kv.shape[1], LANES), lambda p, i: (0, 0, first + p)) for kv in kvs],
        out_specs=[block, block],
        compiler_params=limits(24),
        cost_estimate=lasting(n * keys * count // 280000),
        name="attend",
    )(q, *kvs)


def attend_back_kernel(*refs, pieces, valid, step, split):
    where = refs[0]
    q_ref, do_ref, o_ref, t_ref = refs[1:5]
    kvs = refs[5 : 5 + pieces]
    dq_ref = refs[5 + pieces]
    outs = refs[6 + pieces :]
    n = q_ref.shape[0]
    lane = lane_index()
    low = lane < 64
    half = lane % 64
    q, do, t = q_ref[...], do_ref[...], t_ref[...]
    product = do.astype(F32) * o_ref[...]
    delta = [
        jnp.sum(jnp.where(low, product, 0.0), axis=1, keepdims=True),
        jnp.sum(jnp.where(low, 0.0, product), axis=1, keepdims=True),
    ]
    d = three_parts(-jnp.where(low, delta[1], delta[0]), half)
    queries = [jnp.where(low, q, t), jnp.where(low, t, q)]
    backs = [jnp.where(low, do, d), jnp.where(low, d, do)]
    ones = jnp.where(half < 3, 1.0, 0.0).astype(BF16)
    sums = [jnp.zeros((LANES, n), F32), jnp.zeros((LANES, n), F32)]
    starts = [sum(kv.shape[1] for kv in kvs[:i]) for i in range(pieces)]
    small = None
    for i in reversed(range(pieces)):
        kv = kvs[i]
        for first in range(0, kv.shape[1], step):
            size = min(step, kv.shape[1] - first)
            at = pl.ds(first, size)
            key_sums, value_sums = [], []
            for h in range(2):
                own = low if h == 0 else ~low
                beside = ones
                if starts[i] + first + size > valid:
                    place = lax.broadcasted_iota(jnp.int32, (size, LANES), 0) + (starts[i] + first)
                    wide = lane_index(size) % 64
                    beside = jnp.where(
                        wide < 3, 1.0, jnp.where((place >= valid) & (wide == 3), MASK_LOW, 0.0)
                    ).astype(BF16)
                key = jnp.where(own, kv[0, at, :], beside)
                value = jnp.where(own, kv[1, at, :], ones)
                probs = jnp.exp2(dot_nt(key, queries[h]) * EXP_SCALE)
                back_scores = (probs * dot_nt(value, backs[h])).astype(BF16)
                value_sums.append(dot_nn(probs.astype(BF16), backs[h]))
                key_sums.append(dot_nn(back_scores, queries[h]))
                sums[h] = sums[h] + dot_tn(key, back_scores)
            both = (
                (jnp.where(low, key_sums[0], key_sums[1]) * 0.125).astype(BF16),
                jnp.where(low, value_sums[0], value_sums[1]).astype(BF16),
            )
            for k in range(2):
                if not split:
                    outs[i][k, at, :] = both[k]
                elif i == 0:
                    other = jnp.zeros_like(both[k])
                    if first == 0:
                        rest = jnp.zeros((size - small[k].shape[0], LANES), BF16)
                        other = jnp.concatenate([small[k], rest], axis=0)
                    stays = where[0] == 0
                    outs[0][k, at, :] = jnp.where(stays, both[k], other)
                    outs[1][k, at, :] = jnp.where(stays, other, both[k])
            small = both
    both = jnp.concatenate([sums[0][:64], sums[1][64:]], axis=0)
    dq_ref[...] = (both.T * 0.125).astype(BF16)


def attend_back(where, q, do, first_row, o, t, kvs, valid, step, first, count, split=False):
    n = q.shape[0]
    keys = sum(kv.shape[1] for kv in kvs)
    row = first_row // n
    block = pl.BlockSpec((n, LANES), lambda p: (0, first + p))
    back_block = pl.BlockSpec((n, LANES), lambda p: (row, first + p))
    wide = [pl.BlockSpec((2, kv.shape[1], LANES), lambda p: (0, 0, first + p)) for kv in kvs]
    out = pl.BlockSpec((n, LANES), lambda p: (0, p))
    outs = [kvs[0], kvs[0]] if split else kvs
    out_wide = [pl.BlockSpec((2, kv.shape[1], LANES), lambda p: (0, 0, p)) for kv in outs]
    return pl.pallas_call(
        functools.partial(
            attend_back_kernel, pieces=len(kvs), valid=valid, step=step, split=split
        ),
        out_shape=[shape_of((n, LANES * count), BF16)]
        + [shape_of((2, kv.shape[1], LANES * count), BF16) for kv in outs],
        grid=(count,),
        in_specs=[SMEM, block, back_block, block, block] + wide,
        out_specs=[out] + out_wide,
        compiler_params=limits(56),
        cost_estimate=lasting(n * keys * count // 180000),
        name="attend_back",
    )(where, q, do, o, t, *kvs)


def fill_part(where, send, keep, j, block):
    left, right = block[:, :384], block[:, 384:]
    first = where[0] == 0
    for ref, half in (
        (keep, jnp.where(first, left, right)),
        (send, jnp.where(first, right, left)),
    ):
        for p in range(16):
            ref[p ^ where[1], pl.ds(j * 48, 48), :] = half[p * 48 : (p + 1) * 48]


def attended_rows(att_full, att_short, i, rows):
    if i == 2:
        return att_short[...].astype(BF16)
    at = pl.ds(i * rows, rows)
    return att_full[at, :].astype(BF16)


def feed_kernel(
    where, att_full_in, att_short_in, x13_in, x2_in, c13, c2, w_out_in, vecs, w1, b1, w2,
    o13, o2, mid_out, normed_out, hidden_low, send, keep, gb1,
    att_full, att_short, x13, x2, w_out, mid, normed, out_sum, cot, active, sems,
    *, steps, tile,
):
    j = pl.program_id(0)
    xs, outs = (x13.at[0], x2, x13.at[1]), (o13.at[0], o2, o13.at[1])
    rows = x2.shape[0]
    bias_out, gain, shift, b2 = (vecs[i : i + 1, :] for i in range(4))

    def at(i):
        return pl.ds(i * rows, rows)

    def leaving():
        return [
            pltpu.make_async_copy(mid, mid_out, sems.at[0]),
            pltpu.make_async_copy(normed, normed_out, sems.at[1]),
        ]

    @pl.when(j == 0)
    def _():
        copies = start_copies(
            [w_out_in, att_full_in, x13_in, x2_in, att_short_in, c13.at[0], c2, c13.at[1]],
            [w_out, att_full, x13, x2, att_short] + [cot.at[at(i), :] for i in range(3)],
            sems,
        )
        for copy in copies[:4]:
            copy.wait()
        for i in range(3):
            if i == 2:
                copies[4].wait()
            att = attended_rows(att_full, att_short, i, rows)
            m = xs[i][...].astype(F32) + dot_nn(att, w_out[...]) + bias_out
            mid[at(i), :] = m
            centre, recip = centred(m)
            normed[at(i), :] = (centre * recip * gain + shift).astype(BF16)
            out_sum[at(i), :] = m + b2
        for copy in copies[5:]:
            copy.wait()
        for copy in leaving():
            copy.start()

    w1_tile, w2_tile = w1[...], w2[...]
    bias = b1[...]
    bias_sum = jnp.zeros((1, tile), F32)
    for i in range(3):
        h = dot_nn(normed[at(i), :], w1_tile) + bias
        back_active = dot_nt(cot[at(i), :], w2_tile)
        share = 0.5 + 0.5 * lax.erf(h * math.sqrt(0.5))
        act = (h * share).astype(BF16)
        slope = share + h * (math.sqrt(0.5 / math.pi) * jnp.exp(h * h * (-0.5)))
        back_hidden = back_active * slope
        bias_sum = bias_sum + jnp.sum(back_hidden, axis=0, keepdims=True)
        active[at(i), :] = act
        hidden_low[at(i), :] = back_hidden.astype(BF16)
        out_sum[at(i), :] += dot_nn(act, w2_tile)
    gb1[...] = bias_sum
    grad = dot_tn(active[...], cot[...]).astype(BF16)
    fill_part(where, send, keep, 0, grad)

    @pl.when(j == steps - 1)
    def _():
        for copy in leaving():
            copy.wait()
        for i in range(3):
            outs[i][...] = out_sum[at(i), :].astype(BF16)


def feed(where, att_full, att_short, xs, cots, w_out, vecs, w1, b1, w2):
    rows = xs[1].shape[0]
    n = rows * 3
    wide = w1.shape[1]
    tile = 768
    steps = wide // tile
    across = pl.BlockSpec((768, tile), lambda j: (0, j))
    down = pl.BlockSpec((tile, 768), lambda j: (j, 0))
    line = pl.BlockSpec((1, tile), lambda j: (0, j))
    return pl.pallas_call(
        functools.partial(feed_kernel, steps=steps, tile=tile),
        grid=(steps,),
        in_specs=[SMEM] + [ANY] * 7 + [VMEM, across, line, down],
        out_specs=[VMEM] * 2
        + [ANY] * 2
        + [pl.BlockSpec((n, tile), lambda j: (0, j))]
        + [pl.BlockSpec((16, 48, 384), lambda j: (0, j, 0))] * 2
        + [line],
        out_shape=[shape_of((2, rows, 768), BF16), shape_of((rows, 768), BF16)]
        + [
            shape_of((n, 768), F32),
            shape_of((n, 768), BF16),
            shape_of((n, wide), BF16),
            shape_of((16, 48 * steps, 384), BF16),
            shape_of((16, 48 * steps, 384), BF16),
            shape_of((1, wide), F32),
        ],
        scratch_shapes=[
            pltpu.VMEM(v.shape, v.dtype) for v in (att_full, att_short, *xs, w_out)
        ]
        + [
            pltpu.VMEM((n, 768), F32),
            pltpu.VMEM((n, 768), BF16),
            pltpu.VMEM((n, 768), F32),
            pltpu.VMEM((n, 768), BF16),
            pltpu.VMEM((n, tile), BF16),
            pltpu.SemaphoreType.DMA((8,)),
        ],
        compiler_params=limits(40),
        cost_estimate=lasting(36),
        name="feed",
    )(where, att_full, att_short, *xs, *cots, w_out, vecs, w1, b1, w2)


def feed_back_kernel(
    where, att_full_in, att_short_in, c13_in, c2_in, w_out, vecs, mid_in, normed,
    hidden_low, w1,
    back_att, back_mid, send, keep, sums,
    back_sum, flipped, low_mid, att, att_full, att_short, c13, c2, mid, sems,
    *, steps,
):
    j = pl.program_id(0)
    late = (att_full, att_short, c13, c2, mid)
    sources = (att_full_in, att_short_in, c13_in, c2_in, mid_in)
    cots = (c13.at[0], c2, c13.at[1])
    rows = c2.shape[0]
    gain = vecs[1:2, :]

    def at(i):
        return pl.ds(i * rows, rows)

    @pl.when(j == 0)
    def _():
        start_copies(sources, late, sems)
        flipped[...] = normed[...].T
        for i in range(3):
            back_sum[at(i), :] = jnp.zeros((rows, 768), F32)

    @pl.when(j < steps)
    def _():
        for i in range(3):
            back_sum[at(i), :] += dot_nt(hidden_low[at(i), :], w1[...])
        fill_part(where, send, keep, 0, dot_nn(flipped[...], hidden_low[...]).astype(BF16))

    @pl.when(j == steps)
    def _():
        for i in range(len(late)):
            pltpu.make_async_copy(sources[i], late[i], sems.at[i]).wait()
        zero = jnp.zeros((1, 768), F32)
        grad_out, grad_gain, grad_shift, grad_b2 = zero, zero, zero, zero
        for i in range(3):
            centre, recip = centred(mid[at(i), :])
            back = back_sum[at(i), :]
            unit, through = norm_back(centre, recip, back, gain)
            c = cots[i][...].astype(F32)
            m = c + through
            grad_gain = grad_gain + jnp.sum(back * unit, axis=0, keepdims=True)
            grad_shift = grad_shift + jnp.sum(back, axis=0, keepdims=True)
            grad_out = grad_out + jnp.sum(m, axis=0, keepdims=True)
            grad_b2 = grad_b2 + jnp.sum(c, axis=0, keepdims=True)
            back_mid[at(i), :] = m
            low = m.astype(BF16)
            low_mid[at(i), :] = low
            back_att[at(i), :] = dot_nt(low, w_out[...]).astype(BF16)
            att[at(i), :] = attended_rows(att_full, att_short, i, rows)
        fill_part(where, send, keep, 0, dot_tn(att[...], low_mid[...]).astype(BF16))
        sums[...] = jnp.concatenate(
            [grad_out, grad_gain, grad_shift, grad_b2, zero, zero, zero, zero], axis=0
        )


def feed_back(where, att_full, att_short, cots, w_out, vecs, mid, normed, hidden_low, w1):
    rows = cots[1].shape[0]
    n = rows * 3
    wide = w1.shape[1]
    tile = 768
    steps = wide // tile
    part = pl.BlockSpec((16, 48, 384), lambda j: (0, j, 0))
    return pl.pallas_call(
        functools.partial(feed_back_kernel, steps=steps),
        grid=(steps + 1,),
        in_specs=[SMEM]
        + [ANY] * 4
        + [VMEM, VMEM, ANY, VMEM]
        + [
            pl.BlockSpec((n, tile), lambda j: (0, jnp.minimum(j, steps - 1))),
            pl.BlockSpec((768, tile), lambda j: (0, jnp.minimum(j, steps - 1))),
        ],
        out_specs=[VMEM, VMEM, part, part, VMEM],
        out_shape=[
            shape_of((n, 768), BF16),
            shape_of((n, 768), F32),
            shape_of((16, 48 * (steps + 1), 384), BF16),
            shape_of((16, 48 * (steps + 1), 384), BF16),
            shape_of((8, 768), F32),
        ],
        scratch_shapes=[
            pltpu.VMEM((n, 768), F32),
            pltpu.VMEM((768, n), BF16),
            pltpu.VMEM((n, 768), BF16),
            pltpu.VMEM((n, 768), BF16),
        ]
        + [
            pltpu.VMEM(v.shape, v.dtype) for v in (att_full, att_short, *cots, mid)
        ]
        + [pltpu.SemaphoreType.DMA((5,))],
        compiler_params=limits(38),
        cost_estimate=lasting(26),
        name="feed_back",
    )(where, att_full, att_short, *cots, w_out, vecs, mid, normed, hidden_low, w1)


def project_back_kernel(
    where, x13_in, x2_in, vecs, dq_full_in, dq_short_in, own_full_in, got_full_in,
    keep_short_in, got_pair_in, got_near_in, send, keep, back_out,
    x13, x2, dq_full, dq_short, own_full, got_full, keep_short, got_pair, got_near, back, flipped,
    sems,
):
    rows = x2.shape[0]
    full = dq_full.shape[0]
    gain, shift = vecs[0:1, :], vecs[1:2, :]
    odd = where[1] % 2
    own_rows = pl.ds(pl.multiple_of(odd * rows, rows), rows)
    sources = [
        x13_in, x2_in, dq_full_in, dq_short_in, own_full_in, got_full_in,
        keep_short_in.at[:, own_rows, :], got_pair_in.at[:, own_rows, :], got_near_in,
    ]
    targets = [x13, x2, dq_full, dq_short, own_full, got_full, keep_short, got_pair, got_near]
    copies = start_copies(sources, targets, sems)
    for copy in copies[:2]:
        copy.wait()
    for i, x in enumerate((x13.at[0], x2, x13.at[1])):
        centre, recip = centred(x[...].astype(F32))
        flipped[:, pl.ds(i * rows, rows)] = (centre * recip * gain + shift).astype(BF16).T
    for copy in copies[2:4]:
        copy.wait()
    back[0, :full, :] = dq_full[...]
    back[0, full:, :] = dq_short[...]
    outs = [pltpu.make_async_copy(back.at[k], back_out.at[k], sems.at[k]) for k in range(3)]
    outs[0].start()
    fill_part(where, send, keep, 0, dot_nn(flipped[...], back[0]).astype(BF16))
    for copy in copies[4:]:
        copy.wait()
    for k in range(2):
        total = own_full[k].astype(F32) + got_full[k].astype(F32)
        back[k + 1, :full, :] = total.astype(BF16)
        total = keep_short[k].astype(F32) + got_pair[k].astype(F32) + got_near[k].astype(F32)
        back[k + 1, full:, :] = total.astype(BF16)
        outs[k + 1].start()
        fill_part(where, send, keep, k + 1, dot_nn(flipped[...], back[k + 1]).astype(BF16))
    for copy in outs:
        copy.wait()


def project_back(where, xs, vecs, *backs):
    rows = xs[1].shape[0]
    n = rows * 3
    short = (2, rows, 768)
    held = [(v.shape, v.dtype) for v in (*xs, *backs[:4])] + [(short, BF16)] * 3
    return pl.pallas_call(
        project_back_kernel,
        in_specs=[SMEM, ANY, ANY, VMEM] + [ANY] * 7,
        out_specs=[VMEM] * 2 + [ANY],
        out_shape=[shape_of((16, 144, 384), BF16)] * 2 + [shape_of((3, n, 768), BF16)],
        scratch_shapes=[pltpu.VMEM(*each) for each in held]
        + [pltpu.VMEM((3, n, 768), BF16), pltpu.VMEM((768, n), BF16)]
        + [pltpu.SemaphoreType.DMA((9,))],
        compiler_params=limits(40),
        cost_estimate=lasting(11),
        name="project_back",
    )(where, *xs, vecs, *backs)


def input_back_kernel(
    where, x13, x2, vecs, w_in, back_mid, back, sums, gb1, o13, o2, lines, total, w, sems
):
    i = pl.program_id(0)
    rows = x2.shape[0]
    gain = vecs[0:1, :]

    @pl.when(i == 0)
    def _():
        (copy,) = start_copies([w_in], [w], sems)
        total[...] = jnp.zeros(total.shape, F32)
        copy.wait()

    x = jnp.where(i == 1, x2[...], x13[0])
    centre, recip = centred(x.astype(F32))
    back_normed = dot_nt(back[0], w[:, :768])
    for k in (1, 2):
        back_normed = back_normed + dot_nt(back[k], w[:, 768 * k : 768 * (k + 1)])
    unit, through = norm_back(centre, recip, back_normed, gain)
    out = (back_mid[...] + through).astype(BF16)

    @pl.when(i == 1)
    def _():
        o2[...] = out

    @pl.when(i != 1)
    def _():
        o13[0] = out

    ones = jnp.ones((8, rows), BF16)
    total[...] += jnp.concatenate(
        [
            jnp.sum(back_normed * unit, axis=0, keepdims=True),
            jnp.sum(back_normed, axis=0, keepdims=True),
            dot_nn(ones, back[0])[0:1],
            dot_nn(ones, back[2])[0:1],
            jnp.zeros((4, 768), F32),
        ],
        axis=0,
    )

    @pl.when(i == 2)
    def _():
        each = [sums[k : k + 1, :] for k in range(4)] + [total[k : k + 1, :] for k in range(4)]
        each += [gb1[:, k * 768 : (k + 1) * 768] for k in range(gb1.shape[1] // 768)]
        for k in range(16):
            block = jnp.zeros((16, 384), F32)
            if k < len(each):
                block = jnp.concatenate(
                    [each[k][:, :384], each[k][:, 384:], block[:14]], axis=0
                )
            lines[k ^ where[1]] = block.astype(BF16)


def input_back(where, xs, vecs, w, back_mid, back, sums, gb1):
    rows = xs[1].shape[0]
    return pl.pallas_call(
        input_back_kernel,
        grid=(3,),
        in_specs=[
            SMEM,
            pl.BlockSpec((1, rows, 768), lambda i: (i // 2, 0, 0)),
            VMEM,
            VMEM,
            ANY,
            pl.BlockSpec((rows, 768), lambda i: (i, 0)),
            pl.BlockSpec((3, rows, 768), lambda i: (0, i, 0)),
            VMEM,
            VMEM,
        ],
        out_specs=[pl.BlockSpec((1, rows, 768), lambda i: (i // 2, 0, 0)), VMEM, VMEM],
        out_shape=[
            shape_of((2, rows, 768), BF16),
            shape_of((rows, 768), BF16),
            shape_of((16, 16, 384), BF16),
        ],
        scratch_shapes=[
            pltpu.VMEM((8, 768), F32),
            pltpu.VMEM(w.shape, w.dtype),
            pltpu.SemaphoreType.DMA((1,)),
        ],
        compiler_params=limits(56),
        cost_estimate=lasting(9),
        name="input_back",
    )(where, *xs, vecs, w, back_mid, back, sums, gb1)


def finish_kernel(where, mine, other, *refs, with_lines):
    if with_lines:
        mine_rows, other_rows, out, *vectors, rows = refs
    else:
        (out,) = refs
    first = where[0] == 0
    for q in range(16):
        a, b = mine[q // 4, q % 4].astype(F32), other[q // 4, q % 4].astype(F32)
        at = pl.ds(pl.multiple_of((q ^ where[1]) * 48, 48), 48)
        out[at, :384] = jnp.where(first, a, b)
        out[at, 384:] = jnp.where(first, b, a)
    if not with_lines:
        return

    @pl.when(pl.program_id(0) == 0)
    def _():
        for q in range(16):
            both = mine_rows[q // 4, q % 4].astype(F32) + other_rows[q // 4, q % 4].astype(F32)
            rows[pl.ds(q ^ where[1], 1), :] = jnp.concatenate([both[0:1], both[1:2]], axis=1)
        for k in range(len(vectors) - 1):
            vectors[k][...] = rows[k, :]
        size = rows.shape[1]
        for k in range(vectors[-1].shape[0] // size):
            vectors[-1][pl.ds(k * size, size)] = rows[len(vectors) - 1 + k, :]


def finish(where, mine, other, start, count, across, with_lines=False):
    block = pl.BlockSpec((4, 4, 48, 384), lambda j: (0, 0, start + j, 0))
    spare = pl.BlockSpec((4, 4, 16, 384), lambda j: (0, 0, 3 * count, 0))
    shape = (768, 768 * count) if across else (768 * count, 768)
    result = [shape_of(shape, F32)]
    specs = [pl.BlockSpec((768, 768), (lambda j: (0, j)) if across else (lambda j: (j, 0)))]
    scratch = []
    if with_lines:
        result += [shape_of((768,), F32)] * 8 + [shape_of((3072,), F32)]
        specs += [VMEM] * 9
        scratch = [pltpu.VMEM((16, 768), F32)]
    out = pl.pallas_call(
        functools.partial(finish_kernel, with_lines=with_lines),
        grid=(count,),
        in_specs=[SMEM, block, block] + [spare, spare] * with_lines,
        out_specs=specs,
        out_shape=result,
        scratch_shapes=scratch,
        compiler_params=limits(20),
        cost_estimate=lasting(4),
        name="finish",
    )(where, mine, other, *[mine, other] * with_lines)
    return out if with_lines else out[0]


FIRST_TO = {
    (0, 0): (0, 0), (0, 1): (0, 1), (0, 2): (1, 0), (0, 3): (1, 1),
    (1, 0): (0, 2), (1, 1): (0, 3), (1, 2): (1, 2), (1, 3): (1, 3),
}
SECOND_TO = {
    (0, 0): (0, 1), (0, 1): (0, 0), (0, 2): (1, 1), (0, 3): (1, 0),
    (1, 0): (0, 3), (1, 1): (0, 2), (1, 2): (1, 3), (1, 3): (1, 2),
}


def column_pairs(table):
    pairs = []
    for chip in range(4):
        for (core, z), (core_to, z_to) in table.items():
            pairs.append(((chip * 2 + core) * 4 + z, (chip * 2 + core_to) * 4 + z_to))
    return pairs


def exchange_short(block):
    pairs = ([], [], [])
    for chip in range(4):
        for core in range(2):
            for z in range(4):
                if core == 1 and z % 2 == 1:
                    continue
                me = (chip * 2 + core) * 4 + z
                to = (chip * 2 + 1 - core) * 4
                pairs[0].append((me, (chip * 2 + core) * 4 + (z ^ 1)))
                pairs[1].append((me, to + z))
                pairs[2].append((me, to + (z ^ 1)))
    return tuple(lax.ppermute(block, ("dp", "blk"), p) for p in pairs)


CHIPS = [[0, 2, 4, 6], [1, 3, 5, 7]]


def flip_pairs(size, mask):
    return [(i, i ^ mask) for i in range(size)]


def swap(array, axis, mask):
    return lax.ppermute(array, axis, flip_pairs(8 if axis == "dp" else 4, mask))


def add_low(*terms):
    return sum(term.astype(F32) for term in terms).astype(BF16)


def find_slots(counts, odd):
    short = jnp.where(counts[1] < counts[0], 1, jnp.where(counts[2] < counts[0], 2, 0))
    one = jnp.where(short == 0, 1, 0)
    two = jnp.where(short == 2, 1, 2)
    return jnp.where(odd == 0, one, two), jnp.where(odd == 0, two, one), short


def leave_kernel(counts, odd, source, pair, single, sems):
    slots = find_slots(counts, odd[0])
    copies = start_copies(
        [source.at[slots[0]], source.at[slots[2]], source.at[slots[1]]],
        [pair.at[0], pair.at[1], single],
        sems,
    )
    for copy in copies:
        copy.wait()


def leave(counts, odd, array):
    rows = array.shape[1]
    return pl.pallas_call(
        leave_kernel,
        in_specs=[SMEM, SMEM, ANY],
        out_specs=[VMEM, VMEM],
        out_shape=[shape_of((2, rows, 768), BF16), shape_of((rows, 768), BF16)],
        scratch_shapes=[pltpu.SemaphoreType.DMA((3,))],
        cost_estimate=lasting(2),
        name="leave",
    )(counts, odd.reshape(1).astype(jnp.int32), array)


class Place:
    def __init__(self):
        dp = lax.axis_index("dp")
        self.z = lax.axis_index("blk")
        self.core = dp % 2
        self.chip = dp // 2


def after(value, *others):
    return lax.optimization_barrier((value,) + others)[0]


def by_chip(keep, got):
    return [add_low(keep[4 * k : 4 * k + 4], got[4 * k : 4 * k + 4]) for k in range(4)]


def over_chips(sums):
    return [swap(sums[k], "dp", 2 * k) for k in (1, 2, 3)]


def over_line(quarter):
    return [swap(quarter[k], "blk", k) for k in (1, 2, 3)]


def gather_all(part):
    every = lax.all_gather(part, ("dp", "blk"), axis=0)
    return every.reshape((4, 2, 4) + every.shape[1:])


def local_paired(
    tokens,
    counts,
    ln1_gain,
    ln1_shift,
    w_qkv,
    bias_q,
    bias_v,
    w_out,
    bias_out,
    ln2_gain,
    ln2_shift,
    w_fc1,
    bias_fc1,
    w_fc2,
    bias_fc2,
    cotangent,
):
    place = Place()
    odd = place.z % 2
    slots = find_slots(counts, odd)

    def arrange(pieces):
        (one, three), two = pieces
        return jnp.stack(
            [
                jnp.where(slots[0] == i, one, jnp.where(slots[1] == i, two, three))
                for i in range(3)
            ]
        )

    where = jnp.stack(
        [place.core, place.chip * 4 + place.z, 2 * place.core + odd]
    ).astype(jnp.int32)

    def move(pieces):
        return tuple(
            lax.ppermute(piece, ("dp", "blk"), column_pairs(table))
            for piece, table in zip(pieces, (FIRST_TO, SECOND_TO))
        )

    def give(pieces):
        return tuple(
            None
            if piece is None
            else lax.ppermute(piece, ("dp", "blk"), [pair[::-1] for pair in column_pairs(table)])
            for piece, table in zip(pieces, (FIRST_TO, SECOND_TO))
        )

    wide = w_fc1.shape[1] // 768
    rows = tokens.shape[1]
    vectors = [ln1_gain, ln1_shift, bias_q, bias_v, bias_out, ln2_gain, ln2_shift, bias_fc2]
    vecs, b1, w_near = prepare(jnp.stack(vectors), bias_fc1.reshape(1, -1), w_qkv)
    vecs_one, vecs_two = vecs[:4], vecs[4:]
    token_sends = leave(counts, odd, tokens)
    x13, x2 = move(token_sends)
    xs = (x13, x2)
    cot_sends = leave(counts, odd, after(cotangent, *token_sends))
    x3 = after(x13[1], x2, vecs, *cot_sends)
    short_blocks = exchange_short(x3)
    q_full, kv_full = project(x13, after(x2, x3), vecs_one, w_near)
    kv_other = swap(kv_full, "dp", 1)
    cots = move(after(cot_sends, x3))
    seq = 2 * kv_full.shape[1]
    kv_both = [kv_full, kv_other]
    att_full, t_full = attend(q_full, kv_both, seq, 768, 384)
    spare = -(-(SHORT - 2 * rows) // LANES) * LANES
    q_short, kv_head, kv_tail = project_short(
        where, x13, *after(short_blocks, att_full), vecs_one, w_near, spare
    )
    kv_short = [kv_head, kv_tail]
    att_short, t_short = attend(q_short, kv_short, SHORT, 384, 384)
    cots = after(cots, att_short)
    o13, o2, mid, normed_two, hidden_low, send_a, keep_a, gb1 = feed(
        where, att_full, att_short, xs, cots, w_out, vecs_two, w_fc1, b1, w_fc2
    )
    got_a = swap(send_a, "dp", 1)
    home_one = give((o13, o2))
    sums_a = by_chip(keep_a, got_a)
    chips_a = over_chips(sums_a)
    back_att, back_mid, send_b, keep_b, feed_sums = feed_back(
        where, att_full, att_short, cots, w_out, vecs_two, after(mid, *sums_a), normed_two,
        hidden_low, w_fc1,
    )
    home = (after(home_one[0], back_mid), home_one[1])
    quarter_a = add_low(after(sums_a[0], back_mid, home[0]), *chips_a)
    line_a = over_line(quarter_a)
    got_b = swap(after(send_b, quarter_a), "dp", 1)

    n_full = q_full.shape[0]
    dq_short, keep_short, send_pair = attend_back(
        where, after(q_short, quarter_a), back_att, n_full, att_short, t_short, kv_short, SHORT,
        768, 0, 6, True,
    )
    home = (home[0], after(home[1], dq_short))
    part_a = add_low(after(quarter_a[0], dq_short, home[1]), *line_a)
    all_a = gather_all(part_a)
    got_pair = swap(after(send_pair, part_a), "dp", 1)
    sums_b = by_chip(after(keep_b, dq_short, part_a), got_b)
    chips_b = over_chips(sums_b)
    away = (1 - odd) * rows
    send_short = add_low(
        lax.dynamic_slice_in_dim(keep_short, away, rows, 1),
        lax.dynamic_slice_in_dim(after(got_pair, *sums_b), away, rows, 1),
    )
    got_near = swap(send_short, "blk", 1)
    dq_full, own_full, sent_full = attend_back(
        where, after(q_full, send_short), back_att, 0, att_full, t_full, kv_both, seq, 768, 0, 6
    )
    got_near = after(got_near, dq_full)
    quarter_b = add_low(after(sums_b[0], dq_full, got_near), *chips_b)
    got_full = swap(after(sent_full, quarter_b), "dp", 1)
    line_b = over_line(quarter_b)
    send_c, keep_c, back = project_back(
        where, xs, vecs_one, dq_full, dq_short, own_full, got_full, keep_short, got_pair, got_near
    )
    i13, i2, line_sums = input_back(
        where, xs, vecs_one, w_qkv, back_mid, back, feed_sums, gb1
    )
    part_b = add_low(after(quarter_b[0], i2), *line_b)
    got_c = swap(after(send_c, part_b), "dp", 1)
    near_b = over_line([part_b] * 4)
    sums_c = [
        jnp.concatenate([total, line_sums[4 * k : 4 * k + 4]], axis=1)
        for k, total in enumerate(by_chip(after(keep_c, i2, part_b), got_c))
    ]
    near_b = jnp.stack([after(part_b, *sums_c)] + near_b)
    half_b = lax.all_gather(near_b, "dp", axis=0, axis_index_groups=CHIPS)
    chips_c = over_chips(sums_c)
    (i13_home,) = give((after(i13, *sums_c), None))[:1]
    output = arrange(after(home, *sums_c))
    all_a = after(all_a, *sums_c)
    halves_a = [all_a[:, c] for c in range(2)]
    grad_w_fc2 = finish(jnp.zeros((3,), jnp.int32), *halves_a, 0, wide, False)
    i13_home = after(i13_home, grad_w_fc2, output)
    quarter_c = add_low(after(sums_c[0], i13_home), *chips_c)
    line_c = over_line(quarter_c)
    part_c = add_low(quarter_c[0], *line_c)
    near_c = jnp.stack([part_c] + over_line([part_c] * 4))
    far_c = over_chips([near_c] * 4)
    i2_home = give((None, after(i2, near_c)))[1]
    half_b = after(half_b, near_c)
    other_b = swap(half_b, "dp", 1)
    inside = where * jnp.array([1, 0, 0], jnp.int32) + jnp.array([0, 1, 0], jnp.int32) * place.z
    grad_w_fc1 = finish(inside, half_b, other_b, 0, wide, True)
    grad_w_out = finish(inside, half_b, other_b, wide, 1, True)
    i2_home = after(i2_home, grad_w_fc1, grad_w_out)
    whole_c = jnp.stack([after(near_c, i2_home)] + far_c)
    other_c = swap(whole_c, "dp", 1)
    input_grad = arrange(after((i13_home, i2_home), whole_c)).astype(F32)
    grad_w_qkv, *lines = finish(where, whole_c, other_c, 0, 3, True, True)
    return (
        output,
        input_grad,
        lines[4],
        lines[5],
        grad_w_qkv,
        lines[6],
        lines[7],
        grad_w_out,
        lines[0],
        lines[1],
        lines[2],
        grad_w_fc1,
        lines[8],
        grad_w_fc2,
        lines[3],
    )


def solution(mesh):
    paired = mesh.shape["dp"] == 8 and mesh.shape["blk"] == 4
    chosen = local_paired if paired else local
    return jax.shard_map(
        chosen,
        mesh=mesh,
        in_specs=(
            P("dp", "blk", None),
            P("dp"),
            P(),
            P(),
            P(),
            P(),
            P(),
            P(),
            P(),
            P(),
            P(),
            P(),
            P(),
            P(),
            P(),
            P("dp", "blk", None),
        ),
        out_specs=(
            P("dp", "blk", None),
            P("dp", "blk", None),
            P(),
            P(),
            P(),
            P(),
            P(),
            P(),
            P(),
            P(),
            P(),
            P(),
            P(),
            P(),
            P(),
        ),
        check_vma=False,
    )
```
